32 devices in a mesh: dp: 8 (over z, y), seq: 4 (over x, core).
Axes of the slice: x: 2, y: 2, z: 4, core: 2. Of those that a mesh axis runs over, the one named last changes fastest.
Arguments:
- char_ids: int32 [16384], P(('dp', 'seq')), may hold values from 0 to 255
- char_table: bfloat16 [1024, 256], P(('dp', 'seq')), may hold values from -6 to 6
- attn_gain: bfloat16 [1024], P(('dp', 'seq')), may hold values from 0.5 to 1.5
- query_weight: bfloat16 [1024, 1024], P(('dp', 'seq')), may hold values from -0.1875 to 0.1875
- key_weight: bfloat16 [1024, 1024], P(('dp', 'seq')), may hold values from -0.1875 to 0.1875
- value_weight: bfloat16 [1024, 1024], P(('dp', 'seq')), may hold values from -0.1875 to 0.1875
- out_weight: bfloat16 [1024, 1024], P(('dp', 'seq')), may hold values from -1 to 1
- state_key_weight: bfloat16 [1024, 1024], P(('dp', 'seq')), may hold values from -0.1875 to 0.1875
- state_value_weight: bfloat16 [1024, 1024], P(('dp', 'seq')), may hold values from -0.1875 to 0.1875
- update_weight: bfloat16 [1024, 1024], P(('dp', 'seq')), may hold values from -1 to 1
- state_query: bfloat16 [1024, 512], P(('dp', 'seq')), may hold values from -6 to 6
- state_init: bfloat16 [1024, 512], P(('dp', 'seq')), may hold values from -6 to 6
- gate_bias: bfloat16 [1024], P(('dp', 'seq')), may hold values from -1 to 6
- position_table: bfloat16 [8, 512], replicated, may hold values from -5 to 5
- mlp_gain: bfloat16 [1024], P(('dp', 'seq')), may hold values from 0.5 to 1.5
- up_weight: bfloat16 [1024, 4096], P(('dp', 'seq')), may hold values from -0.1875 to 0.1875
- up_bias: bfloat16 [4096], P(('dp', 'seq')), may hold values from -3 to 3
- down_weight: bfloat16 [4096, 1024], P(('dp', 'seq')), may hold values from -0.09375 to 0.09375
- down_bias: bfloat16 [1024], P(('dp', 'seq')), may hold values from -3 to 3
- out_grad: bfloat16 [16384, 1024], P(('dp', 'seq')), may hold values from -6 to 6
Outputs:
- output: bfloat16 [16384, 1024], P(('dp', 'seq'))
- embedded_grad: float32 [16384, 1024], P(('dp', 'seq'))
- char_table_grad: float32 [1024, 256], P(('dp', 'seq'))
- attn_gain_grad: float32 [1024], P(('dp', 'seq'))
- query_weight_grad: float32 [1024, 1024], P(('dp', 'seq'))
- key_weight_grad: float32 [1024, 1024], P(('dp', 'seq'))
- value_weight_grad: float32 [1024, 1024], P(('dp', 'seq'))
- out_weight_grad: float32 [1024, 1024], P(('dp', 'seq'))
- state_key_matrix_gradient: float32 [1024, 1024], P(('dp', 'seq'))
- state_value_weight_grad: float32 [1024, 1024], P(('dp', 'seq'))
- update_weight_grad: float32 [1024, 1024], P(('dp', 'seq'))
- state_query_grad: float32 [1024, 512], P(('dp', 'seq'))
- state_init_grad: float32 [1024, 512], P(('dp', 'seq'))
- gate_bias_grad: float32 [1024], P(('dp', 'seq'))
- position_table_grad: float32 [8, 512], replicated
- mlp_gain_grad: float32 [1024], P(('dp', 'seq'))
- up_weight_grad: float32 [1024, 4096], P(('dp', 'seq'))
- up_bias_grad: float32 [4096], P(('dp', 'seq'))
- down_weight_grad: float32 [4096, 1024], P(('dp', 'seq'))
- down_bias_grad: float32 [1024], P(('dp', 'seq'))
The draws below stay inside these ranges and needn't reach their ends.
All inputs are finite; a program needn't handle non-finite values.
Results may differ from the reference program's by a relative error of at most 0.03.
Values may be sent and summed in bfloat16 or wider, within the bound.
No kernel may reach another device: no remote copies, remote signals or barrier semaphores. Data moves between devices by JAX's collectives and lax.ppermute only.
A program may use at most 320 MiB of HBM per device.

```python
import math
from functools import partial
import jax
import jax.numpy as jnp
import numpy as np
from jax import lax

D = 1024
HEADS = 8
HD = 128
FF = 4096
NSTATE = 512
VOCAB = 256
BLK = 512
TOKENS = 16384
N_DP = 8
N_SEQ = 4


def set_ends(values, stream_key, smallest, largest):
    dims = values.shape
    index_at = [jax.random.randint(jax.random.fold_in(stream_key, axis), (), 0, dims[axis]) for axis in range(len(dims))]
    values = values.at[tuple(index_at)].set(smallest)
    longest = dims.index(max(dims))
    index_at[longest] = (index_at[longest] + 1) % dims[longest]
    return values.at[tuple(index_at)].set(largest)


def shard_levels(stream_key, shape, shards, least, largest):
    gain = 1.0
    for position, parts in shards:
        draws = jax.random.uniform(jax.random.fold_in(jax.random.fold_in(stream_key, 6), position), (parts,), jnp.float32, least / len(shards), largest / len(shards))
        gain = gain * jnp.repeat(jnp.exp(draws), shape[position] // parts).reshape((-1,) + (1,) * (len(shape) - 1 - position))
    return gain


def rank_bounds(number_of, skew):
    loads = [(1 << 20) // math.isqrt(standing ** skew) + 1 for standing in range(1, number_of + 1)]
    spread = 1 + sum(loads) // (1 << 30)
    return np.cumsum(np.array([max(1, weight // spread) for weight in loads]))


def skewed_ids(rng, dims, number_of, lean):
    table = rank_bounds(number_of, lean)
    lot = jax.random.randint(jax.random.fold_in(rng, 1), dims, 0, int(table[number_of - 1]))
    standing = jnp.searchsorted(jnp.asarray(table, jnp.int32), lot, side="right")
    return jax.random.permutation(jax.random.fold_in(rng, 2), number_of)[standing].astype(jnp.int32)


def scatter_about(stream_key, dims, spread, most, pieces=(), kind=jnp.bfloat16):
    gain = shard_levels(stream_key, dims, pieces, -0.22, 0.18) if pieces else 1.0
    drawn = jax.random.normal(stream_key, dims, jnp.float32) * spread * gain
    return jnp.minimum(jnp.maximum(drawn, -most), most).astype(kind)


def setup_inputs(seed: int = 0) -> dict:
    arg_keys = jax.random.split(jax.random.key(seed), 21)
    char_ids = set_ends(skewed_ids(arg_keys[0], (TOKENS,), VOCAB, 2), jax.random.fold_in(arg_keys[0], 3), 0, VOCAB - 1).astype(jnp.int32)
    char_table = scatter_about(arg_keys[1], (D, VOCAB), 1.0, 6.0, ((0, 32),))
    attn_gain = jnp.clip(1.0 + 0.1 * jax.random.normal(arg_keys[2], (D,), jnp.float32), 0.5, 1.5).astype(jnp.bfloat16)
    query_weight = scatter_about(arg_keys[3], (D, D), D ** -0.5, 0.1875, ((0, 32),))
    key_weight = scatter_about(arg_keys[4], (D, D), D ** -0.5, 0.1875, ((0, 32),))
    value_weight = scatter_about(arg_keys[5], (D, D), D ** -0.5, 0.1875, ((0, 32),))
    out_weight = scatter_about(arg_keys[6], (D, D), (D // 32) ** -0.5, 1.0, ((0, 32),))
    state_key_weight = scatter_about(arg_keys[7], (D, D), D ** -0.5, 0.1875, ((0, 32),))
    state_value_weight = scatter_about(arg_keys[8], (D, D), D ** -0.5, 0.1875, ((0, 32),))
    update_weight = scatter_about(arg_keys[9], (D, D), (D // 32) ** -0.5, 1.0, ((0, 32),))
    state_query = scatter_about(arg_keys[10], (D, NSTATE), 1.0, 6.0, ((0, 32),))
    state_init = scatter_about(arg_keys[11], (D, NSTATE), 1.0, 6.0, ((0, 32),))
    gate_bias = jnp.clip(-1.0 + 7.0 * jax.random.uniform(arg_keys[12], (D,), jnp.float32) ** shard_levels(arg_keys[12], (D,), ((0, 32),), -0.2, 0.2), -1.0, 6.0).astype(jnp.bfloat16)
    position_table = scatter_about(arg_keys[13], (HEADS, BLK), 1.0, 5.0)
    mlp_gain = jnp.clip(1.0 + 0.1 * jax.random.normal(arg_keys[14], (D,), jnp.float32), 0.5, 1.5).astype(jnp.bfloat16)
    up_weight = scatter_about(arg_keys[15], (D, FF), D ** -0.5, 0.1875, ((0, 32),))
    up_bias = scatter_about(arg_keys[16], (FF,), 0.5, 3.0, ((0, 32),))
    down_weight = scatter_about(arg_keys[17], (FF, D), FF ** -0.5, 0.09375, ((0, 32),))
    down_bias = scatter_about(arg_keys[18], (D,), 0.5, 3.0, ((0, 32),))
    out_grad = scatter_about(arg_keys[19], (TOKENS, D), 1.0, 6.0, ((0, 32),))
    return dict(char_ids=char_ids, char_table=char_table, attn_gain=attn_gain, query_weight=query_weight, key_weight=key_weight, value_weight=value_weight, out_weight=out_weight, state_key_weight=state_key_weight, state_value_weight=state_value_weight, update_weight=update_weight, state_query=state_query, state_init=state_init, gate_bias=gate_bias, position_table=position_table, mlp_gain=mlp_gain, up_weight=up_weight, up_bias=up_bias, down_weight=down_weight, down_bias=down_bias, out_grad=out_grad)


@jax.custom_vjp
def low(v):
    return lax.optimization_barrier(v.astype(jnp.bfloat16)).astype(jnp.float32)

@jax.custom_vjp
def low_back(v):
    return v

def low_keep(v):
    return (low(v), None)

def low_pass(kept, grad):
    return (grad,)

def back_keep(v):
    return (v, None)

def back_low(kept, grad):
    return (low(grad),)
low.defvjp(low_keep, low_pass)
low_back.defvjp(back_keep, back_low)
HIGHEST_PRECISION = lax.Precision.HIGHEST

def matrix_product(left_side, right_side):
    return jnp.dot(left_side, right_side, precision=HIGHEST_PRECISION, preferred_element_type=jnp.float32)

def rms_norm(values, scale_gain):
    return values * lax.rsqrt(lax.optimization_barrier(jnp.mean(values * values, -1, keepdims=True)) + 1e-06) * scale_gain

def softmax_rows(scores):
    shifted = scores - lax.optimization_barrier(jnp.max(scores, -1, keepdims=True))
    powers = jnp.exp(shifted)
    return powers / lax.optimization_barrier(jnp.sum(powers, -1, keepdims=True))

def position_bias(bias_table):
    row_pos = jnp.arange(BLK)[:, None]
    col_pos = jnp.arange(2 * BLK)[None, :]
    distance = jnp.clip(row_pos - col_pos + BLK, 0, BLK - 1)
    gathered = jnp.take(bias_table, distance, axis=1)
    padding = jnp.zeros((HEADS, BLK, NSTATE), jnp.float32)
    return jnp.concatenate([gathered, padding], 2)

def position_mask(is_first):
    row_pos = jnp.arange(BLK)[:, None]
    col_pos = jnp.arange(2 * BLK)[None, :]
    distance = row_pos - col_pos + BLK
    allowed = (distance >= 0) & (distance < BLK) & ((col_pos >= BLK) | jnp.logical_not(is_first))
    return jnp.concatenate([allowed, jnp.ones((BLK, NSTATE), jnp.bool_)], 1)

def layer_block(params, state_carry, inputs):
    attn_gain, query_weight, key_weight, value_weight, out_weight, state_key_weight, state_value_weight, update_weight, state_query, gate_bias, position_table, mlp_gain, up_weight, up_bias, down_weight, down_bias = params
    state_now, key_prev, value_prev = state_carry
    embedded, is_first = inputs
    score_scale = HD ** (-0.5)
    normed = low(rms_norm(embedded, attn_gain))
    query_now = low(low_back(matrix_product(normed, query_weight)))
    key_now = low(low_back(matrix_product(normed, key_weight)))
    value_now = low(low_back(matrix_product(normed, value_weight)))
    state_reduced_precision = low(state_now)
    recurrent_state_key = low(low_back(matrix_product(state_reduced_precision, state_key_weight)))
    state_value = low(low_back(matrix_product(state_reduced_precision, state_value_weight)))
    keys_all = jnp.concatenate([key_prev, key_now, recurrent_state_key], 0).reshape(2 * BLK + NSTATE, HEADS, HD)
    values_all = jnp.concatenate([value_prev, value_now, state_value], 0).reshape(2 * BLK + NSTATE, HEADS, HD)
    raw_scores = jnp.einsum('ihd,jhd->hij', query_now.reshape(BLK, HEADS, HD), keys_all, precision=HIGHEST_PRECISION)
    scores = low_back(jnp.where(position_mask(is_first)[None], raw_scores * score_scale + position_bias(position_table), -1e+30))
    attn_probs = softmax_rows(scores)
    attn_mixed = jnp.einsum('hij,jhd->ihd', low(attn_probs), values_all, precision=HIGHEST_PRECISION)
    attn_mixed = low(low_back(attn_mixed.reshape(BLK, D)))
    hidden = embedded + low_back(matrix_product(attn_mixed, out_weight))
    state_raw = jnp.einsum('hds,jhd->hsj', state_query.reshape(HEADS, HD, NSTATE), key_now.reshape(BLK, HEADS, HD), precision=HIGHEST_PRECISION)
    state_probs = softmax_rows(low_back(state_raw * score_scale))
    state_mix = jnp.einsum('hsj,jhd->shd', low(state_probs), value_now.reshape(BLK, HEADS, HD), precision=HIGHEST_PRECISION)
    state_mix = low(low_back(state_mix.reshape(NSTATE, D)))
    update = low_back(matrix_product(state_mix, update_weight))
    keep_gate = jax.nn.sigmoid(gate_bias)
    new_state = keep_gate * state_now + (1.0 - keep_gate) * update
    normed_mlp = low(rms_norm(hidden, mlp_gain))
    up_pre = low_back(matrix_product(normed_mlp, up_weight) + up_bias)
    activation = low(jax.nn.gelu(up_pre))
    output = hidden + low_back(matrix_product(activation, down_weight)) + down_bias
    return ((new_state, key_now, value_now), output)

def forward_sequence(params, init_columns, embedded):
    start_state = jnp.transpose(init_columns)
    blocks = embedded.reshape(N_SEQ, BLK, D)
    is_first = jnp.arange(N_SEQ) == 0
    zero_keys = jnp.zeros((BLK, D), embedded.dtype)
    block_step = jax.checkpoint(partial(layer_block, params))
    final_carry, outputs = lax.scan(block_step, (start_state, zero_keys, zero_keys), (blocks, is_first))
    return outputs.reshape(N_SEQ * BLK, D)

def reference(char_ids, char_table, attn_gain, query_weight, key_weight, value_weight, out_weight, state_key_weight, state_value_weight, update_weight, state_query, state_init, gate_bias, position_table, mlp_gain, up_weight, up_bias, down_weight, down_bias, out_grad):
    params = tuple((weight.astype(jnp.float32) for weight in (attn_gain, query_weight, key_weight, value_weight, out_weight, state_key_weight, state_value_weight, update_weight, state_query, gate_bias, position_table, mlp_gain, up_weight, up_bias, down_weight, down_bias)))
    table_full = char_table.astype(jnp.float32)
    start_columns = state_init.astype(jnp.float32)
    ids_all = char_ids.reshape(N_DP, N_SEQ * BLK)
    cot_all = out_grad.astype(jnp.float32).reshape(N_DP, N_SEQ * BLK, D)

    def one_sequence(totals, inputs):
        seq_ids, seq_cot = inputs
        embedded, take_back = jax.vjp(lambda source: jnp.transpose(jnp.take(source, seq_ids, axis=1)), table_full)
        result, pullback = jax.vjp(forward_sequence, params, start_columns, embedded)
        grad_params, grad_state, grad_embedded = pullback(seq_cot)
        grad_table, = take_back(grad_embedded)
        totals = jax.tree.map(jnp.add, totals, (grad_params, grad_state, grad_table))
        return (totals, (result, grad_embedded))
    initial_totals = jax.tree.map(jnp.zeros_like, (params, start_columns, table_full))
    totals, (results, grads_in) = lax.scan(one_sequence, initial_totals, (ids_all, cot_all))
    grad_params, grad_state, grad_table = totals
    return (results.reshape(-1, D).astype(jnp.bfloat16), grads_in.reshape(-1, D), grad_table, grad_params[0], grad_params[1], grad_params[2], grad_params[3], grad_params[4], grad_params[5], grad_params[6], grad_params[7], grad_params[8], grad_state, grad_params[9], grad_params[10], grad_params[11], grad_params[12], grad_params[13], grad_params[14], grad_params[15])
```

```python
import functools

import jax
import jax.numpy as jnp
from jax import lax
from jax.experimental import pallas as pl
from jax.experimental.pallas import tpu as pltpu
from jax.sharding import PartitionSpec as P

D = 1024
HEADS = 8
HD = 128
NSTATE = 512
VOCAB = 256
BLK = 512
AX = ("dp", "seq")
VEC = 128


def f32(v):
    return v.astype(jnp.float32)


def low(v):
    return v.astype(jnp.bfloat16)


def route(move):
    pairs = []
    for z in range(4):
        for y in range(2):
            for x in range(2):
                for c in range(2):
                    tz, ty, tx, tc = move(z, y, x, c)
                    pairs.append((z * 8 + y * 4 + x * 2 + c, tz * 8 + ty * 4 + tx * 2 + tc))
    return pairs


A_ROUTE = route(lambda z, y, x, c: (z, y, 1 - x, c) if c == 0 else (z, 1 - y, x, c))
B_ROUTE = route(lambda z, y, x, c: (z, 1 - y, x, c) if c == 0 else (z, y, 1 - x, c))
CORE_ROUTE = route(lambda z, y, x, c: (z, y, x, 1 - c))
X_ROUTE = route(lambda z, y, x, c: (z, y, 1 - x, c))
Z_ROUTE = {k: route(lambda z, y, x, c, k=k: ((z + k) % 4, y, x, c)) for k in (1, 2, 3)}


def place():
    d, s = lax.axis_index("dp"), lax.axis_index("seq")
    return d // 2, d % 2, s // 2, s % 2


def send(v, pairs):
    return lax.ppermute(v, AX, pairs)


def stack_z(shard, *others):
    def body(*refs):
        z = lax.axis_index("dp") // 2
        for i, src in enumerate(refs[:4]):
            refs[4][lax.rem(z + 4 - i, 4)] = src[...]

    return pl.pallas_call(
        body, out_shape=jax.ShapeDtypeStruct((4,) + shard.shape, shard.dtype), name="stack_z"
    )(shard, *others)


def assemble(pieces, layout):
    rows, width = pieces[0].shape[1:]

    def body(*refs):
        ins, outs = refs[:8], refs[8:]
        y = lax.rem(lax.axis_index("dp"), 2)
        s = lax.axis_index("seq")
        x, c = s // 2, lax.rem(s, 2)
        for i, src in enumerate(ins):
            core = c if i < 4 else 1 - c
            flip_x = (0, 1 - core, core, 1)[i % 4]
            flip_y = (0, core, 1 - core, 1)[i % 4]
            tx, ty = lax.rem(x + flip_x, 2), lax.rem(y + flip_y, 2)
            for (first, w, folds), out in zip(layout, outs):
                for q in range(folds):
                    out[0, ty, tx, core, q * rows : (q + 1) * rows, :] = src[
                        0, :, first + q * w : first + (q + 1) * w
                    ]

    full = pl.pallas_call(
        body,
        out_shape=[
            jax.ShapeDtypeStruct((4, 2, 2, 2, rows * n, w), pieces[0].dtype) for _, w, n in layout
        ],
        grid=(4,),
        in_specs=[pl.BlockSpec((1, rows, width), lambda z: (z, 0, 0))] * 8,
        out_specs=[
            pl.BlockSpec((1, 2, 2, 2, rows * n, w), lambda z: (z, 0, 0, 0, 0, 0))
            for _, w, n in layout
        ],
        compiler_params=pltpu.CompilerParams(vmem_limit_bytes=40 * 2**20),
        name="assemble",
    )(*pieces)
    return [o.reshape(32 * rows * n, w) for o, (_, w, n) in zip(full, layout)]


def gather(shard, layout, after=None):
    if after is not None:
        shard, _ = lax.optimization_barrier((shard, after))
    others = [send(shard, Z_ROUTE[k]) for k in (1, 2, 3)]
    p = stack_z(shard, *others)
    pa, pb, qp = send(p, A_ROUTE), send(p, B_ROUTE), send(p, CORE_ROUTE)
    pd, qa, qb = send(pa, B_ROUTE), send(pa, CORE_ROUTE), send(pb, CORE_ROUTE)
    qd = send(pd, CORE_ROUTE)
    return assemble((p, pa, pb, pd, qp, qa, qb, qd), layout), p


def scatter(grad):
    total, width = grad.shape
    rows = total // 32
    z, y, x, c = place()
    parts = low(grad).reshape(4, 2, 2, 2, rows, width)

    def pick(a, i, axis):
        return lax.dynamic_index_in_dim(a, i, axis, keepdims=False)

    keep = pick(parts, c, 3)
    got = send(pick(parts, 1 - c, 3), CORE_ROUTE)

    def part(ty, tx):
        at = [
            lax.dynamic_slice(a, (0, ty, tx, 0, 0), (4, 1, 1, rows, width)) for a in (keep, got)
        ]
        return (f32(at[0]) + f32(at[1])).reshape(4, rows, width)

    ax, ay = jnp.where(c == 0, 1 - x, x), jnp.where(c == 0, y, 1 - y)
    bx, by = jnp.where(c == 0, x, 1 - x), jnp.where(c == 0, 1 - y, y)
    across = send(low(part(1 - y, 1 - x)), B_ROUTE)
    from_b = send(low(part(by, bx)), B_ROUTE)
    from_a = send(low(part(ay, ax) + f32(across)), A_ROUTE)
    own = part(y, x) + f32(from_a) + f32(from_b)
    rest = [send(low(pick(own, (z + k) % 4, 0)), Z_ROUTE[k]) for k in (1, 2, 3)]
    return pick(own, z, 0) + f32(rest[0]) + f32(rest[1]) + f32(rest[2])


def gather_any(shard, layout, after=None):
    rows = shard.shape[0]
    full = lax.all_gather(shard, AX, axis=0, tiled=True)
    outs = []
    for first, w, folds in layout:
        part = full[:, first : first + w * folds]
        if folds > 1:
            part = part.reshape(-1, rows, folds, w).transpose(0, 2, 1, 3).reshape(-1, w)
        outs.append(part)
    return outs, full


def scatter_any(grad):
    return lax.psum_scatter(f32(grad), AX, scatter_dimension=0, tiled=True)


def earlier_sum(keep_gate, mine, start):
    z, y, x, c = place()
    sibling = send(mine, CORE_ROUTE)
    first = jnp.where(c == 0, f32(mine), f32(sibling))
    second = jnp.where(c == 0, f32(sibling), f32(mine))
    chip = low(keep_gate * first + second)
    half = NSTATE // 2
    near = send(lax.dynamic_slice(chip, (c * half, 0), (half, D)), X_ROUTE)
    far = send(near, CORE_ROUTE)
    other = jnp.concatenate([jnp.where(c == 0, near, far), jnp.where(c == 0, far, near)], 0)
    before = jnp.where(x == 0, start, keep_gate * keep_gate * start + f32(other))
    return jnp.where(c == 0, before, keep_gate * before + f32(sibling))


def later_sum(keep_gate, mine):
    z, y, x, c = place()
    sibling = send(mine, CORE_ROUTE)
    first = jnp.where(c == 0, f32(mine), f32(sibling))
    second = jnp.where(c == 0, f32(sibling), f32(mine))
    chip = low(first + keep_gate * second)
    half = NSTATE // 2
    near = send(lax.dynamic_slice(chip, (c * half, 0), (half, D)), X_ROUTE)
    far = send(near, CORE_ROUTE)
    other = jnp.concatenate([jnp.where(c == 0, near, far), jnp.where(c == 0, far, near)], 0)
    after = jnp.where(x == 0, f32(other), 0.0)
    return jnp.where(c == 0, f32(sibling) + keep_gate * after, after)

def from_behind(block, axis, distance):
    devices = range(lax.axis_size(axis))
    route = [(i - distance, i) for i in devices if i - distance in devices]
    return lax.ppermute(block, axis, route)


def entering(shard, axis, combine, identity, reverse):
    devices, mine = (lax.axis_size(axis), lax.axis_index(axis))
    everything = jax.tree.map(
        lambda part, kind: lax.all_gather(part.astype(kind), axis),
        shard,
        (jnp.bfloat16, jnp.bfloat16),
    )
    start = jax.tree.map(
        lambda part, zero: jnp.broadcast_to(jnp.asarray(zero, part.dtype), part.shape),
        shard,
        identity,
    )

    def turn(k, before):
        at = devices - 1 - k if reverse else k
        reached = at > mine if reverse else at < mine
        new = combine(
            before, jax.tree.map(lambda part, own: part[at].astype(own.dtype), everything, shard)
        )
        return jax.tree.map(lambda a, b: jnp.where(reached, a, b), new, before)

    return lax.fori_loop(0, devices, turn, start)


def matrix_product(left_side, right_side):
    return jnp.dot(left_side, right_side, preferred_element_type=jnp.float32)


def matrix_product_transposed_left(left_side, right_side):
    return lax.dot_general(
        left_side, right_side, (((0,), (0,)), ((), ())), preferred_element_type=jnp.float32
    )


def matrix_product_transposed_right(left_side, right_side):
    return lax.dot_general(
        left_side, right_side, (((1,), (1,)), ((), ())), preferred_element_type=jnp.float32
    )


def rms_norm(values, scale_gain):
    return values * lax.rsqrt(jnp.mean(values * values, -1, keepdims=True) + 1e-06) * scale_gain


def softmax_rows(scores):
    shifted = scores - jnp.max(scores, -1, keepdims=True)
    powers = jnp.exp(shifted)
    return powers / jnp.sum(powers, -1, keepdims=True)


def position_bias(bias_table):
    heads = bias_table.shape[0]
    width = bias_table.shape[1]
    base_row = jnp.concatenate(
        [
            jnp.zeros((heads, 1), jnp.float32),
            jnp.flip(bias_table, 1),
            jnp.zeros((heads, width), jnp.float32),
        ],
        1,
    )
    repeated = jnp.broadcast_to(base_row[:, None, :], (heads, width, 2 * width + 1)).reshape(
        heads, -1
    )
    skewed = repeated[:, : width * 2 * width].reshape(heads, width, 2 * width)
    padding = jnp.zeros((heads, width, NSTATE), jnp.float32)
    return jnp.concatenate([skewed, padding], 2)


def diagonal_sums(token_grads):
    heads = token_grads.shape[0]
    width = token_grads.shape[1]
    flat = token_grads.reshape(heads, -1)
    flat = jnp.concatenate([flat, jnp.zeros((heads, width), jnp.float32)], 1)
    skewed = flat.reshape(heads, width, 2 * width + 1)
    return jnp.flip(jnp.sum(skewed[:, :, 1 : width + 1], 1), 1)


def position_mask(is_first):
    row_pos = jnp.arange(BLK)[:, None]
    col_pos = jnp.arange(2 * BLK)[None, :]
    distance = row_pos - col_pos + BLK
    allowed = (distance >= 0) & (distance < BLK) & ((col_pos >= BLK) | jnp.logical_not(is_first))
    return jnp.concatenate([allowed, jnp.ones((BLK, NSTATE), jnp.bool_)], 1)


def combine(earlier_pair, later_pair):
    return (earlier_pair[0] * later_pair[0], later_pair[0] * earlier_pair[1] + later_pair[1])


def attention_scores(query_heads, keys_all, pos_bias, allowed):
    raw_scores = jnp.einsum(
        "ihd,jhd->hij", query_heads, keys_all, preferred_element_type=jnp.float32
    )
    return jnp.where(allowed[None], raw_scores * HD ** (-0.5) + pos_bias, -1e30)


def shards(
    fast,
    char_ids,
    char_table,
    attn_gain,
    query_weight,
    key_weight,
    value_weight,
    out_weight,
    state_key_weight,
    state_value_weight,
    update_weight,
    state_query,
    state_init,
    gate_bias,
    position_table,
    mlp_gain,
    up_weight,
    up_bias,
    down_weight,
    down_bias,
    out_grad,
):
    take, add = (gather, scatter) if fast else (gather_any, scatter_any)
    rows = attn_gain.shape[0]
    vectors = jnp.concatenate(
        [v.reshape(rows, -1) for v in (attn_gain, mlp_gain, gate_bias, down_bias, up_bias)], 1
    )
    vectors = jnp.pad(vectors, ((0, 0), (0, VEC - vectors.shape[1])))
    ff = up_weight.shape[1]
    folds = ff // D
    (table_vec, qkv_full, squery_full), ahead = take(
        jnp.concatenate(
            [char_table, vectors, query_weight, key_weight, value_weight, state_query], 1
        ),
        ((0, VOCAB + VEC, 1), (VOCAB + VEC, 3 * D, 1), (VOCAB + VEC + 3 * D, NSTATE, 1)),
    )
    (sinit_full, update_full, skv_full, out_full), ahead = take(
        jnp.concatenate(
            [state_init, update_weight, state_key_weight, state_value_weight, out_weight], 1
        ),
        (
            (0, NSTATE, 1),
            (NSTATE, D, 1),
            (NSTATE + D, 2 * D, 1),
            (NSTATE + 3 * D, D, 1),
        ),
        ahead,
    )
    down_folded = down_weight.reshape(folds, rows, D).transpose(1, 0, 2).reshape(rows, ff)
    (up_full, down_full), _ = take(
        jnp.concatenate([up_weight, down_folded], 1), ((0, ff, 1), (ff, D, folds)), ahead
    )
    table_full = table_vec[:, :VOCAB]
    columns = jnp.transpose(table_vec[:, VOCAB : VOCAB + 4])
    gain_attn, gain_mlp, gbias_full, downbias_full = (columns[i] for i in range(4))
    upbias_full = table_vec[:, VOCAB + 4 : VOCAB + 4 + folds].reshape(-1)
    query_full, key_full, value_full = (qkv_full[:, i * D : (i + 1) * D] for i in range(3))
    state_key_complete, svalue_full = skv_full[:, :D], skv_full[:, D:]
    count_of_rows = char_ids.shape[0]
    score_scale = HD ** (-0.5)
    is_first = lax.axis_index("seq") == 0
    one_hot = (char_ids[:, None] == jnp.arange(VOCAB)[None, :]).astype(jnp.bfloat16)
    embedded = matrix_product_transposed_right(one_hot, table_full)
    normed, norm_back = jax.vjp(rms_norm, embedded, gain_attn.astype(jnp.float32))
    normed_low = normed.astype(jnp.bfloat16)
    query_now = matrix_product(normed_low, query_full).astype(jnp.bfloat16)
    key_now = matrix_product(normed_low, key_full).astype(jnp.bfloat16)
    value_now = matrix_product(normed_low, value_full).astype(jnp.bfloat16)
    previous = from_behind(jnp.stack([key_now, value_now]), "seq", 1)
    keep_gate = jax.nn.sigmoid(gbias_full.astype(jnp.float32))
    key_heads = key_now.reshape(count_of_rows, HEADS, HD)
    value_heads = value_now.reshape(count_of_rows, HEADS, HD)
    squery_heads = squery_full.reshape(HEADS, HD, NSTATE)
    state_raw = jnp.einsum(
        "hds,jhd->hsj", squery_heads, key_heads, preferred_element_type=jnp.float32
    )
    state_probs = softmax_rows(state_raw * score_scale)
    state_probs_low = state_probs.astype(jnp.bfloat16)
    state_mix = jnp.einsum(
        "hsj,jhd->shd", state_probs_low, value_heads, preferred_element_type=jnp.float32
    )
    state_mix = state_mix.reshape(NSTATE, D).astype(jnp.bfloat16)
    update = matrix_product(state_mix, update_full)
    unit_gain = jnp.ones_like(keep_gate)
    zero_state = jnp.zeros_like(update)
    start = jnp.transpose(f32(sinit_full))
    if fast:
        state_prev = earlier_sum(keep_gate, low((1.0 - keep_gate) * update), start)
    else:
        prefix_gain, prefix_sum = entering(
            (keep_gate, (1.0 - keep_gate) * update), "seq", combine, (unit_gain, zero_state), False
        )
        state_prev = prefix_gain * start + prefix_sum
    state_reduced_precision = state_prev.astype(jnp.bfloat16)
    recurrent_state_key = matrix_product(state_reduced_precision, state_key_complete).astype(
        jnp.bfloat16
    )
    state_value = matrix_product(state_reduced_precision, svalue_full).astype(jnp.bfloat16)
    keys_all = jnp.concatenate([previous[0], key_now, recurrent_state_key], 0).reshape(
        2 * count_of_rows + NSTATE, HEADS, HD
    )
    values_all = jnp.concatenate([previous[1], value_now, state_value], 0).reshape(
        2 * count_of_rows + NSTATE, HEADS, HD
    )
    pos_bias = position_bias(position_table.astype(jnp.float32))
    allowed = position_mask(is_first)
    query_heads = query_now.reshape(count_of_rows, HEADS, HD)
    scores = attention_scores(query_heads, keys_all, pos_bias, allowed)
    row_max = jnp.max(scores, -1, keepdims=True)
    log_total = row_max + jnp.log(jnp.sum(jnp.exp(scores - row_max), -1, keepdims=True))
    attn_probs = jnp.exp(scores - log_total)
    attn_mixed = jnp.einsum(
        "hij,jhd->ihd",
        attn_probs.astype(jnp.bfloat16),
        values_all,
        preferred_element_type=jnp.float32,
    )
    attn_mixed = attn_mixed.reshape(count_of_rows, D).astype(jnp.bfloat16)
    hidden = embedded + matrix_product(attn_mixed, out_full)
    normed_mlp, norm_mlp_back = jax.vjp(rms_norm, hidden, gain_mlp.astype(jnp.float32))
    normed_mlp_low = normed_mlp.astype(jnp.bfloat16)
    up_pre = matrix_product(normed_mlp_low, up_full) + upbias_full.astype(jnp.float32)
    activation, gelu_back = jax.vjp(jax.nn.gelu, up_pre)
    activation_low = activation.astype(jnp.bfloat16)
    output = hidden + matrix_product(activation_low, down_full) + downbias_full.astype(jnp.float32)
    up_back, down_back = up_full, down_full
    grad_out = out_grad.astype(jnp.float32)
    grad_down = grad_out.astype(jnp.bfloat16)
    down_bias_grad = jnp.sum(grad_out, 0)
    down_weight_grad = matrix_product_transposed_left(activation_low, grad_down)
    (grad_up_pre,) = gelu_back(matrix_product_transposed_right(grad_down, down_back))
    grad_up = grad_up_pre.astype(jnp.bfloat16)
    up_bias_grad = jnp.sum(grad_up.astype(jnp.float32), 0)
    up_weight_grad = matrix_product_transposed_left(normed_mlp_low, grad_up)
    grad_hidden_norm, mlp_gain_grad = norm_mlp_back(
        matrix_product_transposed_right(grad_up, up_back)
    )
    grad_hidden = grad_out + grad_hidden_norm
    up_grad, down_grad = add(up_weight_grad), add(down_weight_grad)
    query_back, key_back, value_back = query_full, key_full, value_full
    out_back, update_back, squery_back = out_full, update_full, squery_full
    state_key_backward, state_value_backward = state_key_complete, svalue_full
    grad_branch = grad_hidden.astype(jnp.bfloat16)
    out_weight_grad = matrix_product_transposed_left(attn_mixed, grad_branch)
    grad_mixed = (
        matrix_product_transposed_right(grad_branch, out_back)
        .astype(jnp.bfloat16)
        .reshape(count_of_rows, HEADS, HD)
    )
    scores = attention_scores(query_heads, keys_all, pos_bias, allowed)
    attn_probs = jnp.exp(scores - log_total)
    grad_values_all = jnp.einsum(
        "hij,ihd->jhd",
        attn_probs.astype(jnp.bfloat16),
        grad_mixed,
        preferred_element_type=jnp.float32,
    ).reshape(-1, D)
    grad_probs = jnp.einsum(
        "ihd,jhd->hij", grad_mixed, values_all, preferred_element_type=jnp.float32
    )
    grad_scores = attn_probs * (grad_probs - jnp.sum(attn_probs * grad_probs, -1, keepdims=True))
    grad_scores_low = grad_scores.astype(jnp.bfloat16)
    table_grad_local = diagonal_sums(grad_scores_low[:, :, : 2 * count_of_rows].astype(jnp.float32))
    grad_query = jnp.einsum(
        "hij,jhd->ihd", grad_scores_low, keys_all, preferred_element_type=jnp.float32
    )
    grad_query = (grad_query * score_scale).reshape(count_of_rows, D).astype(jnp.bfloat16)
    every_key_gradient = jnp.einsum(
        "hij,ihd->jhd", grad_scores_low, query_heads, preferred_element_type=jnp.float32
    )
    every_key_gradient = (every_key_gradient * score_scale).reshape(-1, D)
    grad_key_prev = every_key_gradient[:count_of_rows]
    grad_key_local = every_key_gradient[count_of_rows : 2 * count_of_rows]
    state_key_gradient = every_key_gradient[2 * count_of_rows :].astype(jnp.bfloat16)
    grad_value_prev = grad_values_all[:count_of_rows]
    grad_value_local = grad_values_all[count_of_rows : 2 * count_of_rows]
    state_value_gradient = grad_values_all[2 * count_of_rows :].astype(jnp.bfloat16)
    from_next = from_behind(
        jnp.stack([grad_key_prev, grad_value_prev]).astype(jnp.bfloat16), "seq", -1
    ).astype(jnp.float32)
    state_key_matrix_gradient = matrix_product_transposed_left(
        state_reduced_precision, state_key_gradient
    )
    state_value_weight_grad = matrix_product_transposed_left(
        state_reduced_precision, state_value_gradient
    )
    readout_gradient = matrix_product_transposed_right(
        state_key_gradient, state_key_backward
    ) + matrix_product_transposed_right(state_value_gradient, state_value_backward)
    if fast:
        after_grad = later_sum(keep_gate, low(readout_gradient))
    else:
        later_gain, after_grad = entering(
            (keep_gate, readout_gradient), "seq", combine, (unit_gain, zero_state), True
        )
    gate_term = jnp.sum(after_grad * (state_prev - update), 0)
    gate_bias_grad = gate_term * keep_gate * (1.0 - keep_gate)
    state_init_grad = jnp.transpose(
        jnp.where(is_first, readout_gradient + keep_gate * after_grad, 0.0)
    )
    grad_update = ((1.0 - keep_gate) * after_grad).astype(jnp.bfloat16)
    update_weight_grad = matrix_product_transposed_left(state_mix, grad_update)
    grad_smix = (
        matrix_product_transposed_right(grad_update, update_back)
        .astype(jnp.bfloat16)
        .reshape(NSTATE, HEADS, HD)
    )
    grad_value_state = jnp.einsum(
        "hsj,shd->jhd", state_probs_low, grad_smix, preferred_element_type=jnp.float32
    ).reshape(count_of_rows, D)
    grad_sprobs = jnp.einsum(
        "shd,jhd->hsj", grad_smix, value_heads, preferred_element_type=jnp.float32
    )
    grad_sscores = state_probs * (
        grad_sprobs - jnp.sum(state_probs * grad_sprobs, -1, keepdims=True)
    )
    grad_sscores = grad_sscores.astype(jnp.bfloat16)
    state_query_grad = jnp.einsum(
        "hsj,jhd->hds", grad_sscores, key_heads, preferred_element_type=jnp.float32
    )
    state_query_grad = (state_query_grad * score_scale).reshape(D, NSTATE)
    grad_key_state = jnp.einsum(
        "hsj,hds->jhd",
        grad_sscores,
        squery_back.reshape(HEADS, HD, NSTATE),
        preferred_element_type=jnp.float32,
    )
    grad_key_state = (grad_key_state * score_scale).reshape(count_of_rows, D)
    grad_key = (grad_key_local + grad_key_state + from_next[0]).astype(jnp.bfloat16)
    grad_value = (grad_value_local + grad_value_state + from_next[1]).astype(jnp.bfloat16)
    query_weight_grad = matrix_product_transposed_left(normed_low, grad_query)
    key_weight_grad = matrix_product_transposed_left(normed_low, grad_key)
    value_weight_grad = matrix_product_transposed_left(normed_low, grad_value)
    grad_normed = (
        matrix_product_transposed_right(grad_query, query_back)
        + matrix_product_transposed_right(grad_key, key_back)
        + matrix_product_transposed_right(grad_value, value_back)
    )
    grad_embedded_norm, attn_gain_grad = norm_back(grad_normed)
    embedded_grad = grad_hidden + grad_embedded_norm
    char_table_grad = lax.dot_general(
        embedded_grad,
        one_hot.astype(jnp.float32),
        (((0,), (0,)), ((), ())),
        precision=lax.Precision.HIGHEST,
        preferred_element_type=jnp.float32,
    )
    rows_of_table = jnp.pad(table_grad_local, ((0, HEADS), (0, 0)))
    position_table_grad = jnp.sum(lax.all_gather(rows_of_table, AX), 0)[:HEADS]
    vector_grads = jnp.concatenate(
        [
            v.reshape(D, -1)
            for v in (attn_gain_grad, mlp_gain_grad, gate_bias_grad, down_bias_grad, up_bias_grad)
        ],
        1,
    )
    vector_grads = jnp.pad(vector_grads, ((0, 0), (0, VEC - vector_grads.shape[1])))
    out_weight_sum = add(out_weight_grad)
    state_sum = add(jnp.concatenate([state_key_matrix_gradient, state_value_weight_grad], 1))
    update_sum = add(
        jnp.concatenate([update_weight_grad, state_query_grad, state_init_grad], 1)
    )
    last = add(
        jnp.concatenate(
            [
                char_table_grad,
                vector_grads,
                query_weight_grad,
                key_weight_grad,
                value_weight_grad,
            ],
            1,
        )
    )
    table_sum, vector_sum = last[:, :VOCAB], last[:, VOCAB : VOCAB + VEC]
    main = VOCAB + VEC
    return (
        low(output),
        embedded_grad,
        table_sum,
        vector_sum[:, 0],
        last[:, main : main + D],
        last[:, main + D : main + 2 * D],
        last[:, main + 2 * D :],
        out_weight_sum,
        state_sum[:, :D],
        state_sum[:, D:],
        update_sum[:, :D],
        update_sum[:, D : D + NSTATE],
        update_sum[:, D + NSTATE :],
        vector_sum[:, 2],
        position_table_grad,
        vector_sum[:, 1],
        up_grad,
        vector_sum[:, 4 : 4 + folds].reshape(-1),
        down_grad,
        vector_sum[:, 3],
    )


def solution(mesh):
    fast = dict(mesh.shape) == {"dp": 8, "seq": 4}
    return jax.shard_map(
        functools.partial(shards, fast),
        mesh=mesh,
        in_specs=(
            P(("dp", "seq")),
            P(("dp", "seq"), None),
            P(("dp", "seq")),
            P(("dp", "seq"), None),
            P(("dp", "seq"), None),
            P(("dp", "seq"), None),
            P(("dp", "seq"), None),
            P(("dp", "seq"), None),
            P(("dp", "seq"), None),
            P(("dp", "seq"), None),
            P(("dp", "seq"), None),
            P(("dp", "seq"), None),
            P(("dp", "seq")),
            P(),
            P(("dp", "seq")),
            P(("dp", "seq"), None),
            P(("dp", "seq")),
            P(("dp", "seq"), None),
            P(("dp", "seq")),
            P(("dp", "seq"), None),
        ),
        out_specs=(
            P(("dp", "seq"), None),
            P(("dp", "seq"), None),
            P(("dp", "seq"), None),
            P(("dp", "seq")),
            P(("dp", "seq"), None),
            P(("dp", "seq"), None),
            P(("dp", "seq"), None),
            P(("dp", "seq"), None),
            P(("dp", "seq"), None),
            P(("dp", "seq"), None),
            P(("dp", "seq"), None),
            P(("dp", "seq"), None),
            P(("dp", "seq"), None),
            P(("dp", "seq")),
            P(),
            P(("dp", "seq")),
            P(("dp", "seq"), None),
            P(("dp", "seq")),
            P(("dp", "seq"), None),
            P(("dp", "seq")),
        ),
        check_vma=False,
    )
```

```python
import functools

import jax
import jax.numpy as jnp
from jax import lax
from jax.experimental import pallas as pl
from jax.experimental.pallas import tpu as pltpu
from jax.sharding import PartitionSpec as P

D = 1024
HEADS = 8
HD = 128
NSTATE = 512
VOCAB = 256
BLK = 512
AX = ("dp", "seq")
VEC = 128


def f32(v):
    return v.astype(jnp.float32)


def low(v):
    return v.astype(jnp.bfloat16)


def route(move):
    pairs = []
    for z in range(4):
        for y in range(2):
            for x in range(2):
                for c in range(2):
                    tz, ty, tx, tc = move(z, y, x, c)
                    pairs.append((z * 8 + y * 4 + x * 2 + c, tz * 8 + ty * 4 + tx * 2 + tc))
    return pairs


A_ROUTE = route(lambda z, y, x, c: (z, y, 1 - x, c) if c == 0 else (z, 1 - y, x, c))
B_ROUTE = route(lambda z, y, x, c: (z, 1 - y, x, c) if c == 0 else (z, y, 1 - x, c))
CORE_ROUTE = route(lambda z, y, x, c: (z, y, x, 1 - c))
X_ROUTE = route(lambda z, y, x, c: (z, y, 1 - x, c))
Z_ROUTE = {k: route(lambda z, y, x, c, k=k: ((z + k) % 4, y, x, c)) for k in (1, 2, 3)}


def place():
    d, s = lax.axis_index("dp"), lax.axis_index("seq")
    return d // 2, d % 2, s // 2, s % 2


def send(v, pairs):
    return lax.ppermute(v, AX, pairs)


def stack_z(shard, *others):
    def body(*refs):
        z = lax.axis_index("dp") // 2
        for i, src in enumerate(refs[:4]):
            refs[4][lax.rem(z + 4 - i, 4)] = src[...]

    return pl.pallas_call(
        body, out_shape=jax.ShapeDtypeStruct((4,) + shard.shape, shard.dtype), name="stack_z"
    )(shard, *others)


def assemble(pieces, layout):
    rows, width = pieces[0].shape[1:]

    def body(*refs):
        ins, outs = refs[:8], refs[8:]
        y = lax.rem(lax.axis_index("dp"), 2)
        s = lax.axis_index("seq")
        x, c = s // 2, lax.rem(s, 2)
        for i, src in enumerate(ins):
            core = c if i < 4 else 1 - c
            flip_x = (0, 1 - core, core, 1)[i % 4]
            flip_y = (0, core, 1 - core, 1)[i % 4]
            tx, ty = lax.rem(x + flip_x, 2), lax.rem(y + flip_y, 2)
            for (first, w, folds), out in zip(layout, outs):
                for q in range(folds):
                    out[0, ty, tx, core, q * rows : (q + 1) * rows, :] = src[
                        0, :, first + q * w : first + (q + 1) * w
                    ]

    full = pl.pallas_call(
        body,
        out_shape=[
            jax.ShapeDtypeStruct((4, 2, 2, 2, rows * n, w), pieces[0].dtype) for _, w, n in layout
        ],
        grid=(4,),
        in_specs=[pl.BlockSpec((1, rows, width), lambda z: (z, 0, 0))] * 8,
        out_specs=[
            pl.BlockSpec((1, 2, 2, 2, rows * n, w), lambda z: (z, 0, 0, 0, 0, 0))
            for _, w, n in layout
        ],
        compiler_params=pltpu.CompilerParams(vmem_limit_bytes=40 * 2**20),
        name="assemble",
    )(*pieces)
    return [o.reshape(32 * rows * n, w) for o, (_, w, n) in zip(full, layout)]


def tie(value, *others):
    return lax.optimization_barrier((value, others))[0]


def join(*values):
    return lax.optimization_barrier(values)


def along_z(shard):
    return [send(shard, Z_ROUTE[k]) for k in (1, 2, 3)]


def to_sides(p):
    return send(p, A_ROUTE), send(p, B_ROUTE)


def to_corner(p, sides):
    return send(sides[0], B_ROUTE), [send(v, CORE_ROUTE) for v in (p,) + tuple(sides)]


def full(p, sides, corner, layout):
    last = send(corner[0], CORE_ROUTE)
    return assemble((p,) + tuple(sides) + (corner[0],) + tuple(corner[1]) + (last,), layout)


def to_core(away):
    return send(away, CORE_ROUTE)


def chip_part(keep, got, ty, tx):
    rows, width = keep.shape[0] // 16, keep.shape[1]
    at = [
        lax.dynamic_slice(
            a.reshape(2, 2, 4, rows, width), (ty, tx, 0, 0, 0), (1, 1, 4, rows, width)
        )
        for a in (keep, got)
    ]
    return (f32(at[0]) + f32(at[1])).reshape(4, rows, width)


def from_corner(keep, got):
    z, y, x, c = place()
    bx, by = jnp.where(c == 0, x, 1 - x), jnp.where(c == 0, 1 - y, y)
    corner, side = chip_part(keep, got, 1 - y, 1 - x), chip_part(keep, got, by, bx)
    return send(low(corner), B_ROUTE), send(low(side), B_ROUTE)


def from_side(keep, got, across):
    z, y, x, c = place()
    ax, ay = jnp.where(c == 0, 1 - x, x), jnp.where(c == 0, y, 1 - y)
    return send(low(chip_part(keep, got, ay, ax) + f32(across)), A_ROUTE)


def from_ends(keep, got, side_a, side_b):
    z, y, x, c = place()
    own = chip_part(keep, got, y, x) + f32(side_a) + f32(side_b)
    rest = [low(lax.dynamic_index_in_dim(own, (z + k) % 4, 0, False)) for k in (1, 2, 3)]
    mine = lax.dynamic_index_in_dim(own, z, 0, False)
    return [mine] + [send(v, Z_ROUTE[k]) for v, k in zip(rest, (1, 2, 3))]


def finish(parts):
    return parts[0] + f32(parts[1]) + f32(parts[2]) + f32(parts[3])


def gather_any(shard, layout):
    rows = shard.shape[0]
    full = lax.all_gather(shard, AX, axis=0, tiled=True)
    outs = []
    for first, w, folds in layout:
        part = full[:, first : first + w * folds]
        if folds > 1:
            part = part.reshape(-1, rows, folds, w).transpose(0, 2, 1, 3).reshape(-1, w)
        outs.append(part)
    return outs


def scatter_any(grad):
    return lax.psum_scatter(f32(grad), AX, scatter_dimension=0, tiled=True)


def earlier_sum(keep_gate, mine, start):
    z, y, x, c = place()
    sibling = send(mine, CORE_ROUTE)
    first = jnp.where(c == 0, f32(mine), f32(sibling))
    second = jnp.where(c == 0, f32(sibling), f32(mine))
    chip = low(keep_gate * first + second)
    half = NSTATE // 2
    near = send(lax.dynamic_slice(chip, (c * half, 0), (half, D)), X_ROUTE)
    far = send(near, CORE_ROUTE)
    other = jnp.concatenate([jnp.where(c == 0, near, far), jnp.where(c == 0, far, near)], 0)
    before = jnp.where(x == 0, start, keep_gate * keep_gate * start + f32(other))
    return jnp.where(c == 0, before, keep_gate * before + f32(sibling))


def later_sum(keep_gate, mine):
    z, y, x, c = place()
    sibling = send(mine, CORE_ROUTE)
    first = jnp.where(c == 0, f32(mine), f32(sibling))
    second = jnp.where(c == 0, f32(sibling), f32(mine))
    chip = low(first + keep_gate * second)
    half = NSTATE // 2
    near = send(lax.dynamic_slice(chip, (c * half, 0), (half, D)), X_ROUTE)
    far = send(near, CORE_ROUTE)
    other = jnp.concatenate([jnp.where(c == 0, near, far), jnp.where(c == 0, far, near)], 0)
    after = jnp.where(x == 0, f32(other), 0.0)
    return jnp.where(c == 0, f32(sibling) + keep_gate * after, after)


def from_behind(block, axis, distance):
    devices = range(lax.axis_size(axis))
    pairs = [(i - distance, i) for i in devices if i - distance in devices]
    return lax.ppermute(block, axis, pairs)


def entering(keep_gate, mine, reverse):
    devices, at_home = lax.axis_size("seq"), lax.axis_index("seq")
    everything = lax.all_gather(mine, "seq")

    def turn(k, before):
        at = devices - 1 - k if reverse else k
        reached = at > at_home if reverse else at < at_home
        gain, total = before
        return (
            jnp.where(reached, gain * keep_gate, gain),
            jnp.where(reached, keep_gate * total + f32(everything[at]), total),
        )

    start = (jnp.ones_like(keep_gate), jnp.zeros(mine.shape, jnp.float32))
    return lax.fori_loop(0, devices, turn, start)


def norm_scale(values):
    return lax.rsqrt(jnp.mean(values * values, -1, keepdims=True) + 1e-06)


def halves_of_columns(a):
    parts = a.reshape(a.shape[0], CHUNKS, 2, -1)
    return [parts[:, :, i].reshape(a.shape[0], -1) for i in range(2)]


def halves_of_rows(a, chunks):
    parts = a.reshape(chunks, 2, -1, a.shape[1])
    return [parts[:, i].reshape(-1, a.shape[1]) for i in range(2)]


def fold(a, rows):
    return a.reshape(-1, rows, D).transpose(1, 0, 2).reshape(rows, -1)


def unfold(a):
    rows = a.shape[0]
    return a.reshape(rows, -1, D).transpose(1, 0, 2).reshape(-1, D)


SCALE = HD ** (-0.5)


def dot(a, b, dims):
    return lax.dot_general(a, b, (dims, ((), ())), preferred_element_type=jnp.float32)


NN, NT, TN = ((1,), (0,)), ((1,), (1,)), ((0,), (0,))


def head_block(first):
    return pl.BlockSpec((BLK, HD), lambda h: (0, first + h))


def pair_block():
    return pl.BlockSpec((2, BLK, HD), lambda h: (0, 0, h))


def row_block():
    return pl.BlockSpec((1, 1, BLK), lambda h: (h, 0, 0))


def token_scores(q, k, kp, bias_row, is_first):
    row = lax.broadcasted_iota(jnp.int32, (BLK, BLK), 0)
    col = lax.broadcasted_iota(jnp.int32, (BLK, BLK), 1)
    own = row <= col
    bias = jnp.concatenate([bias_row] + [pltpu.roll(bias_row, i, 1) for i in range(1, 8)], 0)
    while bias.shape[0] < BLK:
        bias = jnp.concatenate([bias, pltpu.roll(bias, bias.shape[0], 1)], 0)
    raw = jnp.where(own, dot(k, q, NT), dot(kp, q, NT))
    scores = raw * SCALE + bias
    return jnp.where(own | jnp.logical_not(is_first), scores, -1e30), own


def attention_body(q, k, v, kp, vp, sk, sv, bias, mixed, lse):
    is_first = lax.axis_index("seq") == 0
    q = q[...]
    tokens, own = token_scores(q, k[...], kp[...], bias[0], is_first)
    states = dot(sk[...], q, NT) * SCALE
    top = jnp.maximum(jnp.max(tokens, 0, keepdims=True), jnp.max(states, 0, keepdims=True))
    tokens, states = jnp.exp(tokens - top), jnp.exp(states - top)
    total = jnp.sum(tokens, 0, keepdims=True) + jnp.sum(states, 0, keepdims=True)
    lse[0] = top + jnp.log(total)
    mix = dot(jnp.transpose(v[...]), low(jnp.where(own, tokens, 0.0)), NN)
    mix += dot(jnp.transpose(vp[...]), low(jnp.where(own, 0.0, tokens)), NN)
    mix += dot(jnp.transpose(sv[...]), low(states), NN)
    mixed[...] = low(jnp.transpose(mix * (1.0 / total)))


def attention(qkv, prev, skv, bias):
    return pl.pallas_call(
        attention_body,
        grid=(HEADS,),
        in_specs=[head_block(0), head_block(HEADS), head_block(2 * HEADS)]
        + [head_block(0), head_block(HEADS)] * 2
        + [row_block()],
        out_specs=[head_block(0), row_block()],
        out_shape=[
            jax.ShapeDtypeStruct((BLK, D), jnp.bfloat16),
            jax.ShapeDtypeStruct((HEADS, 1, BLK), jnp.float32),
        ],
        compiler_params=pltpu.CompilerParams(vmem_limit_bytes=40 * 2**20),
        cost_estimate=pl.CostEstimate(
            flops=12 * HEADS * BLK * BLK * HD,
            bytes_accessed=9 * 2**20,
            transcendentals=2 * HEADS * BLK * BLK,
        ),
        name="attention",
    )(qkv, qkv, qkv, prev, prev, skv, skv, bias)


def attention_back_body(
    q, k, v, kp, vp, sk, sv, bias, lse, go, gq, gkv, gprev, gstate, gbias
):
    is_first = lax.axis_index("seq") == 0
    q, k, kp, sk, go = q[...], k[...], kp[...], sk[...], go[...]
    tokens, own = token_scores(q, k, kp, bias[0], is_first)
    log_total = lse[0]
    tokens = jnp.exp(tokens - log_total)
    states = jnp.exp(dot(sk, q, NT) * SCALE - log_total)
    gtokens = jnp.where(own, dot(v[...], go, NT), dot(vp[...], go, NT))
    gstates = dot(sv[...], go, NT)
    mean = jnp.sum(tokens * gtokens, 0, keepdims=True) + jnp.sum(states * gstates, 0, keepdims=True)
    gkv[1] = dot(low(jnp.where(own, tokens, 0.0)), go, NN)
    gprev[1] = low(dot(low(jnp.where(own, 0.0, tokens)), go, NN))
    gstate[1] = low(dot(low(states), go, NN))
    gtokens = low(tokens * (gtokens - mean))
    gstates = low(states * (gstates - mean))
    wide = f32(gtokens)
    gown, gbefore = low(jnp.where(own, wide, 0.0)), low(jnp.where(own, 0.0, wide))
    gkv[0] = dot(gown, q, NN) * SCALE
    gprev[0] = low(dot(gbefore, q, NN) * SCALE)
    gstate[0] = low(dot(gstates, q, NN) * SCALE)
    g = dot(jnp.transpose(k), gown, NN)
    g += dot(jnp.transpose(kp), gbefore, NN)
    g += dot(jnp.transpose(sk), gstates, NN)
    gq[...] = low(jnp.transpose(g * SCALE))
    rows = BLK
    while rows > 1:
        rows //= 2
        wide = wide[:rows] + pltpu.roll(wide[rows:], BLK - rows, 1)
    gbias[0] = wide


def attention_back(qkv, prev, skv, bias, lse, go):
    return pl.pallas_call(
        attention_back_body,
        grid=(HEADS,),
        in_specs=[head_block(0), head_block(HEADS), head_block(2 * HEADS)]
        + [head_block(0), head_block(HEADS)] * 2
        + [row_block(), row_block(), head_block(0)],
        out_specs=[head_block(0), pair_block(), pair_block(), pair_block(), row_block()],
        out_shape=[
            jax.ShapeDtypeStruct((BLK, D), jnp.bfloat16),
            jax.ShapeDtypeStruct((2, BLK, D), jnp.float32),
            jax.ShapeDtypeStruct((2, BLK, D), jnp.bfloat16),
            jax.ShapeDtypeStruct((2, BLK, D), jnp.bfloat16),
            jax.ShapeDtypeStruct((HEADS, 1, BLK), jnp.float32),
        ],
        compiler_params=pltpu.CompilerParams(vmem_limit_bytes=48 * 2**20),
        cost_estimate=pl.CostEstimate(
            flops=30 * HEADS * BLK * BLK * HD,
            bytes_accessed=18 * 2**20,
            transcendentals=2 * HEADS * BLK * BLK,
        ),
        name="attention_back",
    )(qkv, qkv, qkv, prev, prev, skv, skv, bias, lse, go)


def query_block():
    return pl.BlockSpec((HD, NSTATE), lambda h: (h, 0))


def state_body(k, v, query, mixed, lse):
    scores = dot(k[...], query[...], NN) * SCALE
    top = jnp.max(scores, 0, keepdims=True)
    scores = jnp.exp(scores - top)
    total = jnp.sum(scores, 0, keepdims=True)
    lse[0] = top + jnp.log(total)
    mix = dot(jnp.transpose(v[...]), low(scores), NN)
    mixed[...] = low(jnp.transpose(mix * (1.0 / total)))


def state_attention(qkv, query):
    return pl.pallas_call(
        state_body,
        grid=(HEADS,),
        in_specs=[head_block(HEADS), head_block(2 * HEADS), query_block()],
        out_specs=[head_block(0), row_block()],
        out_shape=[
            jax.ShapeDtypeStruct((NSTATE, D), jnp.bfloat16),
            jax.ShapeDtypeStruct((HEADS, 1, NSTATE), jnp.float32),
        ],
        compiler_params=pltpu.CompilerParams(vmem_limit_bytes=32 * 2**20),
        cost_estimate=pl.CostEstimate(
            flops=4 * HEADS * BLK * BLK * HD,
            bytes_accessed=4 * 2**20,
            transcendentals=HEADS * BLK * BLK,
        ),
        name="state_attention",
    )(qkv, qkv, query)


def state_back_body(k, v, query, lse, go, gkv, gsum, gquery):
    k, query, go = k[...], query[...], go[...]
    probs = jnp.exp(dot(k, query, NN) * SCALE - lse[0])
    gprobs = dot(v[...], go, NT)
    mean = jnp.sum(probs * gprobs, 0, keepdims=True)
    gsum[1] = dot(low(probs), go, NN) + gkv[1]
    gscores = low(probs * (gprobs - mean))
    gsum[0] = dot(gscores, query, NT) * SCALE + gkv[0]
    gquery[...] = low(dot(jnp.transpose(k), gscores, NN) * SCALE)


def state_attention_back(qkv, query, lse, go, gkv):
    return pl.pallas_call(
        state_back_body,
        grid=(HEADS,),
        in_specs=[
            head_block(HEADS),
            head_block(2 * HEADS),
            query_block(),
            row_block(),
            head_block(0),
            pair_block(),
        ],
        out_specs=[pair_block(), query_block()],
        out_shape=[
            jax.ShapeDtypeStruct((2, BLK, D), jnp.float32),
            jax.ShapeDtypeStruct((D, NSTATE), jnp.bfloat16),
        ],
        compiler_params=pltpu.CompilerParams(vmem_limit_bytes=32 * 2**20),
        cost_estimate=pl.CostEstimate(
            flops=10 * HEADS * BLK * BLK * HD,
            bytes_accessed=14 * 2**20,
            transcendentals=HEADS * BLK * BLK,
        ),
        name="state_attention_back",
    )(qkv, qkv, query, lse, go, gkv)


STEP = 512
HALF = 2048
CHUNKS = 32


def owner_row(chip):
    return chip % 4 * 4 + chip // 4


def gelu_parts(x):
    a, b = 0.7978845608028654, 0.044715
    square = x * x
    t = jnp.tanh(a * x * (1.0 + b * square))
    half = 0.5 * (1.0 + t)
    slope = half + (0.5 * a) * x * (1.0 - t * t) * (1.0 + 3.0 * b * square)
    return x * half, slope


def mlp_body(last, core_of, *refs):
    hidden, og, rows, up_bias, up, down = refs[:6]
    if last:
        out_in, u_in, keep, away, up_bias_grad, output, grad, branch, sums = refs[6:15]
        xn, xs, out_acc, u_acc = refs[15:]
    else:
        keep, away, up_bias_grad, out_acc, u_acc = refs[6:11]
        xn, xs = refs[11:]
    j = pl.program_id(0)
    core = core_of()
    rk = D // CHUNKS
    hk = HALF // CHUNKS

    @pl.when(j == 0)
    def _():
        h = hidden[...]
        r = lax.rsqrt(jnp.mean(h * h, -1, keepdims=True) + 1e-06)
        n = low(h * r * rows[0:1, :])
        xn[...] = n
        nt = jnp.transpose(n)
        for i in range(CHUNKS):
            to = owner_row(i // 2) * rk + lax.rem(i % 2 + core, 2) * (D // 2)
            xs[pl.ds(pl.multiple_of(to, rk), rk), :] = nt[i * rk : (i + 1) * rk]
        if last:
            out_acc[...] = out_in[...]
            u_acc[...] = u_in[...]
        else:
            out_acc[...] = jnp.zeros_like(out_acc)
            u_acc[...] = jnp.zeros_like(u_acc)

    up_w, down_w, g_out = up[...], down[...], og[...]
    act, slope = gelu_parts(dot(xn[...], up_w, NN) + up_bias[...])
    act = low(act)
    out_acc[...] += dot(act, down_w, NN)
    g_up = low(slope * dot(g_out, down_w, NT))
    up_bias_grad[...] = jnp.sum(f32(g_up), 0, keepdims=True)
    u_acc[...] += dot(g_up, up_w, NT)
    d_up = low(dot(xs[...], g_up, NN))
    at = pl.ds(pl.multiple_of(j * STEP, STEP), STEP)
    keep[:, at] = d_up[: D // 2]
    away[:, at] = d_up[D // 2 :]
    d_down = low(dot(jnp.transpose(act), g_out, NN))
    for i in range(STEP // hk // 2):
        even = d_down[2 * i * hk : (2 * i + 1) * hk]
        odd = d_down[(2 * i + 1) * hk : (2 * i + 2) * hk]
        mine, other = jnp.where(core == 0, even, odd), jnp.where(core == 0, odd, even)
        to = pl.ds(pl.multiple_of((i * (STEP // hk // 2) + j) * rk, rk), rk)
        for q in range(hk // rk):
            cols = slice(HALF + q * D, HALF + (q + 1) * D)
            keep[to, cols] = mine[q * rk : (q + 1) * rk]
            away[to, cols] = other[q * rk : (q + 1) * rk]

    if last:

        @pl.when(j == pl.num_programs(0) - 1)
        def _():
            h = hidden[...]
            output[...] = low(h + out_acc[...] + rows[1:2, :])
            r = lax.rsqrt(jnp.mean(h * h, -1, keepdims=True) + 1e-06)
            n = h * r
            u = u_acc[...]
            ug = u * rows[0:1, :]
            g = f32(og[...]) + r * (ug - n * jnp.mean(ug * n, -1, keepdims=True))
            grad[...] = g
            branch[...] = low(g)
            sums[0:1, :] = jnp.sum(u * n, 0, keepdims=True)
            sums[1:2, :] = jnp.sum(f32(og[...]), 0, keepdims=True)


def mlp_half(core_of, hidden, og, rows, up_bias, up, down, before):
    last = before is not None
    whole = lambda a, b: pl.BlockSpec((a, b), lambda j: (0, 0))
    tall = lambda a, b: pl.BlockSpec((a, b), lambda j: (0, 0), pipeline_mode=pl.Buffered(1))
    acc = jax.ShapeDtypeStruct((BLK, D), jnp.float32)
    lows = jax.ShapeDtypeStruct((BLK, D), jnp.bfloat16)
    grads = jax.ShapeDtypeStruct((D // 2, 2 * HALF), jnp.bfloat16)
    return pl.pallas_call(
        functools.partial(mlp_body, last, core_of),
        grid=(HALF // STEP,),
        in_specs=[
            tall(BLK, D),
            tall(BLK, D),
            whole(8, D),
            pl.BlockSpec((1, STEP), lambda j: (0, j)),
            pl.BlockSpec((D, STEP), lambda j: (0, j)),
            pl.BlockSpec((STEP, D), lambda j: (j, 0)),
        ]
        + [tall(BLK, D)] * (2 if last else 0),
        out_specs=[tall(D // 2, 2 * HALF)] * 2
        + [pl.BlockSpec((1, STEP), lambda j: (0, j))]
        + ([tall(BLK, D)] * 3 + [whole(8, D)] if last else [tall(BLK, D)] * 2),
        out_shape=[grads, grads, jax.ShapeDtypeStruct((1, HALF), jnp.float32)]
        + (
            [lows, acc, lows, jax.ShapeDtypeStruct((8, D), jnp.float32)]
            if last
            else [acc, acc]
        ),
        scratch_shapes=[pltpu.VMEM((BLK, D), jnp.bfloat16), pltpu.VMEM((D, BLK), jnp.bfloat16)]
        + ([pltpu.VMEM((BLK, D), jnp.float32)] * 2 if last else []),
        compiler_params=pltpu.CompilerParams(vmem_limit_bytes=58 * 2**20),
        cost_estimate=pl.CostEstimate(
            flops=12 * BLK * D * HALF, bytes_accessed=30 * 2**20, transcendentals=BLK * HALF
        ),
        name="mlp_half",
    )(hidden, og, rows, up_bias, up, down, *(before or ()))


def weight_grads_body(core_of, plan, columns, *refs):
    keep, away, split = refs[-3:]
    core = core_of()
    rk = D // CHUNKS

    def put(pairs, first):
        for chip, (even, odd) in enumerate(pairs):
            to = owner_row(chip) * rk
            at = slice(to, to + rk), slice(first, first + even.shape[1])
            keep[at] = jnp.where(core == 0, even, odd)
            away[at] = jnp.where(core == 0, odd, even)

    for (kind, ins), first in zip(plan, columns):
        if kind == "dot":
            nt = jnp.transpose(refs[ins[0]][...])
            for i in range(CHUNKS):
                to = owner_row(i // 2) * rk + lax.rem(i % 2 + core, 2) * (D // 2)
                split[pl.ds(pl.multiple_of(to, rk), rk), :] = nt[i * rk : (i + 1) * rk]
            for i in ins[1:]:
                width = refs[i].shape[-1]
                for s in range(0, width, 512):
                    n = min(512, width - s)
                    g = low(dot(split[...], refs[i][:, s : s + n], NN))
                    keep[:, first + s : first + s + n] = g[: D // 2]
                    away[:, first + s : first + s + n] = g[D // 2 :]
                first += width
        else:
            a = refs[ins[0]][...]
            if kind == "transposed":
                a = low(jnp.transpose(a))
            put(
                [
                    (a[i * rk : (i + 1) * rk], a[(i + 1) * rk : (i + 2) * rk])
                    for i in range(0, CHUNKS, 2)
                ],
                first,
            )


def weight_grads(core_of, plan):
    args, steps, columns, width, flops = [], [], [], 0, 0
    for kind, *arrays in plan:
        steps.append((kind, tuple(range(len(args), len(args) + len(arrays)))))
        args += arrays
        columns.append(width)
        if kind == "dot":
            n = sum(a.shape[1] for a in arrays[1:])
            flops += 2 * BLK * D * n
        else:
            n = arrays[0].shape[1 if kind == "rows" else 0]
        width += n
    return pl.pallas_call(
        functools.partial(weight_grads_body, core_of, steps, columns),
        out_shape=[jax.ShapeDtypeStruct((D // 2, width), jnp.bfloat16)] * 2,
        scratch_shapes=[pltpu.VMEM((D, BLK), jnp.bfloat16)],
        compiler_params=pltpu.CompilerParams(vmem_limit_bytes=48 * 2**20),
        cost_estimate=pl.CostEstimate(
            flops=flops, bytes_accessed=4 * D * width, transcendentals=0
        ),
        name="weight_grads",
    )(*args)


def natural(keep, away):
    parts = [a.reshape(4, 4, -1, a.shape[1]).transpose(1, 0, 2, 3) for a in (keep, away)]
    return jnp.stack(parts, 2).reshape(-1, keep.shape[1])


def layer(
    fast,
    char_ids,
    char_table,
    attn_gain,
    query_weight,
    key_weight,
    value_weight,
    out_weight,
    state_key_weight,
    state_value_weight,
    update_weight,
    state_query,
    state_init,
    gate_bias,
    position_table,
    mlp_gain,
    up_weight,
    up_bias,
    down_weight,
    down_bias,
    out_grad,
):
    rows = attn_gain.shape[0]
    ff = up_weight.shape[1]
    folds = ff // D
    core_of = (lambda: lax.rem(lax.axis_index("seq"), 2)) if fast else (lambda: jnp.int32(0))
    vectors = jnp.concatenate(
        [v.reshape(rows, -1) for v in (attn_gain, mlp_gain, gate_bias, down_bias, up_bias)], 1
    )
    vectors = jnp.pad(vectors, ((0, 0), (0, VEC - vectors.shape[1])))
    main = VOCAB + VEC
    layouts = (
        ((0, main, 1), (main, 3 * D, 1), (main + 3 * D, NSTATE, 1)),
        ((0, NSTATE, 1), (NSTATE, D, 1), (NSTATE + D, 2 * D, 1), (NSTATE + 3 * D, D, 1)),
        ((0, HALF, 1), (HALF, D, folds // 2)),
    )
    packed = [
        jnp.concatenate(
            [char_table, vectors, query_weight, key_weight, value_weight, state_query], 1
        ),
        jnp.concatenate(
            [state_init, update_weight, state_key_weight, state_value_weight, out_weight], 1
        ),
    ]
    if fast:
        packed += [
            jnp.concatenate([up, fold(down, rows)], 1)
            for up, down in zip(halves_of_columns(up_weight), halves_of_rows(down_weight, 1))
        ]
        p1 = stack_z(packed[0], *along_z(packed[0]))
        shard = tie(packed[1], p1)
        sides1, z2 = join(to_sides(p1), along_z(shard))
        corner1, p2 = join(to_corner(p1, sides1), stack_z(shard, *z2))
        shard = tie(packed[2], p2)
        sides2, z3 = to_sides(p2), along_z(shard)
        table_vec, qkv_full, squery_full = full(p1, sides1, corner1, layouts[0])
    else:
        table_vec, qkv_full, squery_full = gather_any(packed[0], layouts[0])

    columns = jnp.transpose(f32(table_vec[:, VOCAB : VOCAB + 4]))
    gain_attn, gain_mlp, gbias_full, downbias_full = (columns[i] for i in range(4))
    mlp_rows = jnp.pad(jnp.stack([gain_mlp, downbias_full]), ((0, 6), (0, 0)))
    upbias_full = f32(table_vec[:, VOCAB + 4 : VOCAB + 4 + folds]).reshape(1, ff)
    keep_gate = jax.nn.sigmoid(gbias_full)
    is_first = lax.axis_index("seq") == 0
    bias_rows = f32(position_table)[:, None, :]

    one_hot = (char_ids[:, None] == jnp.arange(VOCAB)[None, :]).astype(jnp.bfloat16)
    embedded = dot(one_hot, table_vec[:, :VOCAB], NT)
    attn_scale = norm_scale(embedded)
    normed_low = low(embedded * attn_scale * gain_attn)
    qkv = low(dot(normed_low, qkv_full, NN))
    prev = from_behind(qkv[:, D:], "seq", 1)
    state_mix, state_lse = state_attention(qkv, squery_full)
    if fast:
        sides2, z3, state_mix = join(sides2, z3, state_mix)
        corner2, p3 = join(to_corner(p2, sides2), stack_z(shard, *z3))
        shard = tie(packed[3], p3)
        sides3, z4 = to_sides(p3), along_z(shard)
        sinit_full, update_full, skv_full, out_full = full(p2, sides2, corner2, layouts[1])
    else:
        sinit_full, update_full, skv_full, out_full = gather_any(packed[1], layouts[1])
    update = dot(state_mix, update_full, NN)
    start = f32(join(jnp.transpose(sinit_full))[0])
    mine = low((1.0 - keep_gate) * update)
    if fast:
        state_prev = earlier_sum(keep_gate, mine, start)
    else:
        gain, total = entering(keep_gate, mine, False)
        state_prev = gain * start + total
    state_low = low(state_prev)
    skv = low(dot(state_low, skv_full, NN))
    if fast:
        sides3, z4, skv, prev = join(sides3, z4, skv, prev)
        corner3, p4 = to_corner(p3, sides3), stack_z(shard, *z4)
    mixed, lse = attention(qkv, prev, skv, bias_rows)
    if fast:
        corner3, p4, mixed = join(corner3, p4, mixed)
    hidden = embedded + dot(mixed, out_full, NN)

    biases = halves_of_columns(upbias_full)
    if fast:
        sides4 = to_sides(p4)
        keep_a, away_a, bias_a, *before = mlp_half(
            core_of,
            hidden,
            out_grad,
            mlp_rows,
            biases[0],
            *full(p3, sides3, corner3, layouts[2]),
            None,
        )
        sides4, away_a, before = join(sides4, away_a, before)
        corner4, got_a = join(to_corner(p4, sides4), to_core(away_a))
        corner_a = from_corner(keep_a, got_a)
        keep_b, away_b, bias_b, *before = mlp_half(
            core_of,
            hidden,
            out_grad,
            mlp_rows,
            biases[1],
            *full(p4, sides4, corner4, layouts[2]),
            before,
        )
        corner_a, away_b, before = join(corner_a, away_b, before)
    else:
        shard = jnp.concatenate([up_weight, fold(down_weight, rows)], 1)
        up_full, down_full = gather_any(shard, ((0, ff, 1), (ff, D, folds)))
        mlp_weights = list(zip(halves_of_columns(up_full), halves_of_rows(down_full, CHUNKS)))
        keep_a, away_a, bias_a, *before = mlp_half(
            core_of, hidden, out_grad, mlp_rows, biases[0], *mlp_weights[0], None
        )
        keep_b, away_b, bias_b, *before = mlp_half(
            core_of, hidden, out_grad, mlp_rows, biases[1], *mlp_weights[1], before
        )
    output, grad_hidden, grad_branch, mlp_sums = before
    up_bias_grad = jnp.concatenate([b.reshape(CHUNKS, -1) for b in (bias_a, bias_b)], 1)

    grad_mixed = low(dot(grad_branch, out_full, NT))
    if fast:
        side_a, got_b, grad_mixed = join(
            from_side(keep_a, got_a, corner_a[0]), to_core(away_b), grad_mixed
        )
        ends_a = from_ends(keep_a, got_a, side_a, corner_a[1])
        corner_b = from_corner(keep_b, got_b)
    gq, gkv, gprev, gstate, gbias = attention_back(qkv, prev, skv, bias_rows, lse, grad_mixed)
    if fast:
        ends_a, corner_b, gprev, gstate = join(ends_a, corner_b, gprev, gstate)
    gnext = from_behind(gprev, "seq", -1)
    read = dot(gstate[0], skv_full[:, :D], NT) + dot(gstate[1], skv_full[:, D:], NT)
    first = weight_grads(
        core_of, [("dot", mixed, grad_branch), ("dot", state_low, gstate[0], gstate[1])]
    )
    if fast:
        side_b, got_c = from_side(keep_b, got_b, corner_b[0]), to_core(first[1])
        after = later_sum(keep_gate, low(read))
    else:
        after = entering(keep_gate, low(read), True)[1]
    gate_term = jnp.sum(after * (state_prev - update), 0)
    gate_bias_grad = gate_term * keep_gate * (1.0 - keep_gate)
    state_init_grad = jnp.where(is_first, read + keep_gate * after, 0.0)
    grad_update = low((1.0 - keep_gate) * after)
    grad_smix = low(dot(grad_update, update_full, NT))
    if fast:
        side_b, got_c, grad_smix = join(side_b, got_c, grad_smix)
        ends_b = from_ends(keep_b, got_b, side_b, corner_b[1])
        corner_c = from_corner(first[0], got_c)
    gsum, gquery = state_attention_back(qkv, squery_full, state_lse, grad_smix, gkv)
    second = weight_grads(
        core_of,
        [
            ("dot", state_mix, grad_update),
            ("rows", gquery),
            ("transposed", state_init_grad),
            ("dot", normed_low, gq),
        ],
    )
    if fast:
        ends_b, corner_c, second, gsum = join(ends_b, corner_c, second, gsum)
        side_c, got_d = from_side(first[0], got_c, corner_c[0]), to_core(second[1])
    gk, gv = (low(gsum[i] + f32(gnext[i])) for i in range(2))
    grad_normed = sum(
        dot(g, qkv_full[:, i * D : (i + 1) * D], NT) for i, g in enumerate((gq, gk, gv))
    )
    normed = embedded * attn_scale
    gained = grad_normed * gain_attn
    embedded_grad = grad_hidden + attn_scale * (
        gained - normed * jnp.mean(gained * normed, -1, keepdims=True)
    )
    attn_gain_grad = jnp.sum(grad_normed * normed, 0)
    position_rows = jnp.pad(gbias.reshape(HEADS, BLK), ((0, HEADS), (0, 0)))
    position_table_grad = jnp.sum(lax.all_gather(position_rows, AX), 0)[:HEADS]
    vector_grads = jnp.concatenate(
        [v[None] for v in (attn_gain_grad, mlp_sums[0], gate_bias_grad, mlp_sums[1])]
        + [jnp.transpose(up_bias_grad.reshape(D, folds))],
        0,
    )
    vector_grads = jnp.pad(vector_grads, ((0, VEC - vector_grads.shape[0]), (0, 0)))
    embedded_low = low(embedded_grad)
    if fast:
        side_c, got_d, embedded_low = join(side_c, got_d, embedded_low)
        ends_c = from_ends(first[0], got_c, side_c, corner_c[1])
        corner_d = from_corner(second[0], got_d)
    last = weight_grads(
        core_of,
        [
            ("dot", normed_low, gk, gv),
            ("dot", embedded_low, one_hot),
            ("transposed", vector_grads),
        ],
    )
    if fast:
        ends_c, corner_d, last = join(ends_c, corner_d, last)
        side_d, got_e = join(from_side(second[0], got_d, corner_d[0]), to_core(last[1]))
        ends_d = from_ends(second[0], got_d, side_d, corner_d[1])
        corner_e = from_corner(last[0], got_e)
        ends_d, corner_e = join(ends_d, corner_e)
        side_e = from_side(last[0], got_e, corner_e[0])
        ends_e = from_ends(last[0], got_e, side_e, corner_e[1])
        sums = [finish(s) for s in (ends_a, ends_b, ends_c, ends_d, ends_e)]
        up_sum = jnp.concatenate([s[:, :HALF].reshape(rows, CHUNKS, -1) for s in sums[:2]], 2)
        up_sum = up_sum.reshape(rows, ff)
        down_sum = jnp.concatenate([unfold(s[:, HALF:]) for s in sums[:2]], 0)
        first, second, last = sums[2:]
    else:
        pairs = [natural(keep_a, away_a), natural(keep_b, away_b)]
        up_sum = jnp.concatenate([s[:, :HALF].reshape(D, CHUNKS, -1) for s in pairs], 2)
        up_sum = scatter_any(up_sum.reshape(D, ff))
        down_sum = jnp.concatenate(
            [
                s[:, HALF:].reshape(CHUNKS, D // CHUNKS, -1, D).transpose(0, 2, 1, 3)
                for s in pairs
            ],
            1,
        )
        down_sum = scatter_any(down_sum.reshape(ff, D))
        first, second, last = (scatter_any(natural(*s)) for s in (first, second, last))
    table_at = 2 * D
    vector_sum = last[:, table_at + VOCAB :]
    return (
        output,
        embedded_grad,
        last[:, table_at : table_at + VOCAB],
        vector_sum[:, 0],
        second[:, 2 * D :],
        last[:, :D],
        last[:, D : 2 * D],
        first[:, :D],
        first[:, D : 2 * D],
        first[:, 2 * D :],
        second[:, :D],
        second[:, D : D + NSTATE],
        second[:, D + NSTATE : 2 * D],
        vector_sum[:, 2],
        position_table_grad,
        vector_sum[:, 1],
        up_sum,
        vector_sum[:, 4 : 4 + folds].reshape(-1),
        down_sum,
        vector_sum[:, 3],
    )


def solution(mesh):
    fast = dict(mesh.shape) == {"dp": 8, "seq": 4}
    return jax.shard_map(
        functools.partial(layer, fast),
        mesh=mesh,
        in_specs=(
            P(("dp", "seq")),
            P(("dp", "seq"), None),
            P(("dp", "seq")),
            P(("dp", "seq"), None),
            P(("dp", "seq"), None),
            P(("dp", "seq"), None),
            P(("dp", "seq"), None),
            P(("dp", "seq"), None),
            P(("dp", "seq"), None),
            P(("dp", "seq"), None),
            P(("dp", "seq"), None),
            P(("dp", "seq"), None),
            P(("dp", "seq")),
            P(),
            P(("dp", "seq")),
            P(("dp", "seq"), None),
            P(("dp", "seq")),
            P(("dp", "seq"), None),
            P(("dp", "seq")),
            P(("dp", "seq"), None),
        ),
        out_specs=(
            P(("dp", "seq"), None),
            P(("dp", "seq"), None),
            P(("dp", "seq"), None),
            P(("dp", "seq")),
            P(("dp", "seq"), None),
            P(("dp", "seq"), None),
            P(("dp", "seq"), None),
            P(("dp", "seq"), None),
            P(("dp", "seq"), None),
            P(("dp", "seq"), None),
            P(("dp", "seq"), None),
            P(("dp", "seq"), None),
            P(("dp", "seq"), None),
            P(("dp", "seq")),
            P(),
            P(("dp", "seq")),
            P(("dp", "seq"), None),
            P(("dp", "seq")),
            P(("dp", "seq"), None),
            P(("dp", "seq")),
        ),
        check_vma=False,
    )
```

```python
import functools

import jax
import jax.numpy as jnp
from jax import lax
from jax.experimental import pallas as pl
from jax.experimental.pallas import tpu as pltpu
from jax.sharding import PartitionSpec as P

D = 1024
HEADS = 8
HD = 128
NSTATE = 512
VOCAB = 256
BLK = 512
AX = ("dp", "seq")
VEC = 128


def f32(v):
    return v.astype(jnp.float32)


def low(v):
    return v.astype(jnp.bfloat16)


def route(move):
    pairs = []
    for z in range(4):
        for y in range(2):
            for x in range(2):
                for c in range(2):
                    tz, ty, tx, tc = move(z, y, x, c)
                    pairs.append((z * 8 + y * 4 + x * 2 + c, tz * 8 + ty * 4 + tx * 2 + tc))
    return pairs


A_ROUTE = route(lambda z, y, x, c: (z, y, 1 - x, c) if c == 0 else (z, 1 - y, x, c))
B_ROUTE = route(lambda z, y, x, c: (z, 1 - y, x, c) if c == 0 else (z, y, 1 - x, c))
CORE_ROUTE = route(lambda z, y, x, c: (z, y, x, 1 - c))
X_ROUTE = route(lambda z, y, x, c: (z, y, 1 - x, c))
Y_ROUTE = route(lambda z, y, x, c: (z, 1 - y, x, c))
Z_NEAR = route(lambda z, y, x, c: (z ^ 1, y, x, c))
Z_FAR = route(lambda z, y, x, c: (z ^ 2, y, x, c))
Z_ROUTE = {k: route(lambda z, y, x, c, k=k: ((z + k) % 4, y, x, c)) for k in (1, 2, 3)}


def place():
    d, s = lax.axis_index("dp"), lax.axis_index("seq")
    return d // 2, d % 2, s // 2, s % 2


def send(v, pairs):
    return lax.ppermute(v, AX, pairs)


def stack_z(shard, *others):
    others, cyclic = others[:3], others[3]

    def body(*refs):
        z = lax.axis_index("dp") // 2
        near = z + 1 - 2 * lax.rem(z, 2)
        spots = (
            [lax.rem(z + 4 - i, 4) for i in range(4)]
            if cyclic
            else [z, near, lax.rem(z + 2, 4), lax.rem(near + 2, 4)]
        )
        for at, src in zip(spots, refs[:4]):
            refs[4][at] = src[...]

    return pl.pallas_call(
        body, out_shape=jax.ShapeDtypeStruct((4,) + shard.shape, shard.dtype), name="stack_z"
    )(shard, *others)


def here():
    return lax.rem(lax.axis_index("dp"), 2), lax.axis_index("seq") // 2, core_index()


def core_index():
    return lax.rem(lax.axis_index("seq"), 2)


def origin(i, spot, alternate):
    y, x, c = spot
    core = c if i < 4 else 1 - c
    if alternate:
        flip_x = (0, 1 - core, core, 1)[i % 4]
        flip_y = (0, core, 1 - core, 1)[i % 4]
    else:
        flip_x, flip_y = i % 2, i % 4 // 2
    return lax.rem(y + flip_y, 2), lax.rem(x + flip_x, 2), core


def assemble(pieces, layout, alternate):
    rows, width = pieces[0].shape[1:]

    def body(*refs):
        ins, outs = refs[:8], refs[8:]
        spot = here()
        for i, src in enumerate(ins):
            ty, tx, core = origin(i, spot, alternate)
            for (first, w, folds), out in zip(layout, outs):
                for q in range(folds):
                    out[0, ty, tx, core, q * rows : (q + 1) * rows, :] = src[
                        0, :, first + q * w : first + (q + 1) * w
                    ]

    full = pl.pallas_call(
        body,
        out_shape=[
            jax.ShapeDtypeStruct((4, 2, 2, 2, rows * n, w), pieces[0].dtype) for _, w, n in layout
        ],
        grid=(4,),
        in_specs=[pl.BlockSpec((1, rows, width), lambda z: (z, 0, 0))] * 8,
        out_specs=[
            pl.BlockSpec((1, 2, 2, 2, rows * n, w), lambda z: (z, 0, 0, 0, 0, 0))
            for _, w, n in layout
        ],
        compiler_params=pltpu.CompilerParams(vmem_limit_bytes=40 * 2**20),
        name="assemble",
    )(*pieces)
    return [o.reshape(32 * rows * n, w) for o, (_, w, n) in zip(full, layout)]


def tie(value, *others):
    return lax.optimization_barrier((value, others))[0]


def join(*values):
    return lax.optimization_barrier(values)


def along_z(shard):
    return [send(shard, Z_ROUTE[k]) for k in (1, 2, 3)] + [True]


def far_z(shard, near):
    return [near, send(shard, Z_FAR), send(near, Z_FAR), False]


def to_sides(p, a=A_ROUTE, b=B_ROUTE):
    return send(p, a), send(p, b)


def to_corner(p, sides, b=B_ROUTE):
    return send(sides[0], b), [send(v, CORE_ROUTE) for v in (p,) + tuple(sides)]


def last_corner(corner):
    return send(corner[0], CORE_ROUTE)


def pieces(p, sides, corner, last):
    return (p,) + tuple(sides) + (corner[0],) + tuple(corner[1]) + (last,)


def to_core(away):
    return send(away, CORE_ROUTE)


def first_axis():
    z, y, x, c = place()
    return jnp.where(c == 0, y, x), jnp.where(c == 0, x, y)


def chip_part(keep, got, b, a=None):
    rows, width = keep.shape[0] // 16, keep.shape[1]
    start, size = ((b, 0), (1, 2)) if a is None else ((b, a), (1, 1))
    at = [
        lax.dynamic_slice(
            v.reshape(2, 2, 4, rows, width), start + (0, 0, 0), size + (4, rows, width)
        )
        for v in (keep, got)
    ]
    return (f32(at[0]) + f32(at[1])).reshape(size[1], 4, rows, width)


def over_first(keep, got):
    return send(low(chip_part(keep, got, 1 - first_axis()[0])), B_ROUTE)


def over_first_in_two(keep, got, corner):
    b, a = first_axis()
    return send(low(chip_part(keep, got, 1 - b, 1 - a if corner else a)), B_ROUTE)


def of_first(first, i):
    return lax.dynamic_index_in_dim(first, i, 0)


def over_second(keep, got, first):
    b, a = first_axis()
    far = first[0] if isinstance(first, tuple) else of_first(first, 1 - a)
    return send(low(chip_part(keep, got, b, 1 - a) + f32(far)), A_ROUTE)


def own_part(keep, got, first, second):
    b, a = first_axis()
    mine = first[1] if isinstance(first, tuple) else of_first(first, a)
    return (chip_part(keep, got, b, a) + f32(mine) + f32(second))[0]


def over_pairs(keep, got, first, second):
    z = place()[0]
    own = own_part(keep, got, first, second)
    pairs = own.reshape((2, 2) + own.shape[1:])
    away = lax.dynamic_index_in_dim(pairs, 1 - z // 2, 0, False)
    return lax.dynamic_index_in_dim(pairs, z // 2, 0, False), send(low(away), Z_FAR)


def within_pair(mine, got):
    z = place()[0]

    def pick(i):
        return lax.dynamic_index_in_dim(mine, i, 0, False) + f32(
            lax.dynamic_index_in_dim(got, i, 0, False)
        )

    return pick(z % 2), send(low(pick(1 - z % 2)), Z_NEAR)


def over_z(keep, got, first, second):
    z = place()[0]
    own = own_part(keep, got, first, second)
    rest = [low(lax.dynamic_index_in_dim(own, (z + k) % 4, 0, False)) for k in (1, 2, 3)]
    mine = lax.dynamic_index_in_dim(own, z, 0, False)
    return [mine] + [send(v, Z_ROUTE[k]) for v, k in zip(rest, (1, 2, 3))]


def finish(parts):
    return sum(f32(p) for p in parts)


def gather_any(shard, layout):
    rows = shard.shape[0]
    full = lax.all_gather(shard, AX, axis=0, tiled=True)
    outs = []
    for first, w, folds in layout:
        part = full[:, first : first + w * folds]
        if folds > 1:
            part = part.reshape(-1, rows, folds, w).transpose(0, 2, 1, 3).reshape(-1, w)
        outs.append(part)
    return outs


def scatter_any(grad):
    return lax.psum_scatter(f32(grad), AX, scatter_dimension=0, tiled=True)


def exchange(value, pairs):
    return value + send(value, pairs)


def half_across(chip):
    c = place()[3]
    half = NSTATE // 2
    return send(lax.dynamic_slice(chip, (c * half, 0), (half, D)), X_ROUTE)


def both_halves(near):
    c = place()[3]
    far = send(near, CORE_ROUTE)
    return jnp.concatenate([jnp.where(c == 0, near, far), jnp.where(c == 0, far, near)], 0)


def in_order(mine, sibling):
    c = place()[3]
    return jnp.where(c == 0, f32(mine), f32(sibling)), jnp.where(c == 0, f32(sibling), f32(mine))


def earlier_near(keep_gate, mine, sibling):
    first, second = in_order(mine, sibling)
    return half_across(low(keep_gate * first + second))


def earlier_sum(keep_gate, near, sibling, start):
    z, y, x, c = place()
    other = both_halves(near)
    before = jnp.where(x == 0, start, keep_gate * keep_gate * start + f32(other))
    return jnp.where(c == 0, before, keep_gate * before + f32(sibling))


def later_near(keep_gate, mine, sibling):
    first, second = in_order(mine, sibling)
    return half_across(low(first + keep_gate * second))


def later_sum(keep_gate, near, sibling):
    z, y, x, c = place()
    after = jnp.where(x == 0, f32(both_halves(near)), 0.0)
    return jnp.where(c == 0, f32(sibling) + keep_gate * after, after)


def from_behind(block, axis, distance):
    devices = range(lax.axis_size(axis))
    pairs = [(i - distance, i) for i in devices if i - distance in devices]
    return lax.ppermute(block, axis, pairs)


def entering(keep_gate, mine, reverse):
    devices, at_home = lax.axis_size("seq"), lax.axis_index("seq")
    everything = lax.all_gather(mine, "seq")

    def turn(k, before):
        at = devices - 1 - k if reverse else k
        reached = at > at_home if reverse else at < at_home
        gain, total = before
        return (
            jnp.where(reached, gain * keep_gate, gain),
            jnp.where(reached, keep_gate * total + f32(everything[at]), total),
        )

    start = (jnp.ones_like(keep_gate), jnp.zeros(mine.shape, jnp.float32))
    return lax.fori_loop(0, devices, turn, start)


def norm_scale(values):
    return lax.rsqrt(jnp.mean(values * values, -1, keepdims=True) + 1e-06)


def halves_of_columns(a):
    parts = a.reshape(a.shape[0], CHUNKS, 2, -1)
    return [parts[:, :, i].reshape(a.shape[0], -1) for i in range(2)]


def halves_of_rows(a, chunks):
    parts = a.reshape(chunks, 2, -1, a.shape[1])
    return [parts[:, i].reshape(-1, a.shape[1]) for i in range(2)]


def fold(a, rows):
    return a.reshape(-1, rows, D).transpose(1, 0, 2).reshape(rows, -1)


def unfold(a):
    rows = a.shape[0]
    return a.reshape(rows, -1, D).transpose(1, 0, 2).reshape(-1, D)


SCALE = HD ** (-0.5)


def dot(a, b, dims):
    return lax.dot_general(a, b, (dims, ((), ())), preferred_element_type=jnp.float32)


NN, NT, TN = ((1,), (0,)), ((1,), (1,)), ((0,), (0,))


def head_block(first):
    return pl.BlockSpec((BLK, HD), lambda h: (0, first + h))


def pair_block():
    return pl.BlockSpec((2, BLK, HD), lambda h: (0, 0, h))


def row_block():
    return pl.BlockSpec((1, 1, BLK), lambda h: (h, 0, 0))


def token_scores(q, k, kp, bias_row, is_first):
    row = lax.broadcasted_iota(jnp.int32, (BLK, BLK), 0)
    col = lax.broadcasted_iota(jnp.int32, (BLK, BLK), 1)
    own = row <= col
    bias = jnp.concatenate([bias_row] + [pltpu.roll(bias_row, i, 1) for i in range(1, 8)], 0)
    while bias.shape[0] < BLK:
        bias = jnp.concatenate([bias, pltpu.roll(bias, bias.shape[0], 1)], 0)
    raw = jnp.where(own, dot(k, q, NT), dot(kp, q, NT))
    scores = raw * SCALE + bias
    return jnp.where(own | jnp.logical_not(is_first), scores, -1e30), own


def attention_body(q, k, v, kp, vp, sk, sv, bias, mixed, lse):
    is_first = lax.axis_index("seq") == 0
    q = q[...]
    tokens, own = token_scores(q, k[...], kp[...], bias[0], is_first)
    states = dot(sk[...], q, NT) * SCALE
    top = jnp.maximum(jnp.max(tokens, 0, keepdims=True), jnp.max(states, 0, keepdims=True))
    tokens, states = jnp.exp(tokens - top), jnp.exp(states - top)
    total = jnp.sum(tokens, 0, keepdims=True) + jnp.sum(states, 0, keepdims=True)
    lse[0] = top + jnp.log(total)
    mix = dot(jnp.transpose(v[...]), low(jnp.where(own, tokens, 0.0)), NN)
    mix += dot(jnp.transpose(vp[...]), low(jnp.where(own, 0.0, tokens)), NN)
    mix += dot(jnp.transpose(sv[...]), low(states), NN)
    mixed[...] = low(jnp.transpose(mix * (1.0 / total)))


def attention(query, kv, prev, skv, bias):
    return pl.pallas_call(
        attention_body,
        grid=(HEADS,),
        in_specs=[head_block(0)]
        + [head_block(0), head_block(HEADS)] * 3
        + [row_block()],
        out_specs=[head_block(0), row_block()],
        out_shape=[
            jax.ShapeDtypeStruct((BLK, D), jnp.bfloat16),
            jax.ShapeDtypeStruct((HEADS, 1, BLK), jnp.float32),
        ],
        compiler_params=pltpu.CompilerParams(vmem_limit_bytes=40 * 2**20),
        cost_estimate=pl.CostEstimate(
            flops=12 * HEADS * BLK * BLK * HD,
            bytes_accessed=9 * 2**20,
            transcendentals=2 * HEADS * BLK * BLK,
        ),
        name="attention",
    )(query, kv, kv, prev, prev, skv, skv, bias)


def attention_back_body(
    q, k, v, kp, vp, sk, sv, bias, lse, go, gq, gkv, gprev, gstate, gbias
):
    is_first = lax.axis_index("seq") == 0
    q, k, kp, sk, go = q[...], k[...], kp[...], sk[...], go[...]
    tokens, own = token_scores(q, k, kp, bias[0], is_first)
    log_total = lse[0]
    tokens = jnp.exp(tokens - log_total)
    states = jnp.exp(dot(sk, q, NT) * SCALE - log_total)
    gtokens = jnp.where(own, dot(v[...], go, NT), dot(vp[...], go, NT))
    gstates = dot(sv[...], go, NT)
    mean = jnp.sum(tokens * gtokens, 0, keepdims=True) + jnp.sum(states * gstates, 0, keepdims=True)
    gkv[1] = dot(low(jnp.where(own, tokens, 0.0)), go, NN)
    gprev[1] = low(dot(low(jnp.where(own, 0.0, tokens)), go, NN))
    gstate[1] = low(dot(low(states), go, NN))
    gtokens = low(tokens * (gtokens - mean))
    gstates = low(states * (gstates - mean))
    wide = f32(gtokens)
    gown, gbefore = low(jnp.where(own, wide, 0.0)), low(jnp.where(own, 0.0, wide))
    gkv[0] = dot(gown, q, NN) * SCALE
    gprev[0] = low(dot(gbefore, q, NN) * SCALE)
    gstate[0] = low(dot(gstates, q, NN) * SCALE)
    g = dot(jnp.transpose(k), gown, NN)
    g += dot(jnp.transpose(kp), gbefore, NN)
    g += dot(jnp.transpose(sk), gstates, NN)
    gq[...] = low(jnp.transpose(g * SCALE))
    rows = BLK
    while rows > 1:
        rows //= 2
        wide = wide[:rows] + pltpu.roll(wide[rows:], BLK - rows, 1)
    gbias[0] = wide


def attention_back(query, kv, prev, skv, bias, lse, go):
    return pl.pallas_call(
        attention_back_body,
        grid=(HEADS,),
        in_specs=[head_block(0)]
        + [head_block(0), head_block(HEADS)] * 3
        + [row_block(), row_block(), head_block(0)],
        out_specs=[head_block(0), pair_block(), pair_block(), pair_block(), row_block()],
        out_shape=[
            jax.ShapeDtypeStruct((BLK, D), jnp.bfloat16),
            jax.ShapeDtypeStruct((2, BLK, D), jnp.float32),
            jax.ShapeDtypeStruct((2, BLK, D), jnp.bfloat16),
            jax.ShapeDtypeStruct((2, BLK, D), jnp.bfloat16),
            jax.ShapeDtypeStruct((HEADS, 1, BLK), jnp.float32),
        ],
        compiler_params=pltpu.CompilerParams(vmem_limit_bytes=48 * 2**20),
        cost_estimate=pl.CostEstimate(
            flops=30 * HEADS * BLK * BLK * HD,
            bytes_accessed=18 * 2**20,
            transcendentals=2 * HEADS * BLK * BLK,
        ),
        name="attention_back",
    )(query, kv, kv, prev, prev, skv, skv, bias, lse, go)


def query_block():
    return pl.BlockSpec((HD, NSTATE), lambda h: (h, 0))


def state_body(k, v, query, mixed, lse):
    scores = dot(k[...], query[...], NN) * SCALE
    top = jnp.max(scores, 0, keepdims=True)
    scores = jnp.exp(scores - top)
    total = jnp.sum(scores, 0, keepdims=True)
    lse[0] = top + jnp.log(total)
    mix = dot(jnp.transpose(v[...]), low(scores), NN)
    mixed[...] = low(jnp.transpose(mix * (1.0 / total)))


def state_attention(kv, query):
    return pl.pallas_call(
        state_body,
        grid=(HEADS,),
        in_specs=[head_block(0), head_block(HEADS), query_block()],
        out_specs=[head_block(0), row_block()],
        out_shape=[
            jax.ShapeDtypeStruct((NSTATE, D), jnp.bfloat16),
            jax.ShapeDtypeStruct((HEADS, 1, NSTATE), jnp.float32),
        ],
        compiler_params=pltpu.CompilerParams(vmem_limit_bytes=32 * 2**20),
        cost_estimate=pl.CostEstimate(
            flops=4 * HEADS * BLK * BLK * HD,
            bytes_accessed=4 * 2**20,
            transcendentals=HEADS * BLK * BLK,
        ),
        name="state_attention",
    )(kv, kv, query)


def state_back_body(k, v, query, lse, go, gkv, gsum, gquery):
    k, query, go = k[...], query[...], go[...]
    probs = jnp.exp(dot(k, query, NN) * SCALE - lse[0])
    gprobs = dot(v[...], go, NT)
    mean = jnp.sum(probs * gprobs, 0, keepdims=True)
    gsum[1] = dot(low(probs), go, NN) + gkv[1]
    gscores = low(probs * (gprobs - mean))
    gsum[0] = dot(gscores, query, NT) * SCALE + gkv[0]
    gquery[...] = low(dot(jnp.transpose(k), gscores, NN) * SCALE)


def state_attention_back(kv, query, lse, go, gkv):
    return pl.pallas_call(
        state_back_body,
        grid=(HEADS,),
        in_specs=[
            head_block(0),
            head_block(HEADS),
            query_block(),
            row_block(),
            head_block(0),
            pair_block(),
        ],
        out_specs=[pair_block(), query_block()],
        out_shape=[
            jax.ShapeDtypeStruct((2, BLK, D), jnp.float32),
            jax.ShapeDtypeStruct((D, NSTATE), jnp.bfloat16),
        ],
        compiler_params=pltpu.CompilerParams(vmem_limit_bytes=32 * 2**20),
        cost_estimate=pl.CostEstimate(
            flops=10 * HEADS * BLK * BLK * HD,
            bytes_accessed=14 * 2**20,
            transcendentals=HEADS * BLK * BLK,
        ),
        name="state_attention_back",
    )(kv, kv, query, lse, go, gkv)


STEP = 512
HALF = 2048
CHUNKS = 32


def owner_row(chip, swap):
    z, y, x = chip // 4, chip // 2 % 2, chip % 2
    return (x * 8 + y * 4 if swap else y * 8 + x * 4) + z


def gelu_parts(x):
    a, b = 0.7978845608028654, 0.044715
    square = x * x
    t = jnp.tanh(a * x * (1.0 + b * square))
    half = 0.5 * (1.0 + t)
    slope = half + (0.5 * a) * x * (1.0 - t * t) * (1.0 + 3.0 * b * square)
    return x * half, slope


def mlp_body(last, spot_of, alternate, *refs):
    hidden, og, rows, up_bias = refs[:4]
    ups, downs, refs = refs[4:12], refs[12:20], refs[20:]
    if last:
        out_in, u_in, keep, away, up_bias_grad, output, grad, branch, sums = refs[:9]
        up, down, xn, xs, out_acc, u_acc = refs[9:]
    else:
        keep, away, up_bias_grad, out_acc, u_acc = refs[:5]
        up, down, xn, xs = refs[5:]
    j = pl.program_id(0)
    spot = spot_of()
    core = spot[2]
    rk = D // CHUNKS
    hk = HALF // CHUNKS

    @pl.when(j == 0)
    def _():
        h = hidden[...]
        r = lax.rsqrt(jnp.mean(h * h, -1, keepdims=True) + 1e-06)
        n = low(h * r * rows[1:2, :])
        xn[...] = n
        nt = jnp.transpose(n)
        for i in range(CHUNKS):
            to = owner_row(i // 2, i % 2) * rk + lax.rem(i % 2 + core, 2) * (D // 2)
            xs[pl.ds(pl.multiple_of(to, rk), rk), :] = nt[i * rk : (i + 1) * rk]
        if last:
            out_acc[...] = out_in[...]
            u_acc[...] = u_in[...]
        else:
            out_acc[...] = jnp.zeros_like(out_acc)
            u_acc[...] = jnp.zeros_like(u_acc)

    for i in range(8):
        ty, tx, c = origin(i, spot, alternate)
        at = ty * 4 + tx * 2 + c
        for z in range(4):
            up[pl.ds(pl.multiple_of((z * 8 + at) * rk, rk), rk), :] = ups[i][z]
        for q in range(hk // rk):
            down[pl.ds(pl.multiple_of(at * hk + q * rk, rk), rk), :] = downs[i][
                0, :, q * D : (q + 1) * D
            ]
    up_w, down_w, g_out = up[...], down[...], og[...]
    act, slope = gelu_parts(dot(xn[...], up_w, NN) + up_bias[...])
    act = low(act)
    out_acc[...] += dot(act, down_w, NN)
    g_up = low(slope * dot(g_out, down_w, NT))
    up_bias_grad[...] = jnp.sum(f32(g_up), 0, keepdims=True)
    u_acc[...] += dot(g_up, up_w, NT)
    d_up = low(dot(xs[...], g_up, NN))
    at = pl.ds(pl.multiple_of(j * STEP, STEP), STEP)
    keep[:, at] = d_up[: D // 2]
    away[:, at] = d_up[D // 2 :]
    d_down = low(dot(jnp.transpose(act), g_out, NN))
    for i in range(STEP // hk // 2):
        even = d_down[2 * i * hk : (2 * i + 1) * hk]
        odd = d_down[(2 * i + 1) * hk : (2 * i + 2) * hk]
        mine, other = jnp.where(core == 0, even, odd), jnp.where(core == 0, odd, even)
        for q in range(hk // rk):
            cols = slice(HALF + q * D, HALF + (q + 1) * D)
            part = slice(q * rk, (q + 1) * rk)
            for out, value, owner in ((keep, mine, core), (away, other, 1 - core)):
                to = jnp.where(owner == 0, owner_row(i, 0), owner_row(i, 1)) + j
                out[pl.ds(pl.multiple_of(to * rk, rk), rk), cols] = value[part]

    if last:

        @pl.when(j == pl.num_programs(0) - 1)
        def _():
            h = hidden[...]
            output[...] = low(h + out_acc[...] + rows[3:4, :])
            r = lax.rsqrt(jnp.mean(h * h, -1, keepdims=True) + 1e-06)
            n = h * r
            u = u_acc[...]
            ug = u * rows[1:2, :]
            g = f32(og[...]) + r * (ug - n * jnp.mean(ug * n, -1, keepdims=True))
            grad[...] = g
            branch[...] = low(g)
            sums[0:1, :] = jnp.sum(u * n, 0, keepdims=True)
            sums[1:2, :] = jnp.sum(f32(og[...]), 0, keepdims=True)


def mlp_half(spot_of, alternate, hidden, og, rows, up_bias, parts, before):
    last = before is not None
    whole = lambda a, b: pl.BlockSpec((a, b), lambda j: (0, 0))
    tall = lambda a, b: pl.BlockSpec((a, b), lambda j: (0, 0), pipeline_mode=pl.Buffered(1))
    acc = jax.ShapeDtypeStruct((BLK, D), jnp.float32)
    lows = jax.ShapeDtypeStruct((BLK, D), jnp.bfloat16)
    width = 2 * HALF + (D if last else 0)
    grads = jax.ShapeDtypeStruct((D // 2, width), jnp.bfloat16)
    return pl.pallas_call(
        functools.partial(mlp_body, last, spot_of, alternate),
        grid=(HALF // STEP,),
        in_specs=[
            tall(BLK, D),
            tall(BLK, D),
            whole(8, D),
            pl.BlockSpec((1, STEP), lambda j: (0, j)),
        ]
        + [pl.BlockSpec((4, D // CHUNKS, STEP), lambda j: (0, 0, j))] * 8
        + [pl.BlockSpec((1, D // CHUNKS, HALF), lambda j: (j, 0, 1))] * 8
        + [tall(BLK, D)] * (2 if last else 0),
        out_specs=[tall(D // 2, 2 * HALF)] * 2
        + [pl.BlockSpec((1, STEP), lambda j: (0, j))]
        + ([tall(BLK, D)] * 3 + [whole(8, D)] if last else [tall(BLK, D)] * 2),
        out_shape=[grads, grads, jax.ShapeDtypeStruct((1, HALF), jnp.float32)]
        + (
            [lows, acc, lows, jax.ShapeDtypeStruct((8, D), jnp.float32)]
            if last
            else [acc, acc]
        ),
        scratch_shapes=[
            pltpu.VMEM((D, STEP), jnp.bfloat16),
            pltpu.VMEM((STEP, D), jnp.bfloat16),
            pltpu.VMEM((BLK, D), jnp.bfloat16),
            pltpu.VMEM((D, BLK), jnp.bfloat16),
        ]
        + ([pltpu.VMEM((BLK, D), jnp.float32)] * 2 if last else []),
        compiler_params=pltpu.CompilerParams(vmem_limit_bytes=58 * 2**20),
        cost_estimate=pl.CostEstimate(
            flops=12 * BLK * D * HALF, bytes_accessed=30 * 2**20, transcendentals=BLK * HALF
        ),
        name="mlp_half",
    )(hidden, og, rows, up_bias, *parts, *parts, *(before or ()))


def weight_grads_body(core_of, plan, columns, *refs):
    keep, away, split = refs[-3:]
    core = core_of()
    rk = D // CHUNKS

    def put(pairs, first):
        for chip, (even, odd) in enumerate(pairs):
            cols = slice(first, first + even.shape[1])
            mine, other = jnp.where(core == 0, even, odd), jnp.where(core == 0, odd, even)
            for out, value, owner in ((keep, mine, core), (away, other, 1 - core)):
                to = jnp.where(owner == 0, owner_row(chip, 0), owner_row(chip, 1))
                out[pl.ds(pl.multiple_of(to * rk, rk), rk), cols] = value

    for (kind, ins), first in zip(plan, columns):
        if kind == "dot":
            nt = jnp.transpose(refs[ins[0]][...])
            for i in range(CHUNKS):
                to = owner_row(i // 2, i % 2) * rk + lax.rem(i % 2 + core, 2) * (D // 2)
                split[pl.ds(pl.multiple_of(to, rk), rk), :] = nt[i * rk : (i + 1) * rk]
            for i in ins[1:]:
                width = refs[i].shape[-1]
                for s in range(0, width, 512):
                    n = min(512, width - s)
                    g = low(dot(split[...], refs[i][:, s : s + n], NN))
                    keep[:, first + s : first + s + n] = g[: D // 2]
                    away[:, first + s : first + s + n] = g[D // 2 :]
                first += width
        else:
            a = refs[ins[0]][...]
            if kind == "transposed":
                a = low(jnp.transpose(a))
            put(
                [
                    (a[i * rk : (i + 1) * rk], a[(i + 1) * rk : (i + 2) * rk])
                    for i in range(0, CHUNKS, 2)
                ],
                first,
            )


def weight_grads(core_of, plan):
    args, steps, columns, width, flops = [], [], [], 0, 0
    for kind, *arrays in plan:
        steps.append((kind, tuple(range(len(args), len(args) + len(arrays)))))
        args += arrays
        columns.append(width)
        if kind == "dot":
            n = sum(a.shape[1] for a in arrays[1:])
            flops += 2 * BLK * D * n
        else:
            n = arrays[0].shape[1 if kind == "rows" else 0]
        width += n
    return pl.pallas_call(
        functools.partial(weight_grads_body, core_of, steps, columns),
        out_shape=[jax.ShapeDtypeStruct((D // 2, width), jnp.bfloat16)] * 2,
        scratch_shapes=[pltpu.VMEM((D, BLK), jnp.bfloat16)],
        compiler_params=pltpu.CompilerParams(vmem_limit_bytes=48 * 2**20),
        cost_estimate=pl.CostEstimate(
            flops=flops, bytes_accessed=4 * D * width, transcendentals=0
        ),
        name="weight_grads",
    )(*args)


def natural(keep, away):
    parts = [a.reshape(2, 2, 4, -1, a.shape[1]).transpose(2, 0, 1, 3, 4) for a in (keep, away)]
    parts[1] = parts[1].transpose(0, 2, 1, 3, 4)
    return jnp.stack(parts, 3).reshape(-1, keep.shape[1])


def out_weight_grad(core_of, mixed, branch, keep, away):
    def body(x, g, keep_in, away_in, keep_out, away_out, split):
        weight_grads_body(
            core_of, [("dot", (0, 1))], [0], x, g, keep_out, away_out, split
        )

    whole = pl.BlockSpec((BLK, D), lambda i: (0, 0))
    here = pl.BlockSpec(memory_space=pl.ANY)
    last = pl.BlockSpec((D // 2, D), lambda i: (0, keep.shape[1] // D - 1))
    return pl.pallas_call(
        body,
        grid=(1,),
        in_specs=[whole, whole, here, here],
        out_specs=[last, last],
        out_shape=[jax.ShapeDtypeStruct(keep.shape, keep.dtype)] * 2,
        input_output_aliases={2: 0, 3: 1},
        scratch_shapes=[pltpu.VMEM((D, BLK), jnp.bfloat16)],
        compiler_params=pltpu.CompilerParams(vmem_limit_bytes=32 * 2**20),
        cost_estimate=pl.CostEstimate(
            flops=2 * BLK * D * D, bytes_accessed=4 * 2**20, transcendentals=0
        ),
        name="out_weight_grad",
    )(mixed, branch, keep, away)


def pack_first(attn_gain, mlp_gain, gate, down_bias, up_bias, *matrices):
    rows = matrices[0].shape[0]
    vectors = [v.reshape(1, -1) for v in (attn_gain, mlp_gain, gate, down_bias, up_bias)]

    def body(a, m, g, d, u, table, *rest):
        out = rest[-1]
        up = f32(u[...])
        column = [f32(v[...]) for v in (a, m, g, d)]
        column += [up[:, i : i + rows] for i in range(0, up.shape[1], rows)]
        column = jnp.transpose(jnp.concatenate(column, 0))
        column = jnp.concatenate(
            [column, jnp.zeros((rows, VEC - column.shape[1]), jnp.float32)], 1
        )
        first = 0
        for part in [table[...], low(column)] + [r[...] for r in rest[:-1]]:
            out[:, first : first + part.shape[1]] = part
            first += part.shape[1]

    return pl.pallas_call(
        body,
        out_shape=jax.ShapeDtypeStruct((rows, VEC + sum(m.shape[1] for m in matrices)), jnp.bfloat16),
        name="pack_first",
    )(*vectors, *matrices)


def pack_rest(query, sinit, skey, svalue, out_weight, up, down):
    rows = query.shape[0]
    half = down.shape[0] // 2

    def body(r, s, k, w, o, up, down, second, third, fourth):
        first = 0
        for part in (r, s, k, w, o):
            second[:, first : first + part.shape[1]] = part[...]
            first += part.shape[1]
        lane = lax.broadcasted_iota(jnp.int32, (rows, 128), 1) < 64
        for i in range(0, CHUNKS, 2):
            a = f32(up[:, i * 128 : (i + 1) * 128])
            b = f32(up[:, (i + 1) * 128 : (i + 2) * 128])
            at = slice(i * 64, i * 64 + 128)
            third[:, at] = low(jnp.where(lane, a, pltpu.roll(b, 64, 1)))
            fourth[:, at] = low(jnp.where(lane, pltpu.roll(a, 64, 1), b))
        for i, out in enumerate((third, fourth)):
            for q in range(half // rows):
                start = i * half + q * rows
                out[:, HALF + q * D : HALF + (q + 1) * D] = down[start : start + rows, :]

    return pl.pallas_call(
        body,
        out_shape=[
            jax.ShapeDtypeStruct((rows, NSTATE + 4 * D), jnp.bfloat16),
            jax.ShapeDtypeStruct((rows, 2 * HALF), jnp.bfloat16),
            jax.ShapeDtypeStruct((rows, 2 * HALF), jnp.bfloat16),
        ],
        name="pack_rest",
    )(query, sinit, skey, svalue, out_weight, up, down)


def readout(gstate, skv_full):
    def body(g, w, read, sent):
        r = dot(g[0], w[:, :D], NT) + dot(g[1], w[:, D:], NT)
        read[...] = r
        sent[...] = low(r)

    return pl.pallas_call(
        body,
        out_shape=[
            jax.ShapeDtypeStruct((NSTATE, D), jnp.float32),
            jax.ShapeDtypeStruct((NSTATE, D), jnp.bfloat16),
        ],
        compiler_params=pltpu.CompilerParams(vmem_limit_bytes=32 * 2**20),
        cost_estimate=pl.CostEstimate(
            flops=4 * NSTATE * D * D, bytes_accessed=9 * 2**20, transcendentals=0
        ),
        name="readout",
    )(gstate, skv_full)


def embedding_back(gq, gk, gv, query_full, kv_full, embedded, grad_hidden, rows):
    def body(q, k, v, wq, w, e, g_out, r, grad, lowered, gain_grad):
        g = dot(q[...], wq[...], NT) + dot(k[...], w[:, :D], NT) + dot(v[...], w[:, D:], NT)
        emb = e[...]
        scale = lax.rsqrt(jnp.mean(emb * emb, -1, keepdims=True) + 1e-06)
        normed = emb * scale
        gain_grad[...] = jnp.broadcast_to(jnp.sum(g * normed, 0, keepdims=True), gain_grad.shape)
        g = g * r[0:1, :]
        g = g_out[...] + scale * (g - normed * jnp.mean(g * normed, -1, keepdims=True))
        grad[...] = g
        lowered[...] = low(g)

    return pl.pallas_call(
        body,
        out_shape=[
            jax.ShapeDtypeStruct((BLK, D), jnp.float32),
            jax.ShapeDtypeStruct((BLK, D), jnp.bfloat16),
            jax.ShapeDtypeStruct((8, D), jnp.float32),
        ],
        compiler_params=pltpu.CompilerParams(vmem_limit_bytes=48 * 2**20),
        cost_estimate=pl.CostEstimate(
            flops=6 * BLK * D * D, bytes_accessed=18 * 2**20, transcendentals=0
        ),
        name="embedding_back",
    )(gq, gk, gv, query_full, kv_full, embedded, grad_hidden, rows)


def layer(
    fast,
    char_ids,
    char_table,
    attn_gain,
    query_weight,
    key_weight,
    value_weight,
    out_weight,
    state_key_weight,
    state_value_weight,
    update_weight,
    state_query,
    state_init,
    gate_bias,
    position_table,
    mlp_gain,
    up_weight,
    up_bias,
    down_weight,
    down_bias,
    out_grad,
):
    rows = attn_gain.shape[0]
    ff = up_weight.shape[1]
    folds = ff // D
    main = VOCAB + VEC
    spot_of = here if fast else (lambda: (jnp.int32(0),) * 3)
    core_of = core_index if fast else (lambda: jnp.int32(0))
    layouts = (
        ((0, main, 1), (main, 2 * D, 1), (main + 2 * D, NSTATE, 1), (main + 2 * D + NSTATE, D, 1)),
        ((0, D, 1), (D, NSTATE, 1), (D + NSTATE, 2 * D, 1), (D + NSTATE + 2 * D, D, 1)),
    )
    if fast:
        shard1 = pack_first(
            attn_gain,
            mlp_gain,
            gate_bias,
            down_bias,
            up_bias,
            char_table,
            key_weight,
            value_weight,
            state_query,
            update_weight,
        )
        z1 = along_z(shard1)
        shard2, shard3, shard4 = pack_rest(
            query_weight,
            state_init,
            state_key_weight,
            state_value_weight,
            out_weight,
            up_weight,
            down_weight,
        )
        z1[:3], shard2, shard3, shard4 = join(z1[:3], shard2, shard3, shard4)
        p1 = stack_z(shard1, *z1)
        shard2 = tie(shard2, p1)
        z2 = along_z(shard2)
        sides1, z2[:3] = join(to_sides(p1), z2[:3])
        shard3, p2 = join(shard3, stack_z(shard2, *z2))
        corner1, near3 = join(to_corner(p1, sides1), send(shard3, Z_NEAR))
        z3, sides2 = far_z(shard3, near3), to_sides(p2, X_ROUTE, Y_ROUTE)
        table_vec, kv_full, squery_full, update_full = assemble(
            pieces(p1, sides1, corner1, last_corner(corner1)), layouts[0], True
        )
    else:
        vectors = jnp.concatenate([attn_gain, mlp_gain, gate_bias, down_bias, up_bias])
        vectors = vectors.reshape(4 + folds, rows)
        columns = jnp.pad(jnp.transpose(vectors), ((0, 0), (0, VEC - vectors.shape[0])))
        table_vec, kv_full, squery_full, update_full = gather_any(
            jnp.concatenate(
                [char_table, columns, key_weight, value_weight, state_query, update_weight], 1
            ),
            layouts[0],
        )

    vector_rows = jnp.transpose(f32(table_vec[:, VOCAB : VOCAB + 4 + folds]))
    biases = halves_of_columns(
        vector_rows[4:].reshape(folds, -1, rows).transpose(1, 0, 2).reshape(1, ff)
    )
    keep_gate = jax.nn.sigmoid(vector_rows[2])
    is_first = lax.axis_index("seq") == 0
    bias_rows = f32(position_table)[:, None, :]

    one_hot = (char_ids[:, None] == jnp.arange(VOCAB)[None, :]).astype(jnp.bfloat16)
    embedded = dot(one_hot, table_vec[:, :VOCAB], NT)
    normed_low = low(embedded * norm_scale(embedded) * vector_rows[0])
    kv = low(dot(normed_low, kv_full, NN))
    state_mix, state_lse = state_attention(kv, squery_full)
    update = dot(state_mix, update_full, NN)
    mine = low((1.0 - keep_gate) * update)
    if fast:
        sides2, z3[:3], mine = join(sides2, z3[:3], mine)
        sibling = send(mine, CORE_ROUTE)
        near = earlier_near(keep_gate, mine, sibling)
        prev = from_behind(tie(kv, mine), "seq", 1)
        corner2 = to_corner(p2, sides2, Y_ROUTE)
        near, corner2, prev, near4, p3 = join(
            near, corner2, prev, send(tie(shard4, mine), Z_NEAR), stack_z(shard3, *z3)
        )
        sides3, z4 = to_sides(p3), far_z(shard4, near4)
        query_full, sinit_full, skv_full, out_full = assemble(
            pieces(p2, sides2, corner2, last_corner(corner2)), layouts[1], False
        )
    else:
        prev = from_behind(kv, "seq", 1)
        query_full, sinit_full, skv_full, out_full = gather_any(
            jnp.concatenate(
                [query_weight, state_init, state_key_weight, state_value_weight, out_weight], 1
            ),
            layouts[1],
        )
    query = low(dot(normed_low, query_full, NN))
    start = f32(join(jnp.transpose(sinit_full))[0])
    if fast:
        state_prev = earlier_sum(keep_gate, near, sibling, start)
    else:
        gain, total = entering(keep_gate, mine, False)
        state_prev = gain * start + total
    state_low = low(state_prev)
    skv = low(dot(state_low, skv_full, NN))
    if fast:
        skv, query, sides3, z4[:3] = join(skv, query, sides3, z4[:3])
        corner3, p4 = to_corner(p3, sides3), stack_z(shard4, *z4)
    mixed, lse = attention(query, kv, prev, skv, bias_rows)
    hidden = embedded + dot(mixed, out_full, NN)

    if fast:
        corner3, hidden, p4 = join(corner3, hidden, p4)
        sides4 = to_sides(p4)
        parts = pieces(p3, sides3, corner3, last_corner(corner3))
        keep_a, away_a, bias_a, *before = mlp_half(
            spot_of, True, hidden, out_grad, vector_rows, biases[0], parts, None
        )
        sides4, away_a, before = join(sides4, away_a, before)
        corner4, got_a = join(to_corner(p4, sides4), to_core(away_a))
        parts = pieces(p4, sides4, corner4, last_corner(corner4))
        first_a = over_first(keep_a, got_a)
        keep_b, away_b, bias_b, *before = mlp_half(
            spot_of, True, hidden, out_grad, vector_rows, biases[1], parts, before
        )
        first_a, away_b, before = join(first_a, away_b, before)
    else:
        shard = jnp.concatenate([up_weight, fold(down_weight, rows)], 1)
        up_full, down_full = gather_any(shard, ((0, ff, 1), (ff, D, folds)))
        halves = []
        for up, down in zip(halves_of_columns(up_full), halves_of_rows(down_full, CHUNKS)):
            down = down.reshape(CHUNKS, 2, -1, D).transpose(0, 2, 1, 3).reshape(D, HALF)
            both = jnp.concatenate([up, down], 1).reshape(4, 2, 2, 2, -1, 2 * HALF)
            halves.append([both[:, i // 2 % 2, i % 2, i // 4] for i in range(8)])
        keep_a, away_a, bias_a, *before = mlp_half(
            spot_of, False, hidden, out_grad, vector_rows, biases[0], halves[0], None
        )
        keep_b, away_b, bias_b, *before = mlp_half(
            spot_of, False, hidden, out_grad, vector_rows, biases[1], halves[1], before
        )
    output, grad_hidden, grad_branch, mlp_sums = before

    keep_b, away_b = out_weight_grad(core_of, mixed, grad_branch, keep_b, away_b)
    grad_mixed = low(dot(grad_branch, out_full, NT))
    if fast:
        got_b, grad_mixed = join(to_core(away_b), grad_mixed)
        second_a = over_second(keep_a, got_a, first_a)
        corner_b = over_first_in_two(keep_b, got_b, True)
    gq, gkv, gprev, gstate, gbias = attention_back(
        query, kv, prev, skv, bias_rows, lse, grad_mixed
    )
    gbias = gbias.reshape(HEADS, BLK)
    if fast:
        second_a, corner_b, gprev, gstate = join(second_a, corner_b, gprev, gstate)
        side_b = over_first_in_two(keep_b, got_b, False)
    read, sent = readout(gstate, skv_full)
    if fast:
        sibling, gbias = send(sent, CORE_ROUTE), exchange(gbias, CORE_ROUTE)
        near = later_near(keep_gate, sent, sibling)
    first = weight_grads(
        core_of, [("dot", state_low, gstate[0], gstate[1]), ("dot", normed_low, gq)]
    )
    if fast:
        near, side_b, first, gbias = join(near, side_b, first, gbias)
        first_b = (corner_b, side_b)
        gnext = from_behind(tie(gprev, near), "seq", -1)
        pair_a = over_pairs(keep_a, got_a, first_a, second_a)
        got_c = to_core(first[1])
        gbias = exchange(gbias, X_ROUTE)
        after = later_sum(keep_gate, near, sibling)
    else:
        gnext = from_behind(gprev, "seq", -1)
        after = entering(keep_gate, sent, True)[1]
    grad_update = low((1.0 - keep_gate) * after)
    grad_smix = low(dot(grad_update, update_full, NT))
    if fast:
        grad_smix, second_b = join(grad_smix, over_second(keep_b, got_b, first_b))
    gsum, gquery = state_attention_back(kv, squery_full, state_lse, grad_smix, gkv)
    if fast:
        gsum, after = join(gsum, after)
    state_init_grad = jnp.where(is_first, read + keep_gate * after, 0.0)
    second = weight_grads(
        core_of,
        [
            ("dot", state_mix, grad_update),
            ("rows", gquery),
            ("transposed", state_init_grad),
        ],
    )
    if fast:
        gnext, pair_a, got_c, second, gbias = join(gnext, pair_a, got_c, second, gbias)
        first_c = over_first(first[0], got_c)
        pair_b = over_pairs(keep_b, got_b, first_b, second_b)
        got_d = to_core(second[1])
        gbias = exchange(gbias, Y_ROUTE)
    gk, gv = (low(gsum[i] + f32(gnext[i])) for i in range(2))
    key_grads = weight_grads(core_of, [("dot", normed_low, gk, gv)])
    if fast:
        gk, got_e = tie((gk, key_grads[1]), key_grads[0])
        got_e = to_core(got_e)
    embedded_grad, embedded_low, gain_grad = embedding_back(
        gq, gk, gv, query_full, kv_full, embedded, grad_hidden, vector_rows
    )
    if fast:
        first_c, got_d, got_e, embedded_low, gbias = join(
            first_c, got_d, got_e, embedded_low, gbias
        )
        second_c = over_second(first[0], got_c, first_c)
        first_d, first_e = over_first(second[0], got_d), over_first(key_grads[0], got_e)
        position_table_grad = exchange(exchange(gbias, Z_NEAR), Z_FAR)
        after, mlp_sums, bias_a, bias_b = join(after, mlp_sums, bias_a, bias_b, gain_grad)[:4]
    else:
        position_table_grad = lax.psum(gbias, AX)
    gate_bias_grad = jnp.sum(after * (state_prev - update), 0) * keep_gate * (1.0 - keep_gate)
    up_bias_grad = jnp.concatenate([b.reshape(CHUNKS, -1) for b in (bias_a, bias_b)], 1)
    vector_grads = jnp.concatenate(
        [gain_grad[:1], mlp_sums[:1], gate_bias_grad[None], mlp_sums[1:2]]
        + [up_bias_grad.reshape(-1, folds, rows).transpose(1, 0, 2).reshape(folds, D)]
        + [jnp.zeros((VEC - 4 - folds, D), jnp.float32)],
        0,
    )
    last = weight_grads(
        core_of, [("dot", embedded_low, one_hot), ("transposed", vector_grads)]
    )
    if fast:
        second_c, first_d, first_e, pair_b, got_f, position_table_grad = join(
            second_c, first_d, first_e, pair_b, to_core(last[1]), position_table_grad
        )
        second_d = over_second(second[0], got_d, first_d)
        second_e = over_second(key_grads[0], got_e, first_e)
        first_f = over_first(last[0], got_f)
        pair_c = over_pairs(first[0], got_c, first_c, second_c)
        end_b = within_pair(*pair_b)
        second_d, second_e, first_f, pair_c, end_b = join(
            second_d, second_e, first_f, pair_c, end_b
        )
        end_e = over_z(key_grads[0], got_e, first_e, second_e)
        second_f = over_second(last[0], got_f, first_f)
        pair_d = over_pairs(second[0], got_d, first_d, second_d)
        end_e, second_f, pair_d = join(end_e, second_f, pair_d)
        end_f = over_z(last[0], got_f, first_f, second_f)
        end_c, end_d = within_pair(*pair_c), within_pair(*pair_d)
        end_a = within_pair(*pair_a)
        sums = [finish(s) for s in (end_a, end_b, end_c, end_d, end_e, end_f)]
        up_sum = jnp.concatenate([s[:, :HALF].reshape(rows, CHUNKS, -1) for s in sums[:2]], 2)
        up_sum = up_sum.reshape(rows, ff)
        down_sum = jnp.concatenate([unfold(s[:, HALF : 2 * HALF]) for s in sums[:2]], 0)
        out_sum = sums[1][:, 2 * HALF :]
        first, second, key_sum, last = sums[2:]
    else:
        pairs = [natural(keep_a, away_a), natural(keep_b, away_b)]
        out_sum = scatter_any(pairs[1][:, 2 * HALF :])
        up_sum = jnp.concatenate([s[:, :HALF].reshape(D, CHUNKS, -1) for s in pairs], 2)
        up_sum = scatter_any(up_sum.reshape(D, ff))
        down_sum = jnp.concatenate(
            [
                s[:, HALF : 2 * HALF].reshape(CHUNKS, D // CHUNKS, -1, D).transpose(0, 2, 1, 3)
                for s in pairs
            ],
            1,
        )
        down_sum = scatter_any(down_sum.reshape(ff, D))
        first, second, key_sum, last = (
            scatter_any(natural(*s)) for s in (first, second, key_grads, last)
        )
    vector_sum = last[:, VOCAB:]
    return (
        output,
        embedded_grad,
        last[:, :VOCAB],
        vector_sum[:, 0],
        first[:, 2 * D :],
        key_sum[:, :D],
        key_sum[:, D:],
        out_sum,
        first[:, :D],
        first[:, D : 2 * D],
        second[:, :D],
        second[:, D : D + NSTATE],
        second[:, D + NSTATE :],
        vector_sum[:, 2],
        position_table_grad,
        vector_sum[:, 1],
        up_sum,
        jnp.transpose(vector_sum[:, 4 : 4 + folds]).reshape(-1),
        down_sum,
        vector_sum[:, 3],
    )


def solution(mesh):
    fast = dict(mesh.shape) == {"dp": 8, "seq": 4}
    return jax.shard_map(
        functools.partial(layer, fast),
        mesh=mesh,
        in_specs=(
            P(("dp", "seq")),
            P(("dp", "seq"), None),
            P(("dp", "seq")),
            P(("dp", "seq"), None),
            P(("dp", "seq"), None),
            P(("dp", "seq"), None),
            P(("dp", "seq"), None),
            P(("dp", "seq"), None),
            P(("dp", "seq"), None),
            P(("dp", "seq"), None),
            P(("dp", "seq"), None),
            P(("dp", "seq"), None),
            P(("dp", "seq")),
            P(),
            P(("dp", "seq")),
            P(("dp", "seq"), None),
            P(("dp", "seq")),
            P(("dp", "seq"), None),
            P(("dp", "seq")),
            P(("dp", "seq"), None),
        ),
        out_specs=(
            P(("dp", "seq"), None),
            P(("dp", "seq"), None),
            P(("dp", "seq"), None),
            P(("dp", "seq")),
            P(("dp", "seq"), None),
            P(("dp", "seq"), None),
            P(("dp", "seq"), None),
            P(("dp", "seq"), None),
            P(("dp", "seq"), None),
            P(("dp", "seq"), None),
            P(("dp", "seq"), None),
            P(("dp", "seq"), None),
            P(("dp", "seq"), None),
            P(("dp", "seq")),
            P(),
            P(("dp", "seq")),
            P(("dp", "seq"), None),
            P(("dp", "seq")),
            P(("dp", "seq"), None),
            P(("dp", "seq")),
        ),
        check_vma=False,
    )
```

```python
import functools

import jax
import jax.numpy as jnp
from jax import lax
from jax.experimental import pallas as pl
from jax.experimental.pallas import tpu as pltpu
from jax.sharding import PartitionSpec as P

D = 1024
HEADS = 8
HD = 128
NSTATE = 512
VOCAB = 256
BLK = 512
AX = ("dp", "seq")
VEC = 128


def f32(v):
    return v.astype(jnp.float32)


def low(v):
    return v.astype(jnp.bfloat16)


def route(move):
    pairs = []
    for z in range(4):
        for y in range(2):
            for x in range(2):
                for c in range(2):
                    tz, ty, tx, tc = move(z, y, x, c)
                    pairs.append((z * 8 + y * 4 + x * 2 + c, tz * 8 + ty * 4 + tx * 2 + tc))
    return pairs


A_ROUTE = route(lambda z, y, x, c: (z, y, 1 - x, c) if c == 0 else (z, 1 - y, x, c))
B_ROUTE = route(lambda z, y, x, c: (z, 1 - y, x, c) if c == 0 else (z, y, 1 - x, c))
CORE_ROUTE = route(lambda z, y, x, c: (z, y, x, 1 - c))
X_ROUTE = route(lambda z, y, x, c: (z, y, 1 - x, c))
Y_ROUTE = route(lambda z, y, x, c: (z, 1 - y, x, c))
Z_NEAR = route(lambda z, y, x, c: (z ^ 1, y, x, c))
Z_FAR = route(lambda z, y, x, c: (z ^ 2, y, x, c))
Z_ROUTE = {k: route(lambda z, y, x, c, k=k: ((z + k) % 4, y, x, c)) for k in (1, 2, 3)}


def place():
    d, s = lax.axis_index("dp"), lax.axis_index("seq")
    return d // 2, d % 2, s // 2, s % 2


def send(v, pairs):
    return lax.ppermute(v, AX, pairs)


def stack_z(shard, *others):
    others, cyclic = others[:3], others[3]

    def body(*refs):
        z = lax.axis_index("dp") // 2
        near = z + 1 - 2 * lax.rem(z, 2)
        spots = (
            [lax.rem(z + 4 - i, 4) for i in range(4)]
            if cyclic
            else [z, near, lax.rem(z + 2, 4), lax.rem(near + 2, 4)]
        )
        for at, src in zip(spots, refs[:4]):
            refs[4][at] = src[...]

    return pl.pallas_call(
        body, out_shape=jax.ShapeDtypeStruct((4,) + shard.shape, shard.dtype), name="stack_z"
    )(shard, *others)


def here():
    return lax.rem(lax.axis_index("dp"), 2), lax.axis_index("seq") // 2, core_index()


def core_index():
    return lax.rem(lax.axis_index("seq"), 2)


def origin(i, spot, alternate):
    y, x, c = spot
    core = c if i < 4 else 1 - c
    if alternate:
        flip_x = (0, 1 - core, core, 1)[i % 4]
        flip_y = (0, core, 1 - core, 1)[i % 4]
    else:
        flip_x, flip_y = i % 2, i % 4 // 2
    return lax.rem(y + flip_y, 2), lax.rem(x + flip_x, 2), core


def assemble(pieces, layout, alternate):
    rows, width = pieces[0].shape[1:]

    def body(*refs):
        ins, outs = refs[:8], refs[8:]
        spot = here()
        for i, src in enumerate(ins):
            ty, tx, core = origin(i, spot, alternate)
            for (first, w, folds), out in zip(layout, outs):
                for q in range(folds):
                    out[0, ty, tx, core, q * rows : (q + 1) * rows, :] = src[
                        0, :, first + q * w : first + (q + 1) * w
                    ]

    full = pl.pallas_call(
        body,
        out_shape=[
            jax.ShapeDtypeStruct((4, 2, 2, 2, rows * n, w), pieces[0].dtype) for _, w, n in layout
        ],
        grid=(4,),
        in_specs=[pl.BlockSpec((1, rows, width), lambda z: (z, 0, 0))] * 8,
        out_specs=[
            pl.BlockSpec((1, 2, 2, 2, rows * n, w), lambda z: (z, 0, 0, 0, 0, 0))
            for _, w, n in layout
        ],
        compiler_params=pltpu.CompilerParams(vmem_limit_bytes=40 * 2**20),
        name="assemble",
    )(*pieces)
    return [o.reshape(32 * rows * n, w) for o, (_, w, n) in zip(full, layout)]


def tie(value, *others):
    return lax.optimization_barrier((value, others))[0]


def join(*values):
    return lax.optimization_barrier(values)


def along_z(shard):
    return [send(shard, Z_ROUTE[k]) for k in (1, 2, 3)] + [True]


def far_z(shard, near):
    return [near, send(shard, Z_FAR), send(near, Z_FAR), False]


def to_sides(p, a=A_ROUTE, b=B_ROUTE):
    return send(p, a), send(p, b)


def to_corner(p, sides, b=B_ROUTE):
    return send(sides[0], b), [send(v, CORE_ROUTE) for v in (p,) + tuple(sides)]


def last_corner(corner):
    return send(corner[0], CORE_ROUTE)


def pieces(p, sides, corner, last):
    return (p,) + tuple(sides) + (corner[0],) + tuple(corner[1]) + (last,)


def to_core(away):
    return send(away, CORE_ROUTE)


def first_axis():
    z, y, x, c = place()
    return jnp.where(c == 0, y, x), jnp.where(c == 0, x, y)


def chip_part(keep, got, b, a=None):
    rows, width = keep.shape[0] // 16, keep.shape[1]
    start, size = ((b, 0), (1, 2)) if a is None else ((b, a), (1, 1))
    at = [
        lax.dynamic_slice(
            v.reshape(2, 2, 4, rows, width), start + (0, 0, 0), size + (4, rows, width)
        )
        for v in (keep, got)
    ]
    return (f32(at[0]) + f32(at[1])).reshape(size[1], 4, rows, width)


def over_first(keep, got):
    return send(low(chip_part(keep, got, 1 - first_axis()[0])), B_ROUTE)


def of_first(first, i):
    return lax.dynamic_index_in_dim(first, i, 0)


def over_second(keep, got, first):
    b, a = first_axis()
    far = of_first(first, 1 - a)
    return send(low(chip_part(keep, got, b, 1 - a) + f32(far)), A_ROUTE)


def own_part(keep, got, first, second):
    b, a = first_axis()
    mine = of_first(first, a)
    return (chip_part(keep, got, b, a) + f32(mine) + f32(second))[0]


def over_pairs(keep, got, first, second):
    z = place()[0]
    own = own_part(keep, got, first, second)
    pairs = own.reshape((2, 2) + own.shape[1:])
    away = lax.dynamic_index_in_dim(pairs, 1 - z // 2, 0, False)
    return lax.dynamic_index_in_dim(pairs, z // 2, 0, False), send(low(away), Z_FAR)


def within_pair(mine, got):
    z = place()[0]

    def pick(i):
        return lax.dynamic_index_in_dim(mine, i, 0, False) + f32(
            lax.dynamic_index_in_dim(got, i, 0, False)
        )

    return pick(z % 2), send(low(pick(1 - z % 2)), Z_NEAR)


def over_z(keep, got, first, second):
    z = place()[0]
    own = own_part(keep, got, first, second)
    rest = [low(lax.dynamic_index_in_dim(own, (z + k) % 4, 0, False)) for k in (1, 2, 3)]
    mine = lax.dynamic_index_in_dim(own, z, 0, False)
    return [mine] + [send(v, Z_ROUTE[k]) for v, k in zip(rest, (1, 2, 3))]


def finish(parts):
    return sum(f32(p) for p in parts)


def gather_any(shard, layout):
    rows = shard.shape[0]
    full = lax.all_gather(shard, AX, axis=0, tiled=True)
    outs = []
    for first, w, folds in layout:
        part = full[:, first : first + w * folds]
        if folds > 1:
            part = part.reshape(-1, rows, folds, w).transpose(0, 2, 1, 3).reshape(-1, w)
        outs.append(part)
    return outs


def scatter_any(grad):
    return lax.psum_scatter(f32(grad), AX, scatter_dimension=0, tiled=True)


def exchange(value, pairs):
    return value + send(value, pairs)


def half_across(chip):
    c = place()[3]
    half = NSTATE // 2
    return send(lax.dynamic_slice(chip, (c * half, 0), (half, D)), X_ROUTE)


def both_halves(near):
    c = place()[3]
    far = send(near, CORE_ROUTE)
    return jnp.concatenate([jnp.where(c == 0, near, far), jnp.where(c == 0, far, near)], 0)


def in_order(mine, sibling):
    c = place()[3]
    return jnp.where(c == 0, f32(mine), f32(sibling)), jnp.where(c == 0, f32(sibling), f32(mine))


def earlier_near(keep_gate, mine, sibling):
    first, second = in_order(mine, sibling)
    return half_across(low(keep_gate * first + second))


def earlier_sum(keep_gate, near, sibling, start):
    z, y, x, c = place()
    other = both_halves(near)
    before = jnp.where(x == 0, start, keep_gate * keep_gate * start + f32(other))
    return jnp.where(c == 0, before, keep_gate * before + f32(sibling))


def later_near(keep_gate, mine, sibling):
    first, second = in_order(mine, sibling)
    return half_across(low(first + keep_gate * second))


def later_sum(keep_gate, near, sibling):
    z, y, x, c = place()
    after = jnp.where(x == 0, f32(both_halves(near)), 0.0)
    return jnp.where(c == 0, f32(sibling) + keep_gate * after, after)


def from_behind(block, axis, distance):
    devices = range(lax.axis_size(axis))
    pairs = [(i - distance, i) for i in devices if i - distance in devices]
    return lax.ppermute(block, axis, pairs)


def entering(keep_gate, mine, reverse):
    devices, at_home = lax.axis_size("seq"), lax.axis_index("seq")
    everything = lax.all_gather(mine, "seq")

    def turn(k, before):
        at = devices - 1 - k if reverse else k
        reached = at > at_home if reverse else at < at_home
        gain, total = before
        return (
            jnp.where(reached, gain * keep_gate, gain),
            jnp.where(reached, keep_gate * total + f32(everything[at]), total),
        )

    start = (jnp.ones_like(keep_gate), jnp.zeros(mine.shape, jnp.float32))
    return lax.fori_loop(0, devices, turn, start)


def norm_scale(values):
    return lax.rsqrt(jnp.mean(values * values, -1, keepdims=True) + 1e-06)


def halves_of_columns(a):
    parts = a.reshape(a.shape[0], CHUNKS, 2, -1)
    return [parts[:, :, i].reshape(a.shape[0], -1) for i in range(2)]


def halves_of_rows(a, chunks):
    parts = a.reshape(chunks, 2, -1, a.shape[1])
    return [parts[:, i].reshape(-1, a.shape[1]) for i in range(2)]


def fold(a, rows):
    return a.reshape(-1, rows, D).transpose(1, 0, 2).reshape(rows, -1)


def unfold(a):
    rows = a.shape[0]
    return a.reshape(rows, -1, D).transpose(1, 0, 2).reshape(-1, D)


SCALE = HD ** (-0.5)


def dot(a, b, dims):
    return lax.dot_general(a, b, (dims, ((), ())), preferred_element_type=jnp.float32)


NN, NT, TN = ((1,), (0,)), ((1,), (1,)), ((0,), (0,))


def head_block(first):
    return pl.BlockSpec((BLK, HD), lambda h: (0, first + h))


def pair_block():
    return pl.BlockSpec((2, BLK, HD), lambda h: (0, 0, h))


def row_block():
    return pl.BlockSpec((1, 1, BLK), lambda h: (h, 0, 0))


def token_scores(q, k, kp, bias_row, is_first):
    row = lax.broadcasted_iota(jnp.int32, (BLK, BLK), 0)
    col = lax.broadcasted_iota(jnp.int32, (BLK, BLK), 1)
    own = row <= col
    bias = jnp.concatenate([bias_row] + [pltpu.roll(bias_row, i, 1) for i in range(1, 8)], 0)
    while bias.shape[0] < BLK:
        bias = jnp.concatenate([bias, pltpu.roll(bias, bias.shape[0], 1)], 0)
    raw = jnp.where(own, dot(k, q, NT), dot(kp, q, NT))
    scores = raw * SCALE + bias
    return jnp.where(own | jnp.logical_not(is_first), scores, -1e30), own


def attention_body(q, k, v, kp, vp, sk, sv, bias, mixed, lse):
    is_first = lax.axis_index("seq") == 0
    q = q[...]
    tokens, own = token_scores(q, k[...], kp[...], bias[0], is_first)
    states = dot(sk[...], q, NT) * SCALE
    top = jnp.maximum(jnp.max(tokens, 0, keepdims=True), jnp.max(states, 0, keepdims=True))
    tokens, states = jnp.exp(tokens - top), jnp.exp(states - top)
    total = jnp.sum(tokens, 0, keepdims=True) + jnp.sum(states, 0, keepdims=True)
    lse[0] = top + jnp.log(total)
    mix = dot(jnp.transpose(v[...]), low(jnp.where(own, tokens, 0.0)), NN)
    mix += dot(jnp.transpose(vp[...]), low(jnp.where(own, 0.0, tokens)), NN)
    mix += dot(jnp.transpose(sv[...]), low(states), NN)
    mixed[...] = low(jnp.transpose(mix * (1.0 / total)))


def attention(query, kv, prev, skv, bias):
    return pl.pallas_call(
        attention_body,
        grid=(HEADS,),
        in_specs=[head_block(0)]
        + [head_block(0), head_block(HEADS)] * 3
        + [row_block()],
        out_specs=[head_block(0), row_block()],
        out_shape=[
            jax.ShapeDtypeStruct((BLK, D), jnp.bfloat16),
            jax.ShapeDtypeStruct((HEADS, 1, BLK), jnp.float32),
        ],
        compiler_params=pltpu.CompilerParams(vmem_limit_bytes=40 * 2**20),
        cost_estimate=pl.CostEstimate(
            flops=12 * HEADS * BLK * BLK * HD,
            bytes_accessed=9 * 2**20,
            transcendentals=2 * HEADS * BLK * BLK,
        ),
        name="attention",
    )(query, kv, kv, prev, prev, skv, skv, bias)


def attention_back_body(
    q, k, v, kp, vp, sk, sv, bias, lse, go, gq, gkv, gprev, gstate, gbias
):
    is_first = lax.axis_index("seq") == 0
    q, k, kp, sk, go = q[...], k[...], kp[...], sk[...], go[...]
    tokens, own = token_scores(q, k, kp, bias[0], is_first)
    log_total = lse[0]
    tokens = jnp.exp(tokens - log_total)
    states = jnp.exp(dot(sk, q, NT) * SCALE - log_total)
    gtokens = jnp.where(own, dot(v[...], go, NT), dot(vp[...], go, NT))
    gstates = dot(sv[...], go, NT)
    mean = jnp.sum(tokens * gtokens, 0, keepdims=True) + jnp.sum(states * gstates, 0, keepdims=True)
    gkv[1] = dot(low(jnp.where(own, tokens, 0.0)), go, NN)
    gprev[1] = low(dot(low(jnp.where(own, 0.0, tokens)), go, NN))
    gstate[1] = low(dot(low(states), go, NN))
    gtokens = low(tokens * (gtokens - mean))
    gstates = low(states * (gstates - mean))
    wide = f32(gtokens)
    gown, gbefore = low(jnp.where(own, wide, 0.0)), low(jnp.where(own, 0.0, wide))
    gkv[0] = dot(gown, q, NN) * SCALE
    gprev[0] = low(dot(gbefore, q, NN) * SCALE)
    gstate[0] = low(dot(gstates, q, NN) * SCALE)
    g = dot(jnp.transpose(k), gown, NN)
    g += dot(jnp.transpose(kp), gbefore, NN)
    g += dot(jnp.transpose(sk), gstates, NN)
    gq[...] = low(jnp.transpose(g * SCALE))
    rows = BLK
    while rows > 1:
        rows //= 2
        wide = wide[:rows] + pltpu.roll(wide[rows:], BLK - rows, 1)
    gbias[0] = wide


def attention_back(query, kv, prev, skv, bias, lse, go):
    return pl.pallas_call(
        attention_back_body,
        grid=(HEADS,),
        in_specs=[head_block(0)]
        + [head_block(0), head_block(HEADS)] * 3
        + [row_block(), row_block(), head_block(0)],
        out_specs=[head_block(0), pair_block(), pair_block(), pair_block(), row_block()],
        out_shape=[
            jax.ShapeDtypeStruct((BLK, D), jnp.bfloat16),
            jax.ShapeDtypeStruct((2, BLK, D), jnp.float32),
            jax.ShapeDtypeStruct((2, BLK, D), jnp.bfloat16),
            jax.ShapeDtypeStruct((2, BLK, D), jnp.bfloat16),
            jax.ShapeDtypeStruct((HEADS, 1, BLK), jnp.float32),
        ],
        compiler_params=pltpu.CompilerParams(vmem_limit_bytes=48 * 2**20),
        cost_estimate=pl.CostEstimate(
            flops=30 * HEADS * BLK * BLK * HD,
            bytes_accessed=18 * 2**20,
            transcendentals=2 * HEADS * BLK * BLK,
        ),
        name="attention_back",
    )(query, kv, kv, prev, prev, skv, skv, bias, lse, go)


def query_block():
    return pl.BlockSpec((HD, NSTATE), lambda h: (h, 0))


def state_body(k, v, query, mixed, lse):
    scores = dot(k[...], query[...], NN) * SCALE
    top = jnp.max(scores, 0, keepdims=True)
    scores = jnp.exp(scores - top)
    total = jnp.sum(scores, 0, keepdims=True)
    lse[0] = top + jnp.log(total)
    mix = dot(jnp.transpose(v[...]), low(scores), NN)
    mixed[...] = low(jnp.transpose(mix * (1.0 / total)))


def state_attention(kv, query):
    return pl.pallas_call(
        state_body,
        grid=(HEADS,),
        in_specs=[head_block(0), head_block(HEADS), query_block()],
        out_specs=[head_block(0), row_block()],
        out_shape=[
            jax.ShapeDtypeStruct((NSTATE, D), jnp.bfloat16),
            jax.ShapeDtypeStruct((HEADS, 1, NSTATE), jnp.float32),
        ],
        compiler_params=pltpu.CompilerParams(vmem_limit_bytes=32 * 2**20),
        cost_estimate=pl.CostEstimate(
            flops=4 * HEADS * BLK * BLK * HD,
            bytes_accessed=4 * 2**20,
            transcendentals=HEADS * BLK * BLK,
        ),
        name="state_attention",
    )(kv, kv, query)


def state_back_body(k, v, query, lse, go, gkv, gsum, gquery):
    k, query, go = k[...], query[...], go[...]
    probs = jnp.exp(dot(k, query, NN) * SCALE - lse[0])
    gprobs = dot(v[...], go, NT)
    mean = jnp.sum(probs * gprobs, 0, keepdims=True)
    gsum[1] = dot(low(probs), go, NN) + gkv[1]
    gscores = low(probs * (gprobs - mean))
    gsum[0] = dot(gscores, query, NT) * SCALE + gkv[0]
    gquery[...] = low(dot(jnp.transpose(k), gscores, NN) * SCALE)


def state_attention_back(kv, query, lse, go, gkv):
    return pl.pallas_call(
        state_back_body,
        grid=(HEADS,),
        in_specs=[
            head_block(0),
            head_block(HEADS),
            query_block(),
            row_block(),
            head_block(0),
            pair_block(),
        ],
        out_specs=[pair_block(), query_block()],
        out_shape=[
            jax.ShapeDtypeStruct((2, BLK, D), jnp.float32),
            jax.ShapeDtypeStruct((D, NSTATE), jnp.bfloat16),
        ],
        compiler_params=pltpu.CompilerParams(vmem_limit_bytes=32 * 2**20),
        cost_estimate=pl.CostEstimate(
            flops=10 * HEADS * BLK * BLK * HD,
            bytes_accessed=14 * 2**20,
            transcendentals=HEADS * BLK * BLK,
        ),
        name="state_attention_back",
    )(kv, kv, query, lse, go, gkv)


STEP = 512
HALF = 2048
CHUNKS = 32


def owner_row(chip, swap):
    z, y, x = chip // 4, chip // 2 % 2, chip % 2
    return (x * 8 + y * 4 if swap else y * 8 + x * 4) + z


def gelu_parts(x):
    a, b = 0.7978845608028654, 0.044715
    square = x * x
    t = jnp.tanh(a * x * (1.0 + b * square))
    half = 0.5 * (1.0 + t)
    slope = half + (0.5 * a) * x * (1.0 - t * t) * (1.0 + 3.0 * b * square)
    return x * half, slope


def mlp_body(last, spot_of, alternate, *refs):
    hidden, og, rows, up_bias = refs[:4]
    ups, downs, refs = refs[4:12], refs[12:20], refs[20:]
    if last:
        out_in, u_in, keep, away, up_bias_grad, output, grad, branch, sums = refs[:9]
        up, down, xn, xs, out_acc, u_acc = refs[9:]
    else:
        keep, away, up_bias_grad, out_acc, u_acc = refs[:5]
        up, down, xn, xs = refs[5:]
    j = pl.program_id(0)
    spot = spot_of()
    core = spot[2]
    rk = D // CHUNKS
    hk = HALF // CHUNKS

    @pl.when(j == 0)
    def _():
        h = hidden[...]
        r = lax.rsqrt(jnp.mean(h * h, -1, keepdims=True) + 1e-06)
        n = low(h * r * rows[1:2, :])
        xn[...] = n
        nt = jnp.transpose(n)
        for i in range(CHUNKS):
            to = owner_row(i // 2, i % 2) * rk + lax.rem(i % 2 + core, 2) * (D // 2)
            xs[pl.ds(pl.multiple_of(to, rk), rk), :] = nt[i * rk : (i + 1) * rk]
        if last:
            out_acc[...] = out_in[...]
            u_acc[...] = u_in[...]
        else:
            out_acc[...] = jnp.zeros_like(out_acc)
            u_acc[...] = jnp.zeros_like(u_acc)

    for i in range(8):
        ty, tx, c = origin(i, spot, alternate)
        at = ty * 4 + tx * 2 + c
        for z in range(4):
            up[pl.ds(pl.multiple_of((z * 8 + at) * rk, rk), rk), :] = ups[i][z]
        for q in range(hk // rk):
            down[pl.ds(pl.multiple_of(at * hk + q * rk, rk), rk), :] = downs[i][
                0, :, q * D : (q + 1) * D
            ]
    up_w, down_w, g_out = up[...], down[...], og[...]
    act, slope = gelu_parts(dot(xn[...], up_w, NN) + up_bias[...])
    act = low(act)
    out_acc[...] += dot(act, down_w, NN)
    g_up = low(slope * dot(g_out, down_w, NT))
    column = jnp.transpose(
        jnp.broadcast_to(jnp.sum(f32(g_up), 0, keepdims=True), (8, STEP))
    )[:, :1]
    lane = lax.broadcasted_iota(jnp.int32, (rk, VEC), 1) - (4 + 2 * last)
    for i in range(STEP // hk):
        pair = [column[i * hk + q * rk : i * hk + (q + 1) * rk] for q in range(2)]
        up_bias_grad[i * rk : (i + 1) * rk, :] = jnp.where(
            lane == 0, pair[0], jnp.where(lane == 1, pair[1], 0.0)
        )
    u_acc[...] += dot(g_up, up_w, NT)
    d_up = low(dot(xs[...], g_up, NN))
    at = pl.ds(pl.multiple_of(j * STEP, STEP), STEP)
    keep[:, at] = d_up[: D // 2]
    away[:, at] = d_up[D // 2 :]
    d_down = low(dot(jnp.transpose(act), g_out, NN))
    for i in range(STEP // hk // 2):
        even = d_down[2 * i * hk : (2 * i + 1) * hk]
        odd = d_down[(2 * i + 1) * hk : (2 * i + 2) * hk]
        mine, other = jnp.where(core == 0, even, odd), jnp.where(core == 0, odd, even)
        for q in range(hk // rk):
            cols = slice(HALF + q * D, HALF + (q + 1) * D)
            part = slice(q * rk, (q + 1) * rk)
            for out, value, owner in ((keep, mine, core), (away, other, 1 - core)):
                to = jnp.where(owner == 0, owner_row(i, 0), owner_row(i, 1)) + j
                out[pl.ds(pl.multiple_of(to * rk, rk), rk), cols] = value[part]

    if last:

        @pl.when(j == pl.num_programs(0) - 1)
        def _():
            h = hidden[...]
            output[...] = low(h + out_acc[...] + rows[3:4, :])
            r = lax.rsqrt(jnp.mean(h * h, -1, keepdims=True) + 1e-06)
            n = h * r
            u = u_acc[...]
            ug = u * rows[1:2, :]
            g = f32(og[...]) + r * (ug - n * jnp.mean(ug * n, -1, keepdims=True))
            grad[...] = g
            branch[...] = low(g)
            sums[0:1, :] = jnp.sum(u * n, 0, keepdims=True)
            sums[1:2, :] = jnp.sum(f32(og[...]), 0, keepdims=True)


def mlp_half(spot_of, alternate, hidden, og, rows, up_bias, parts, before):
    last = before is not None
    whole = lambda a, b: pl.BlockSpec((a, b), lambda j: (0, 0))
    tall = lambda a, b: pl.BlockSpec((a, b), lambda j: (0, 0), pipeline_mode=pl.Buffered(1))
    acc = jax.ShapeDtypeStruct((BLK, D), jnp.float32)
    lows = jax.ShapeDtypeStruct((BLK, D), jnp.bfloat16)
    grads = jax.ShapeDtypeStruct((D // 2, 2 * HALF), jnp.bfloat16)
    return pl.pallas_call(
        functools.partial(mlp_body, last, spot_of, alternate),
        grid=(HALF // STEP,),
        in_specs=[
            tall(BLK, D),
            tall(BLK, D),
            whole(8, D),
            pl.BlockSpec((1, STEP), lambda j: (0, j)),
        ]
        + [pl.BlockSpec((4, D // CHUNKS, STEP), lambda j: (0, 0, j))] * 8
        + [pl.BlockSpec((1, D // CHUNKS, HALF), lambda j: (j, 0, 1))] * 8
        + [tall(BLK, D)] * (2 if last else 0),
        out_specs=[tall(D // 2, 2 * HALF)] * 2
        + [pl.BlockSpec((D // (HALF // STEP), VEC), lambda j: (j, 0))]
        + ([tall(BLK, D)] * 3 + [whole(8, D)] if last else [tall(BLK, D)] * 2),
        out_shape=[grads, grads, jax.ShapeDtypeStruct((D, VEC), jnp.float32)]
        + (
            [lows, acc, lows, jax.ShapeDtypeStruct((8, D), jnp.float32)]
            if last
            else [acc, acc]
        ),
        scratch_shapes=[
            pltpu.VMEM((D, STEP), jnp.bfloat16),
            pltpu.VMEM((STEP, D), jnp.bfloat16),
            pltpu.VMEM((BLK, D), jnp.bfloat16),
            pltpu.VMEM((D, BLK), jnp.bfloat16),
        ]
        + ([pltpu.VMEM((BLK, D), jnp.float32)] * 2 if last else []),
        compiler_params=pltpu.CompilerParams(vmem_limit_bytes=58 * 2**20),
        cost_estimate=pl.CostEstimate(
            flops=12 * BLK * D * HALF, bytes_accessed=30 * 2**20, transcendentals=BLK * HALF
        ),
        name="mlp_half",
    )(hidden, og, rows, up_bias, *parts, *parts, *(before or ()))


def weight_grads_body(core_of, plan, columns, *refs):
    keep, away, split = refs[-3:]
    core = core_of()
    rk = D // CHUNKS

    def put(pairs, first):
        for chip, (even, odd) in enumerate(pairs):
            cols = slice(first, first + even.shape[1])
            mine, other = jnp.where(core == 0, even, odd), jnp.where(core == 0, odd, even)
            for out, value, owner in ((keep, mine, core), (away, other, 1 - core)):
                to = jnp.where(owner == 0, owner_row(chip, 0), owner_row(chip, 1))
                out[pl.ds(pl.multiple_of(to * rk, rk), rk), cols] = value

    for (kind, ins), first in zip(plan, columns):
        if kind == "dot":
            nt = jnp.transpose(refs[ins[0]][...])
            for i in range(CHUNKS):
                to = owner_row(i // 2, i % 2) * rk + lax.rem(i % 2 + core, 2) * (D // 2)
                split[pl.ds(pl.multiple_of(to, rk), rk), :] = nt[i * rk : (i + 1) * rk]
            for i in ins[1:]:
                width = refs[i].shape[-1]
                for s in range(0, width, 512):
                    n = min(512, width - s)
                    g = low(dot(split[...], refs[i][:, s : s + n], NN))
                    keep[:, first + s : first + s + n] = g[: D // 2]
                    away[:, first + s : first + s + n] = g[D // 2 :]
                first += width
        else:
            a = refs[ins[0]][...]
            if kind == "transposed":
                a = low(jnp.transpose(a))
            elif kind == "vectors":
                sums, gate = refs[ins[1]], refs[ins[2]]
                a = jnp.concatenate([a[0:1], sums[0:1], gate[...], sums[1:2]], 0)
                a = jnp.concatenate([a, jnp.zeros((VEC - 4, D), jnp.float32)], 0)
                a = low(jnp.transpose(a) + refs[ins[3]][...] + refs[ins[4]][...])
            put(
                [
                    (a[i * rk : (i + 1) * rk], a[(i + 1) * rk : (i + 2) * rk])
                    for i in range(0, CHUNKS, 2)
                ],
                first,
            )


def weight_grads(core_of, plan, at=0, total=None, into=None):
    args, steps, columns, width, flops = [], [], [], 0, 0
    for kind, *arrays in plan:
        steps.append((kind, tuple(range(len(args), len(args) + len(arrays)))))
        args += arrays
        columns.append(width)
        if kind == "dot":
            n = sum(a.shape[1] for a in arrays[1:])
            flops += 2 * BLK * D * n
        elif kind == "vectors":
            n = VEC
        else:
            n = arrays[0].shape[1 if kind == "rows" else 0]
        width += n
    padded = -(-width // 512) * 512 if into else width
    total = total or width
    n = len(args)

    def body(*refs):
        outs = refs[n + 2 :] if into else refs[n:]
        weight_grads_body(core_of, steps, columns, *refs[:n], *outs)

    whole = [pl.BlockSpec(a.shape, lambda i, r=a.ndim: (0,) * r) for a in args]
    kept = [pl.BlockSpec(memory_space=pl.ANY)] * 2 if into else []
    return pl.pallas_call(
        body,
        grid=(1,),
        in_specs=whole + kept,
        out_specs=[pl.BlockSpec((D // 2, padded), lambda i: (0, at // padded))] * 2,
        out_shape=[jax.ShapeDtypeStruct((D // 2, total), jnp.bfloat16)] * 2,
        input_output_aliases={n: 0, n + 1: 1} if into else {},
        scratch_shapes=[pltpu.VMEM((D, BLK), jnp.bfloat16)],
        compiler_params=pltpu.CompilerParams(vmem_limit_bytes=56 * 2**20),
        cost_estimate=pl.CostEstimate(
            flops=flops, bytes_accessed=4 * D * width, transcendentals=0
        ),
        name="weight_grads",
    )(*args, *(into or ()))


def natural(keep, away):
    parts = [a.reshape(2, 2, 4, -1, a.shape[1]).transpose(2, 0, 1, 3, 4) for a in (keep, away)]
    parts[1] = parts[1].transpose(0, 2, 1, 3, 4)
    return jnp.stack(parts, 3).reshape(-1, keep.shape[1])


def finish_mlp(end_a, end_b):
    rows = end_a[0].shape[0]

    def body(a0, a1, b0, b1, up, down):
        halves = a0[...] + f32(a1[...]), b0[...] + f32(b1[...])
        lane = lax.broadcasted_iota(jnp.int32, (rows, 128), 1) < 64
        for i in range(0, CHUNKS, 2):
            a, b = (half[:, i * 64 : i * 64 + 128] for half in halves)
            up[:, i * 128 : (i + 1) * 128] = jnp.where(lane, a, pltpu.roll(b, 64, 1))
            up[:, (i + 1) * 128 : (i + 2) * 128] = jnp.where(lane, pltpu.roll(a, 64, 1), b)
        at = 0
        for half in halves:
            for q in range(HALF // D):
                down[at : at + rows, :] = half[:, HALF + q * D : HALF + (q + 1) * D]
                at += rows

    return pl.pallas_call(
        body,
        out_shape=[
            jax.ShapeDtypeStruct((rows, 2 * HALF), jnp.float32),
            jax.ShapeDtypeStruct((4 * rows, D), jnp.float32),
        ],
        name="finish_mlp",
    )(*end_a, *end_b)


def pack_first(attn_gain, mlp_gain, gate, down_bias, up_bias, *matrices):
    rows = matrices[0].shape[0]
    vectors = [v.reshape(1, -1) for v in (attn_gain, mlp_gain, gate, down_bias, up_bias)]

    def body(a, m, g, d, u, table, *rest):
        out = rest[-1]
        up = f32(u[...])
        column = [f32(v[...]) for v in (a, m, g, d)]
        column += [up[:, i : i + rows] for i in range(0, up.shape[1], rows)]
        column = jnp.transpose(jnp.concatenate(column, 0))
        column = jnp.concatenate(
            [column, jnp.zeros((rows, VEC - column.shape[1]), jnp.float32)], 1
        )
        first = 0
        for part in [table[...], low(column)] + [r[...] for r in rest[:-1]]:
            out[:, first : first + part.shape[1]] = part
            first += part.shape[1]

    return pl.pallas_call(
        body,
        out_shape=jax.ShapeDtypeStruct((rows, VEC + sum(m.shape[1] for m in matrices)), jnp.bfloat16),
        name="pack_first",
    )(*vectors, *matrices)


def pack_rest(query, sinit, skey, svalue, out_weight, up, down):
    rows = query.shape[0]
    half = down.shape[0] // 2

    def body(r, s, k, w, o, up, down, second, third, fourth):
        first = 0
        for part in (r, s, k, w, o):
            second[:, first : first + part.shape[1]] = part[...]
            first += part.shape[1]
        lane = lax.broadcasted_iota(jnp.int32, (rows, 128), 1) < 64
        for i in range(0, CHUNKS, 2):
            a = f32(up[:, i * 128 : (i + 1) * 128])
            b = f32(up[:, (i + 1) * 128 : (i + 2) * 128])
            at = slice(i * 64, i * 64 + 128)
            third[:, at] = low(jnp.where(lane, a, pltpu.roll(b, 64, 1)))
            fourth[:, at] = low(jnp.where(lane, pltpu.roll(a, 64, 1), b))
        for i, out in enumerate((third, fourth)):
            for q in range(half // rows):
                start = i * half + q * rows
                out[:, HALF + q * D : HALF + (q + 1) * D] = down[start : start + rows, :]

    return pl.pallas_call(
        body,
        out_shape=[
            jax.ShapeDtypeStruct((rows, NSTATE + 4 * D), jnp.bfloat16),
            jax.ShapeDtypeStruct((rows, 2 * HALF), jnp.bfloat16),
            jax.ShapeDtypeStruct((rows, 2 * HALF), jnp.bfloat16),
        ],
        name="pack_rest",
    )(query, sinit, skey, svalue, out_weight, up, down)


def readout(gstate, skv_full):
    def body(g, w, read, sent):
        r = dot(g[0], w[:, :D], NT) + dot(g[1], w[:, D:], NT)
        read[...] = r
        sent[...] = low(r)

    return pl.pallas_call(
        body,
        out_shape=[
            jax.ShapeDtypeStruct((NSTATE, D), jnp.float32),
            jax.ShapeDtypeStruct((NSTATE, D), jnp.bfloat16),
        ],
        compiler_params=pltpu.CompilerParams(vmem_limit_bytes=32 * 2**20),
        cost_estimate=pl.CostEstimate(
            flops=4 * NSTATE * D * D, bytes_accessed=9 * 2**20, transcendentals=0
        ),
        name="readout",
    )(gstate, skv_full)


def embedding_back(gq, gk, gv, query_full, kv_full, embedded, grad_hidden, rows):
    def body(q, k, v, wq, w, e, g_out, r, grad, lowered, gain_grad):
        g = dot(q[...], wq[...], NT) + dot(k[...], w[:, :D], NT) + dot(v[...], w[:, D:], NT)
        emb = e[...]
        scale = lax.rsqrt(jnp.mean(emb * emb, -1, keepdims=True) + 1e-06)
        normed = emb * scale
        gain_grad[...] = jnp.broadcast_to(jnp.sum(g * normed, 0, keepdims=True), gain_grad.shape)
        g = g * r[0:1, :]
        g = g_out[...] + scale * (g - normed * jnp.mean(g * normed, -1, keepdims=True))
        grad[...] = g
        lowered[...] = low(g)

    return pl.pallas_call(
        body,
        out_shape=[
            jax.ShapeDtypeStruct((BLK, D), jnp.float32),
            jax.ShapeDtypeStruct((BLK, D), jnp.bfloat16),
            jax.ShapeDtypeStruct((8, D), jnp.float32),
        ],
        compiler_params=pltpu.CompilerParams(vmem_limit_bytes=48 * 2**20),
        cost_estimate=pl.CostEstimate(
            flops=6 * BLK * D * D, bytes_accessed=18 * 2**20, transcendentals=0
        ),
        name="embedding_back",
    )(gq, gk, gv, query_full, kv_full, embedded, grad_hidden, rows)


def layer(
    fast,
    char_ids,
    char_table,
    attn_gain,
    query_weight,
    key_weight,
    value_weight,
    out_weight,
    state_key_weight,
    state_value_weight,
    update_weight,
    state_query,
    state_init,
    gate_bias,
    position_table,
    mlp_gain,
    up_weight,
    up_bias,
    down_weight,
    down_bias,
    out_grad,
):
    rows = attn_gain.shape[0]
    ff = up_weight.shape[1]
    folds = ff // D
    main = VOCAB + VEC
    spot_of = here if fast else (lambda: (jnp.int32(0),) * 3)
    core_of = core_index if fast else (lambda: jnp.int32(0))
    layouts = (
        ((0, main, 1), (main, 2 * D, 1), (main + 2 * D, NSTATE, 1), (main + 2 * D + NSTATE, D, 1)),
        ((0, D, 1), (D, NSTATE, 1), (D + NSTATE, 2 * D, 1), (D + NSTATE + 2 * D, D, 1)),
    )
    if fast:
        shard1 = pack_first(
            attn_gain,
            mlp_gain,
            gate_bias,
            down_bias,
            up_bias,
            char_table,
            key_weight,
            value_weight,
            state_query,
            update_weight,
        )
        z1 = along_z(shard1)
        shard2, shard3, shard4 = pack_rest(
            query_weight,
            state_init,
            state_key_weight,
            state_value_weight,
            out_weight,
            up_weight,
            down_weight,
        )
        z1[:3], shard2, shard3, shard4 = join(z1[:3], shard2, shard3, shard4)
        p1 = stack_z(shard1, *z1)
        shard2 = tie(shard2, p1)
        z2 = along_z(shard2)
        sides1, z2[:3] = join(to_sides(p1), z2[:3])
        shard3, p2 = join(shard3, stack_z(shard2, *z2))
        corner1, near3 = join(to_corner(p1, sides1), send(shard3, Z_NEAR))
        z3, sides2 = far_z(shard3, near3), to_sides(p2, X_ROUTE, Y_ROUTE)
        table_vec, kv_full, squery_full, update_full = assemble(
            pieces(p1, sides1, corner1, last_corner(corner1)), layouts[0], True
        )
    else:
        vectors = jnp.concatenate([attn_gain, mlp_gain, gate_bias, down_bias, up_bias])
        vectors = vectors.reshape(4 + folds, rows)
        columns = jnp.pad(jnp.transpose(vectors), ((0, 0), (0, VEC - vectors.shape[0])))
        table_vec, kv_full, squery_full, update_full = gather_any(
            jnp.concatenate(
                [char_table, columns, key_weight, value_weight, state_query, update_weight], 1
            ),
            layouts[0],
        )

    vector_rows = jnp.transpose(f32(table_vec[:, VOCAB : VOCAB + 4 + folds]))
    biases = halves_of_columns(
        vector_rows[4:].reshape(folds, -1, rows).transpose(1, 0, 2).reshape(1, ff)
    )
    keep_gate = jax.nn.sigmoid(vector_rows[2])
    is_first = lax.axis_index("seq") == 0
    bias_rows = f32(position_table)[:, None, :]

    one_hot = (char_ids[:, None] == jnp.arange(VOCAB)[None, :]).astype(jnp.bfloat16)
    embedded = dot(one_hot, table_vec[:, :VOCAB], NT)
    normed_low = low(embedded * norm_scale(embedded) * vector_rows[0])
    kv = low(dot(normed_low, kv_full, NN))
    state_mix, state_lse = state_attention(kv, squery_full)
    update = dot(state_mix, update_full, NN)
    mine = low((1.0 - keep_gate) * update)
    if fast:
        sides2, z3[:3], mine = join(sides2, z3[:3], mine)
        sibling = send(mine, CORE_ROUTE)
        near = earlier_near(keep_gate, mine, sibling)
        prev = from_behind(tie(kv, mine), "seq", 1)
        corner2 = to_corner(p2, sides2, Y_ROUTE)
        near, corner2, prev, near4, p3 = join(
            near, corner2, prev, send(tie(shard4, mine), Z_NEAR), stack_z(shard3, *z3)
        )
        sides3, z4 = to_sides(p3), far_z(shard4, near4)
        query_full, sinit_full, skv_full, out_full = assemble(
            pieces(p2, sides2, corner2, last_corner(corner2)), layouts[1], False
        )
    else:
        prev = from_behind(kv, "seq", 1)
        query_full, sinit_full, skv_full, out_full = gather_any(
            jnp.concatenate(
                [query_weight, state_init, state_key_weight, state_value_weight, out_weight], 1
            ),
            layouts[1],
        )
    query = low(dot(normed_low, query_full, NN))
    start = f32(join(jnp.transpose(sinit_full))[0])
    if fast:
        state_prev = earlier_sum(keep_gate, near, sibling, start)
    else:
        gain, total = entering(keep_gate, mine, False)
        state_prev = gain * start + total
    state_low = low(state_prev)
    skv = low(dot(state_low, skv_full, NN))
    if fast:
        skv, query, sides3, z4[:3] = join(skv, query, sides3, z4[:3])
        corner3, p4 = to_corner(p3, sides3), stack_z(shard4, *z4)
    mixed, lse = attention(query, kv, prev, skv, bias_rows)
    hidden = embedded + dot(mixed, out_full, NN)

    if fast:
        corner3, hidden, p4 = join(corner3, hidden, p4)
        sides4 = to_sides(p4)
        parts = pieces(p3, sides3, corner3, last_corner(corner3))
        keep_a, away_a, bias_a, *before = mlp_half(
            spot_of, True, hidden, out_grad, vector_rows, biases[0], parts, None
        )
        sides4, away_a, before = join(sides4, away_a, before)
        corner4, got_a = join(to_corner(p4, sides4), to_core(away_a))
        parts = pieces(p4, sides4, corner4, last_corner(corner4))
        first_a = over_first(keep_a, got_a)
        keep_b, away_b, bias_b, *before = mlp_half(
            spot_of, True, hidden, out_grad, vector_rows, biases[1], parts, before
        )
        first_a, away_b, before = join(first_a, away_b, before)
    else:
        shard = jnp.concatenate([up_weight, fold(down_weight, rows)], 1)
        up_full, down_full = gather_any(shard, ((0, ff, 1), (ff, D, folds)))
        halves = []
        for up, down in zip(halves_of_columns(up_full), halves_of_rows(down_full, CHUNKS)):
            down = down.reshape(CHUNKS, 2, -1, D).transpose(0, 2, 1, 3).reshape(D, HALF)
            both = jnp.concatenate([up, down], 1).reshape(4, 2, 2, 2, -1, 2 * HALF)
            halves.append([both[:, i // 2 % 2, i % 2, i // 4] for i in range(8)])
        keep_a, away_a, bias_a, *before = mlp_half(
            spot_of, False, hidden, out_grad, vector_rows, biases[0], halves[0], None
        )
        keep_b, away_b, bias_b, *before = mlp_half(
            spot_of, False, hidden, out_grad, vector_rows, biases[1], halves[1], before
        )
    output, grad_hidden, grad_branch, mlp_sums = before

    grad_mixed = low(dot(grad_branch, out_full, NT))
    if fast:
        second_a = over_second(keep_a, got_a, first_a)
        got_b, grad_mixed = join(to_core(away_b), grad_mixed)
        first_b = over_first(keep_b, got_b)
    gq, gkv, gprev, gstate, gbias = attention_back(
        query, kv, prev, skv, bias_rows, lse, grad_mixed
    )
    gbias = gbias.reshape(HEADS, BLK)
    if fast:
        second_a, first_b, gprev, gstate = join(second_a, first_b, gprev, gstate)
    read, sent = readout(gstate, skv_full)
    if fast:
        sibling = send(sent, CORE_ROUTE)
        near = later_near(keep_gate, sent, sibling)
    first = weight_grads(
        core_of,
        [
            ("dot", mixed, grad_branch),
            ("dot", state_low, gstate[0], gstate[1]),
            ("dot", normed_low, gq),
        ],
    )
    if fast:
        pair_a = over_pairs(keep_a, got_a, first_a, tie(second_a, first[0]))
        near, first = join(near, first)
        gprev = tie(gprev, near)
        gnext = from_behind(gprev, "seq", -1)
        got_c = to_core(first[1])
        after = later_sum(keep_gate, near, sibling)
    else:
        gnext = from_behind(gprev, "seq", -1)
        after = entering(keep_gate, sent, True)[1]
    grad_update = low((1.0 - keep_gate) * after)
    grad_smix = low(dot(grad_update, update_full, NT))
    if fast:
        got_c, grad_smix = join(got_c, grad_smix)
        gbias = exchange(tie(gbias, grad_smix), CORE_ROUTE)
    gsum, gquery = state_attention_back(kv, squery_full, state_lse, grad_smix, gkv)
    if fast:
        gsum, after = join(gsum, after)
    state_init_grad = jnp.where(is_first, read + keep_gate * after, 0.0)
    last = weight_grads(
        core_of,
        [
            ("dot", state_mix, grad_update),
            ("rows", gquery),
            ("transposed", state_init_grad),
        ],
        0,
        4 * D + 512,
    )
    if fast:
        gnext, last, gbias, pair_a = join(gnext, last, gbias, pair_a)
        second_b = over_second(keep_b, got_b, tie(first_b, gnext))
        first_c = over_first(first[0], tie(got_c, gnext))
        gbias = exchange(gbias, X_ROUTE)
    gk, gv = (low(gsum[i] + f32(gnext[i])) for i in range(2))
    last = weight_grads(core_of, [("dot", normed_low, gk, gv)], 2 * D, 4 * D + 512, last)
    embedded_grad, embedded_low, gain_grad = embedding_back(
        gq, gk, gv, query_full, kv_full, embedded, grad_hidden, vector_rows
    )
    gate_bias_grad = jnp.sum(after * (state_prev - update), 0) * keep_gate * (1.0 - keep_gate)
    last = weight_grads(
        core_of,
        [
            ("dot", embedded_low, one_hot),
            ("vectors", gain_grad, mlp_sums, gate_bias_grad[None], bias_a, bias_b),
        ],
        4 * D,
        4 * D + 512,
        last,
    )
    if fast:
        second_b, first_c, last, gbias = join(second_b, first_c, last, gbias)
        got_d = to_core(last[1])
        pair_b = over_pairs(keep_b, got_b, first_b, second_b)
        first_d = over_first(last[0], got_d)
        second_c = over_second(first[0], got_c, first_c)
        end_a = within_pair(*pair_a)
        gbias = exchange(gbias, Y_ROUTE)
        second_c, first_d, pair_b, end_a, gbias = join(second_c, first_d, pair_b, end_a, gbias)
        second_d = over_second(last[0], got_d, first_d)
        pair_c = over_pairs(first[0], got_c, first_c, second_c)
        end_b = within_pair(*pair_b)
        gbias = exchange(gbias, Z_NEAR)
        second_d, end_b, gbias = join(second_d, end_b, gbias)
        up_sum, down_sum = finish_mlp(end_a, end_b)
        end_d = over_z(last[0], got_d, first_d, second_d)
        pair_c, up_sum = join(pair_c, up_sum)
        end_c = within_pair(*pair_c)
        position_table_grad = exchange(gbias, Z_FAR)
        first, last = finish(end_c), finish(end_d)
    else:
        pairs = [natural(keep_a, away_a), natural(keep_b, away_b)]
        up_sum = jnp.concatenate([s[:, :HALF].reshape(D, CHUNKS, -1) for s in pairs], 2)
        up_sum = scatter_any(up_sum.reshape(D, ff))
        down_sum = jnp.concatenate(
            [
                s[:, HALF:].reshape(CHUNKS, D // CHUNKS, -1, D).transpose(0, 2, 1, 3)
                for s in pairs
            ],
            1,
        )
        down_sum = scatter_any(down_sum.reshape(ff, D))
        first, last = (scatter_any(natural(*s)) for s in (first, last))
        position_table_grad = lax.psum(gbias, AX)
    main = 4 * D + VOCAB
    vector_sum = last[:, main:]
    return (
        output,
        embedded_grad,
        last[:, 4 * D : main],
        vector_sum[:, 0],
        first[:, 3 * D :],
        last[:, 2 * D : 3 * D],
        last[:, 3 * D : 4 * D],
        first[:, :D],
        first[:, D : 2 * D],
        first[:, 2 * D : 3 * D],
        last[:, :D],
        last[:, D : D + NSTATE],
        last[:, D + NSTATE : 2 * D],
        vector_sum[:, 2],
        position_table_grad,
        vector_sum[:, 1],
        up_sum,
        jnp.transpose(vector_sum[:, 4 : 4 + folds]).reshape(-1),
        down_sum,
        vector_sum[:, 3],
    )


def solution(mesh):
    fast = dict(mesh.shape) == {"dp": 8, "seq": 4}
    return jax.shard_map(
        functools.partial(layer, fast),
        mesh=mesh,
        in_specs=(
            P(("dp", "seq")),
            P(("dp", "seq"), None),
            P(("dp", "seq")),
            P(("dp", "seq"), None),
            P(("dp", "seq"), None),
            P(("dp", "seq"), None),
            P(("dp", "seq"), None),
            P(("dp", "seq"), None),
            P(("dp", "seq"), None),
            P(("dp", "seq"), None),
            P(("dp", "seq"), None),
            P(("dp", "seq"), None),
            P(("dp", "seq")),
            P(),
            P(("dp", "seq")),
            P(("dp", "seq"), None),
            P(("dp", "seq")),
            P(("dp", "seq"), None),
            P(("dp", "seq")),
            P(("dp", "seq"), None),
        ),
        out_specs=(
            P(("dp", "seq"), None),
            P(("dp", "seq"), None),
            P(("dp", "seq"), None),
            P(("dp", "seq")),
            P(("dp", "seq"), None),
            P(("dp", "seq"), None),
            P(("dp", "seq"), None),
            P(("dp", "seq"), None),
            P(("dp", "seq"), None),
            P(("dp", "seq"), None),
            P(("dp", "seq"), None),
            P(("dp", "seq"), None),
            P(("dp", "seq"), None),
            P(("dp", "seq")),
            P(),
            P(("dp", "seq")),
            P(("dp", "seq"), None),
            P(("dp", "seq")),
            P(("dp", "seq"), None),
            P(("dp", "seq")),
        ),
        check_vma=False,
    )
```

```python
import functools

import jax
import jax.numpy as jnp
from jax import lax
from jax.experimental import pallas as pl
from jax.experimental.pallas import tpu as pltpu
from jax.sharding import PartitionSpec as P

D = 1024
HEADS = 8
HD = 128
NSTATE = 512
VOCAB = 256
BLK = 512
AX = ("dp", "seq")
VEC = 128


def f32(v):
    return v.astype(jnp.float32)


def low(v):
    return v.astype(jnp.bfloat16)


def route(move):
    pairs = []
    for z in range(4):
        for y in range(2):
            for x in range(2):
                for c in range(2):
                    tz, ty, tx, tc = move(z, y, x, c)
                    pairs.append((z * 8 + y * 4 + x * 2 + c, tz * 8 + ty * 4 + tx * 2 + tc))
    return pairs


A_ROUTE = route(lambda z, y, x, c: (z, y, 1 - x, c) if c == 0 else (z, 1 - y, x, c))
B_ROUTE = route(lambda z, y, x, c: (z, 1 - y, x, c) if c == 0 else (z, y, 1 - x, c))
CORE_ROUTE = route(lambda z, y, x, c: (z, y, x, 1 - c))
X_ROUTE = route(lambda z, y, x, c: (z, y, 1 - x, c))
Y_ROUTE = route(lambda z, y, x, c: (z, 1 - y, x, c))
Z_NEAR = route(lambda z, y, x, c: (z ^ 1, y, x, c))
Z_FAR = route(lambda z, y, x, c: (z ^ 2, y, x, c))
Z_ROUTE = {k: route(lambda z, y, x, c, k=k: ((z + k) % 4, y, x, c)) for k in (1, 2, 3)}


def place():
    d, s = lax.axis_index("dp"), lax.axis_index("seq")
    return d // 2, d % 2, s // 2, s % 2


def send(v, pairs):
    return lax.ppermute(v, AX, pairs)


def stack_z(shard, *others):
    others, cyclic = others[:3], others[3]

    def body(*refs):
        z = lax.axis_index("dp") // 2
        near = z + 1 - 2 * lax.rem(z, 2)
        spots = (
            [lax.rem(z + 4 - i, 4) for i in range(4)]
            if cyclic
            else [z, near, lax.rem(z + 2, 4), lax.rem(near + 2, 4)]
        )
        for at, src in zip(spots, refs[:4]):
            refs[4][at] = src[...]

    return pl.pallas_call(
        body, out_shape=jax.ShapeDtypeStruct((4,) + shard.shape, shard.dtype), name="stack_z"
    )(shard, *others)


def here():
    return lax.rem(lax.axis_index("dp"), 2), lax.axis_index("seq") // 2, core_index()


def core_index():
    return lax.rem(lax.axis_index("seq"), 2)


def origin(i, spot, alternate):
    y, x, c = spot
    core = c if i < 4 else 1 - c
    if alternate:
        flip_x = (0, 1 - core, core, 1)[i % 4]
        flip_y = (0, core, 1 - core, 1)[i % 4]
    else:
        flip_x, flip_y = i % 2, i % 4 // 2
    return lax.rem(y + flip_y, 2), lax.rem(x + flip_x, 2), core


def assemble(pieces, layout, alternate):
    rows, width = pieces[0].shape[1:]

    def body(*refs):
        ins, outs = refs[:8], refs[8:]
        spot = here()
        for i, src in enumerate(ins):
            ty, tx, core = origin(i, spot, alternate)
            for (first, w, folds), out in zip(layout, outs):
                for q in range(folds):
                    out[0, ty, tx, core, q * rows : (q + 1) * rows, :] = src[
                        0, :, first + q * w : first + (q + 1) * w
                    ]

    full = pl.pallas_call(
        body,
        out_shape=[
            jax.ShapeDtypeStruct((4, 2, 2, 2, rows * n, w), pieces[0].dtype) for _, w, n in layout
        ],
        grid=(4,),
        in_specs=[pl.BlockSpec((1, rows, width), lambda z: (z, 0, 0))] * 8,
        out_specs=[
            pl.BlockSpec((1, 2, 2, 2, rows * n, w), lambda z: (z, 0, 0, 0, 0, 0))
            for _, w, n in layout
        ],
        compiler_params=pltpu.CompilerParams(vmem_limit_bytes=40 * 2**20),
        name="assemble",
    )(*pieces)
    return [o.reshape(32 * rows * n, w) for o, (_, w, n) in zip(full, layout)]


def tie(value, *others):
    return lax.optimization_barrier((value, others))[0]


def join(*values):
    return lax.optimization_barrier(values)


def along_z(shard):
    return [send(shard, Z_ROUTE[k]) for k in (1, 2, 3)] + [True]


def far_z(shard, near):
    return [near, send(shard, Z_FAR), send(near, Z_FAR), False]


def to_sides(p, a=A_ROUTE, b=B_ROUTE):
    return send(p, a), send(p, b)


def to_corner(p, sides, b=B_ROUTE):
    return send(sides[0], b), [send(v, CORE_ROUTE) for v in (p,) + tuple(sides)]


def last_corner(corner):
    return send(corner[0], CORE_ROUTE)


def pieces(p, sides, corner, last):
    return (p,) + tuple(sides) + (corner[0],) + tuple(corner[1]) + (last,)


def to_core(away):
    return send(away, CORE_ROUTE)


def first_axis():
    z, y, x, c = place()
    return jnp.where(c == 0, y, x), jnp.where(c == 0, x, y)


def chip_part(keep, got, b, a=None):
    rows, width = keep.shape[0] // 16, keep.shape[1]
    start, size = ((b, 0), (1, 2)) if a is None else ((b, a), (1, 1))
    at = [
        lax.dynamic_slice(
            v.reshape(2, 2, 4, rows, width), start + (0, 0, 0), size + (4, rows, width)
        )
        for v in (keep, got)
    ]
    return (f32(at[0]) + f32(at[1])).reshape(size[1], 4, rows, width)


def over_first(keep, got):
    return send(low(chip_part(keep, got, 1 - first_axis()[0])), B_ROUTE)


def of_first(first, i):
    return lax.dynamic_index_in_dim(first, i, 0)


def over_second(keep, got, first):
    b, a = first_axis()
    far = of_first(first, 1 - a)
    return send(low(chip_part(keep, got, b, 1 - a) + f32(far)), A_ROUTE)


def own_part(keep, got, first, second):
    b, a = first_axis()
    mine = of_first(first, a)
    return (chip_part(keep, got, b, a) + f32(mine) + f32(second))[0]


def over_pairs(keep, got, first, second):
    z = place()[0]
    own = own_part(keep, got, first, second)
    pairs = own.reshape((2, 2) + own.shape[1:])
    away = lax.dynamic_index_in_dim(pairs, 1 - z // 2, 0, False)
    return lax.dynamic_index_in_dim(pairs, z // 2, 0, False), send(low(away), Z_FAR)


def within_pair(mine, got):
    z = place()[0]

    def pick(i):
        return lax.dynamic_index_in_dim(mine, i, 0, False) + f32(
            lax.dynamic_index_in_dim(got, i, 0, False)
        )

    return pick(z % 2), send(low(pick(1 - z % 2)), Z_NEAR)


def over_z(keep, got, first, second):
    z = place()[0]
    own = own_part(keep, got, first, second)
    rest = [low(lax.dynamic_index_in_dim(own, (z + k) % 4, 0, False)) for k in (1, 2, 3)]
    mine = lax.dynamic_index_in_dim(own, z, 0, False)
    return [mine] + [send(v, Z_ROUTE[k]) for v, k in zip(rest, (1, 2, 3))]


def finish(parts):
    return sum(f32(p) for p in parts)


def gather_any(shard, layout):
    rows = shard.shape[0]
    full = lax.all_gather(shard, AX, axis=0, tiled=True)
    outs = []
    for first, w, folds in layout:
        part = full[:, first : first + w * folds]
        if folds > 1:
            part = part.reshape(-1, rows, folds, w).transpose(0, 2, 1, 3).reshape(-1, w)
        outs.append(part)
    return outs


def scatter_any(grad):
    return lax.psum_scatter(f32(grad), AX, scatter_dimension=0, tiled=True)


def exchange(value, pairs):
    return value + send(value, pairs)


def half_across(chip):
    c = place()[3]
    half = NSTATE // 2
    return send(lax.dynamic_slice(chip, (c * half, 0), (half, D)), X_ROUTE)


def both_halves(near):
    c = place()[3]
    far = send(near, CORE_ROUTE)
    return jnp.concatenate([jnp.where(c == 0, near, far), jnp.where(c == 0, far, near)], 0)


def in_order(mine, sibling):
    c = place()[3]
    return jnp.where(c == 0, f32(mine), f32(sibling)), jnp.where(c == 0, f32(sibling), f32(mine))


def earlier_near(keep_gate, mine, sibling):
    first, second = in_order(mine, sibling)
    return half_across(low(keep_gate * first + second))


def earlier_sum(keep_gate, near, sibling, start):
    z, y, x, c = place()
    other = both_halves(near)
    before = jnp.where(x == 0, start, keep_gate * keep_gate * start + f32(other))
    return jnp.where(c == 0, before, keep_gate * before + f32(sibling))


def later_near(keep_gate, mine, sibling):
    first, second = in_order(mine, sibling)
    return half_across(low(first + keep_gate * second))


def later_sum(keep_gate, near, sibling):
    z, y, x, c = place()
    after = jnp.where(x == 0, f32(both_halves(near)), 0.0)
    return jnp.where(c == 0, f32(sibling) + keep_gate * after, after)


def from_behind(block, axis, distance):
    devices = range(lax.axis_size(axis))
    pairs = [(i - distance, i) for i in devices if i - distance in devices]
    return lax.ppermute(block, axis, pairs)


def entering(keep_gate, mine, reverse):
    devices, at_home = lax.axis_size("seq"), lax.axis_index("seq")
    everything = lax.all_gather(mine, "seq")

    def turn(k, before):
        at = devices - 1 - k if reverse else k
        reached = at > at_home if reverse else at < at_home
        gain, total = before
        return (
            jnp.where(reached, gain * keep_gate, gain),
            jnp.where(reached, keep_gate * total + f32(everything[at]), total),
        )

    start = (jnp.ones_like(keep_gate), jnp.zeros(mine.shape, jnp.float32))
    return lax.fori_loop(0, devices, turn, start)


def norm_scale(values):
    return lax.rsqrt(jnp.mean(values * values, -1, keepdims=True) + 1e-06)


def halves_of_columns(a):
    parts = a.reshape(a.shape[0], CHUNKS, 2, -1)
    return [parts[:, :, i].reshape(a.shape[0], -1) for i in range(2)]


def halves_of_rows(a, chunks):
    parts = a.reshape(chunks, 2, -1, a.shape[1])
    return [parts[:, i].reshape(-1, a.shape[1]) for i in range(2)]


def fold(a, rows):
    return a.reshape(-1, rows, D).transpose(1, 0, 2).reshape(rows, -1)


def unfold(a):
    rows = a.shape[0]
    return a.reshape(rows, -1, D).transpose(1, 0, 2).reshape(-1, D)


SCALE = HD ** (-0.5)


def dot(a, b, dims):
    return lax.dot_general(a, b, (dims, ((), ())), preferred_element_type=jnp.float32)


NN, NT, TN = ((1,), (0,)), ((1,), (1,)), ((0,), (0,))


def head_block(first):
    return pl.BlockSpec((BLK, HD), lambda h: (0, first + h))


def pair_block():
    return pl.BlockSpec((2, BLK, HD), lambda h: (0, 0, h))


def row_block():
    return pl.BlockSpec((1, 1, BLK), lambda h: (h, 0, 0))


def token_scores(q, k, kp, bias_row, is_first):
    row = lax.broadcasted_iota(jnp.int32, (BLK, BLK), 0)
    col = lax.broadcasted_iota(jnp.int32, (BLK, BLK), 1)
    own = row <= col
    bias = jnp.concatenate([bias_row] + [pltpu.roll(bias_row, i, 1) for i in range(1, 8)], 0)
    while bias.shape[0] < BLK:
        bias = jnp.concatenate([bias, pltpu.roll(bias, bias.shape[0], 1)], 0)
    raw = jnp.where(own, dot(k, q, NT), dot(kp, q, NT))
    scores = raw * SCALE + bias
    return jnp.where(own | jnp.logical_not(is_first), scores, -1e30), own


def attention_body(q, k, v, kp, vp, sk, sv, bias, mixed, lse):
    is_first = lax.axis_index("seq") == 0
    q = q[...]
    tokens, own = token_scores(q, k[...], kp[...], bias[0], is_first)
    states = dot(sk[...], q, NT) * SCALE
    top = jnp.maximum(jnp.max(tokens, 0, keepdims=True), jnp.max(states, 0, keepdims=True))
    tokens, states = jnp.exp(tokens - top), jnp.exp(states - top)
    total = jnp.sum(tokens, 0, keepdims=True) + jnp.sum(states, 0, keepdims=True)
    lse[0] = top + jnp.log(total)
    mix = dot(jnp.transpose(v[...]), low(jnp.where(own, tokens, 0.0)), NN)
    mix += dot(jnp.transpose(vp[...]), low(jnp.where(own, 0.0, tokens)), NN)
    mix += dot(jnp.transpose(sv[...]), low(states), NN)
    mixed[...] = low(jnp.transpose(mix * (1.0 / total)))


def attention(query, kv, prev, skv, bias):
    return pl.pallas_call(
        attention_body,
        grid=(HEADS,),
        in_specs=[head_block(0)]
        + [head_block(0), head_block(HEADS)] * 3
        + [row_block()],
        out_specs=[head_block(0), row_block()],
        out_shape=[
            jax.ShapeDtypeStruct((BLK, D), jnp.bfloat16),
            jax.ShapeDtypeStruct((HEADS, 1, BLK), jnp.float32),
        ],
        compiler_params=pltpu.CompilerParams(vmem_limit_bytes=40 * 2**20),
        cost_estimate=pl.CostEstimate(
            flops=12 * HEADS * BLK * BLK * HD,
            bytes_accessed=9 * 2**20,
            transcendentals=2 * HEADS * BLK * BLK,
        ),
        name="attention",
    )(query, kv, kv, prev, prev, skv, skv, bias)


def attention_back_body(
    q, k, v, kp, vp, sk, sv, bias, lse, go, gq, gkv, gprev, gstate, gbias
):
    is_first = lax.axis_index("seq") == 0
    q, k, kp, sk, go = q[...], k[...], kp[...], sk[...], go[...]
    tokens, own = token_scores(q, k, kp, bias[0], is_first)
    log_total = lse[0]
    tokens = jnp.exp(tokens - log_total)
    states = jnp.exp(dot(sk, q, NT) * SCALE - log_total)
    gtokens = jnp.where(own, dot(v[...], go, NT), dot(vp[...], go, NT))
    gstates = dot(sv[...], go, NT)
    mean = jnp.sum(tokens * gtokens, 0, keepdims=True) + jnp.sum(states * gstates, 0, keepdims=True)
    gkv[1] = dot(low(jnp.where(own, tokens, 0.0)), go, NN)
    gprev[1] = low(dot(low(jnp.where(own, 0.0, tokens)), go, NN))
    gstate[1] = low(dot(low(states), go, NN))
    gtokens = low(tokens * (gtokens - mean))
    gstates = low(states * (gstates - mean))
    wide = f32(gtokens)
    gown, gbefore = low(jnp.where(own, wide, 0.0)), low(jnp.where(own, 0.0, wide))
    gkv[0] = dot(gown, q, NN) * SCALE
    gprev[0] = low(dot(gbefore, q, NN) * SCALE)
    gstate[0] = low(dot(gstates, q, NN) * SCALE)
    g = dot(jnp.transpose(k), gown, NN)
    g += dot(jnp.transpose(kp), gbefore, NN)
    g += dot(jnp.transpose(sk), gstates, NN)
    gq[...] = low(jnp.transpose(g * SCALE))
    rows = BLK
    while rows > 1:
        rows //= 2
        wide = wide[:rows] + pltpu.roll(wide[rows:], BLK - rows, 1)
    gbias[0] = wide


def attention_back(query, kv, prev, skv, bias, lse, go):
    return pl.pallas_call(
        attention_back_body,
        grid=(HEADS,),
        in_specs=[head_block(0)]
        + [head_block(0), head_block(HEADS)] * 3
        + [row_block(), row_block(), head_block(0)],
        out_specs=[head_block(0), pair_block(), pair_block(), pair_block(), row_block()],
        out_shape=[
            jax.ShapeDtypeStruct((BLK, D), jnp.bfloat16),
            jax.ShapeDtypeStruct((2, BLK, D), jnp.float32),
            jax.ShapeDtypeStruct((2, BLK, D), jnp.bfloat16),
            jax.ShapeDtypeStruct((2, BLK, D), jnp.bfloat16),
            jax.ShapeDtypeStruct((HEADS, 1, BLK), jnp.float32),
        ],
        compiler_params=pltpu.CompilerParams(vmem_limit_bytes=48 * 2**20),
        cost_estimate=pl.CostEstimate(
            flops=30 * HEADS * BLK * BLK * HD,
            bytes_accessed=18 * 2**20,
            transcendentals=2 * HEADS * BLK * BLK,
        ),
        name="attention_back",
    )(query, kv, kv, prev, prev, skv, skv, bias, lse, go)


def query_block():
    return pl.BlockSpec((HD, NSTATE), lambda h: (h, 0))


def state_body(k, v, query, mixed, lse):
    scores = dot(k[...], query[...], NN) * SCALE
    top = jnp.max(scores, 0, keepdims=True)
    scores = jnp.exp(scores - top)
    total = jnp.sum(scores, 0, keepdims=True)
    lse[0] = top + jnp.log(total)
    mix = dot(jnp.transpose(v[...]), low(scores), NN)
    mixed[...] = low(jnp.transpose(mix * (1.0 / total)))


def state_attention(kv, query):
    return pl.pallas_call(
        state_body,
        grid=(HEADS,),
        in_specs=[head_block(0), head_block(HEADS), query_block()],
        out_specs=[head_block(0), row_block()],
        out_shape=[
            jax.ShapeDtypeStruct((NSTATE, D), jnp.bfloat16),
            jax.ShapeDtypeStruct((HEADS, 1, NSTATE), jnp.float32),
        ],
        compiler_params=pltpu.CompilerParams(vmem_limit_bytes=32 * 2**20),
        cost_estimate=pl.CostEstimate(
            flops=4 * HEADS * BLK * BLK * HD,
            bytes_accessed=4 * 2**20,
            transcendentals=HEADS * BLK * BLK,
        ),
        name="state_attention",
    )(kv, kv, query)


def state_back_body(k, v, query, lse, go, gkv, gsum, gquery):
    k, query, go = k[...], query[...], go[...]
    probs = jnp.exp(dot(k, query, NN) * SCALE - lse[0])
    gprobs = dot(v[...], go, NT)
    mean = jnp.sum(probs * gprobs, 0, keepdims=True)
    gsum[1] = dot(low(probs), go, NN) + gkv[1]
    gscores = low(probs * (gprobs - mean))
    gsum[0] = dot(gscores, query, NT) * SCALE + gkv[0]
    gquery[...] = low(dot(jnp.transpose(k), gscores, NN) * SCALE)


def state_attention_back(kv, query, lse, go, gkv):
    return pl.pallas_call(
        state_back_body,
        grid=(HEADS,),
        in_specs=[
            head_block(0),
            head_block(HEADS),
            query_block(),
            row_block(),
            head_block(0),
            pair_block(),
        ],
        out_specs=[pair_block(), query_block()],
        out_shape=[
            jax.ShapeDtypeStruct((2, BLK, D), jnp.float32),
            jax.ShapeDtypeStruct((D, NSTATE), jnp.bfloat16),
        ],
        compiler_params=pltpu.CompilerParams(vmem_limit_bytes=32 * 2**20),
        cost_estimate=pl.CostEstimate(
            flops=10 * HEADS * BLK * BLK * HD,
            bytes_accessed=14 * 2**20,
            transcendentals=HEADS * BLK * BLK,
        ),
        name="state_attention_back",
    )(kv, kv, query, lse, go, gkv)


STEP = 512
HALF = 2048
CHUNKS = 32


def owner_row(chip, swap):
    z, y, x = chip // 4, chip // 2 % 2, chip % 2
    return (x * 8 + y * 4 if swap else y * 8 + x * 4) + z


def gelu_parts(x):
    a, b = 0.7978845608028654, 0.044715
    square = x * x
    t = jnp.tanh(a * x * (1.0 + b * square))
    half = 0.5 * (1.0 + t)
    slope = half + (0.5 * a) * x * (1.0 - t * t) * (1.0 + 3.0 * b * square)
    return x * half, slope


def mlp_body(last, spot_of, alternate, *refs):
    hidden, og, rows, up_bias = refs[:4]
    ups, downs, refs = refs[4:12], refs[12:20], refs[20:]
    if last:
        out_in, u_in, keep, away, up_bias_grad, output, grad, branch, sums = refs[:9]
        up, down, xn, xs, out_acc, u_acc = refs[9:]
    else:
        keep, away, up_bias_grad, out_acc, u_acc = refs[:5]
        up, down, xn, xs = refs[5:]
    j = pl.program_id(0)
    spot = spot_of()
    core = spot[2]
    rk = D // CHUNKS
    hk = HALF // CHUNKS

    @pl.when(j == 0)
    def _():
        h = hidden[...]
        r = lax.rsqrt(jnp.mean(h * h, -1, keepdims=True) + 1e-06)
        n = low(h * r * rows[1:2, :])
        xn[...] = n
        nt = jnp.transpose(n)
        for i in range(CHUNKS):
            to = owner_row(i // 2, i % 2) * rk + lax.rem(i % 2 + core, 2) * (D // 2)
            xs[pl.ds(pl.multiple_of(to, rk), rk), :] = nt[i * rk : (i + 1) * rk]
        if last:
            out_acc[...] = out_in[...]
            u_acc[...] = u_in[...]
        else:
            out_acc[...] = jnp.zeros_like(out_acc)
            u_acc[...] = jnp.zeros_like(u_acc)

    for i in range(8):
        ty, tx, c = origin(i, spot, alternate)
        at = ty * 4 + tx * 2 + c
        for z in range(4):
            up[pl.ds(pl.multiple_of((z * 8 + at) * rk, rk), rk), :] = ups[i][z]
        for q in range(hk // rk):
            down[pl.ds(pl.multiple_of(at * hk + q * rk, rk), rk), :] = downs[i][
                0, :, q * D : (q + 1) * D
            ]
    up_w, down_w, g_out = up[...], down[...], og[...]
    act, slope = gelu_parts(dot(xn[...], up_w, NN) + up_bias[...])
    act = low(act)
    out_acc[...] += dot(act, down_w, NN)
    g_up = low(slope * dot(g_out, down_w, NT))
    column = jnp.transpose(
        jnp.broadcast_to(jnp.sum(f32(g_up), 0, keepdims=True), (8, STEP))
    )[:, :1]
    lane = lax.broadcasted_iota(jnp.int32, (rk, VEC), 1) - (4 + 2 * last)
    for i in range(STEP // hk):
        pair = [column[i * hk + q * rk : i * hk + (q + 1) * rk] for q in range(2)]
        up_bias_grad[i * rk : (i + 1) * rk, :] = jnp.where(
            lane == 0, pair[0], jnp.where(lane == 1, pair[1], 0.0)
        )
    u_acc[...] += dot(g_up, up_w, NT)
    d_up = low(dot(xs[...], g_up, NN))
    at = pl.ds(pl.multiple_of(j * STEP, STEP), STEP)
    keep[:, at] = d_up[: D // 2]
    away[:, at] = d_up[D // 2 :]
    d_down = low(dot(jnp.transpose(act), g_out, NN))
    for i in range(STEP // hk // 2):
        even = d_down[2 * i * hk : (2 * i + 1) * hk]
        odd = d_down[(2 * i + 1) * hk : (2 * i + 2) * hk]
        mine, other = jnp.where(core == 0, even, odd), jnp.where(core == 0, odd, even)
        for q in range(hk // rk):
            cols = slice(HALF + q * D, HALF + (q + 1) * D)
            part = slice(q * rk, (q + 1) * rk)
            for out, value, owner in ((keep, mine, core), (away, other, 1 - core)):
                to = jnp.where(owner == 0, owner_row(i, 0), owner_row(i, 1)) + j
                out[pl.ds(pl.multiple_of(to * rk, rk), rk), cols] = value[part]

    if last:

        @pl.when(j == pl.num_programs(0) - 1)
        def _():
            h = hidden[...]
            output[...] = low(h + out_acc[...] + rows[3:4, :])
            r = lax.rsqrt(jnp.mean(h * h, -1, keepdims=True) + 1e-06)
            n = h * r
            u = u_acc[...]
            ug = u * rows[1:2, :]
            g = f32(og[...]) + r * (ug - n * jnp.mean(ug * n, -1, keepdims=True))
            grad[...] = g
            branch[...] = low(g)
            sums[0:1, :] = jnp.sum(u * n, 0, keepdims=True)
            sums[1:2, :] = jnp.sum(f32(og[...]), 0, keepdims=True)


def mlp_half(spot_of, alternate, hidden, og, rows, up_bias, parts, before):
    last = before is not None
    whole = lambda a, b: pl.BlockSpec((a, b), lambda j: (0, 0))
    tall = lambda a, b: pl.BlockSpec((a, b), lambda j: (0, 0), pipeline_mode=pl.Buffered(1))
    acc = jax.ShapeDtypeStruct((BLK, D), jnp.float32)
    lows = jax.ShapeDtypeStruct((BLK, D), jnp.bfloat16)
    grads = jax.ShapeDtypeStruct((D // 2, 2 * HALF), jnp.bfloat16)
    return pl.pallas_call(
        functools.partial(mlp_body, last, spot_of, alternate),
        grid=(HALF // STEP,),
        in_specs=[
            tall(BLK, D),
            tall(BLK, D),
            whole(8, D),
            pl.BlockSpec((1, STEP), lambda j: (0, j)),
        ]
        + [pl.BlockSpec((4, D // CHUNKS, STEP), lambda j: (0, 0, j))] * 8
        + [pl.BlockSpec((1, D // CHUNKS, HALF), lambda j: (j, 0, 1))] * 8
        + [tall(BLK, D)] * (2 if last else 0),
        out_specs=[tall(D // 2, 2 * HALF)] * 2
        + [pl.BlockSpec((D // (HALF // STEP), VEC), lambda j: (j, 0))]
        + ([tall(BLK, D)] * 3 + [whole(8, D)] if last else [tall(BLK, D)] * 2),
        out_shape=[grads, grads, jax.ShapeDtypeStruct((D, VEC), jnp.float32)]
        + (
            [lows, acc, lows, jax.ShapeDtypeStruct((8, D), jnp.float32)]
            if last
            else [acc, acc]
        ),
        scratch_shapes=[
            pltpu.VMEM((D, STEP), jnp.bfloat16),
            pltpu.VMEM((STEP, D), jnp.bfloat16),
            pltpu.VMEM((BLK, D), jnp.bfloat16),
            pltpu.VMEM((D, BLK), jnp.bfloat16),
        ]
        + ([pltpu.VMEM((BLK, D), jnp.float32)] * 2 if last else []),
        compiler_params=pltpu.CompilerParams(vmem_limit_bytes=58 * 2**20),
        cost_estimate=pl.CostEstimate(
            flops=12 * BLK * D * HALF, bytes_accessed=30 * 2**20, transcendentals=BLK * HALF
        ),
        name="mlp_half",
    )(hidden, og, rows, up_bias, *parts, *parts, *(before or ()))


def weight_grads_body(core_of, plan, columns, *refs):
    keep, away, split = refs[-3:]
    core = core_of()
    rk = D // CHUNKS

    def put(pairs, first):
        for chip, (even, odd) in enumerate(pairs):
            cols = slice(first, first + even.shape[1])
            mine, other = jnp.where(core == 0, even, odd), jnp.where(core == 0, odd, even)
            for out, value, owner in ((keep, mine, core), (away, other, 1 - core)):
                to = jnp.where(owner == 0, owner_row(chip, 0), owner_row(chip, 1))
                out[pl.ds(pl.multiple_of(to * rk, rk), rk), cols] = value

    for (kind, ins), first in zip(plan, columns):
        if kind == "dot":
            nt = jnp.transpose(refs[ins[0]][...])
            for i in range(CHUNKS):
                to = owner_row(i // 2, i % 2) * rk + lax.rem(i % 2 + core, 2) * (D // 2)
                split[pl.ds(pl.multiple_of(to, rk), rk), :] = nt[i * rk : (i + 1) * rk]
            for i in ins[1:]:
                width = refs[i].shape[-1]
                for s in range(0, width, 512):
                    n = min(512, width - s)
                    g = low(dot(split[...], refs[i][:, s : s + n], NN))
                    keep[:, first + s : first + s + n] = g[: D // 2]
                    away[:, first + s : first + s + n] = g[D // 2 :]
                first += width
        else:
            a = refs[ins[0]][...]
            if kind == "transposed":
                a = low(jnp.transpose(a))
            elif kind == "vectors":
                sums, gate = refs[ins[1]], refs[ins[2]]
                a = jnp.concatenate([a[0:1], sums[0:1], gate[...], sums[1:2]], 0)
                a = jnp.concatenate([a, jnp.zeros((VEC - 4, D), jnp.float32)], 0)
                a = low(jnp.transpose(a) + refs[ins[3]][...] + refs[ins[4]][...])
            put(
                [
                    (a[i * rk : (i + 1) * rk], a[(i + 1) * rk : (i + 2) * rk])
                    for i in range(0, CHUNKS, 2)
                ],
                first,
            )


def weight_grads(core_of, plan, at=0, total=None, into=None):
    args, steps, columns, width, flops = [], [], [], 0, 0
    for kind, *arrays in plan:
        steps.append((kind, tuple(range(len(args), len(args) + len(arrays)))))
        args += arrays
        columns.append(width)
        if kind == "dot":
            n = sum(a.shape[1] for a in arrays[1:])
            flops += 2 * BLK * D * n
        elif kind == "vectors":
            n = VEC
        else:
            n = arrays[0].shape[1 if kind == "rows" else 0]
        width += n
    padded = -(-width // 512) * 512 if into else width
    total = total or width
    n = len(args)

    def body(*refs):
        outs = refs[n + 2 :] if into else refs[n:]
        weight_grads_body(core_of, steps, columns, *refs[:n], *outs)

    whole = [pl.BlockSpec(a.shape, lambda i, r=a.ndim: (0,) * r) for a in args]
    kept = [pl.BlockSpec(memory_space=pl.ANY)] * 2 if into else []
    return pl.pallas_call(
        body,
        grid=(1,),
        in_specs=whole + kept,
        out_specs=[pl.BlockSpec((D // 2, padded), lambda i: (0, at // padded))] * 2,
        out_shape=[jax.ShapeDtypeStruct((D // 2, total), jnp.bfloat16)] * 2,
        input_output_aliases={n: 0, n + 1: 1} if into else {},
        scratch_shapes=[pltpu.VMEM((D, BLK), jnp.bfloat16)],
        compiler_params=pltpu.CompilerParams(vmem_limit_bytes=56 * 2**20),
        cost_estimate=pl.CostEstimate(
            flops=flops, bytes_accessed=4 * D * width, transcendentals=0
        ),
        name="weight_grads",
    )(*args, *(into or ()))


def natural(keep, away):
    parts = [a.reshape(2, 2, 4, -1, a.shape[1]).transpose(2, 0, 1, 3, 4) for a in (keep, away)]
    parts[1] = parts[1].transpose(0, 2, 1, 3, 4)
    return jnp.stack(parts, 3).reshape(-1, keep.shape[1])


def finish_mlp(end_a, end_b):
    rows = end_a[0].shape[0]

    def body(a0, a1, b0, b1, up, down):
        halves = a0[...] + f32(a1[...]), b0[...] + f32(b1[...])
        lane = lax.broadcasted_iota(jnp.int32, (rows, 128), 1) < 64
        for i in range(0, CHUNKS, 2):
            a, b = (half[:, i * 64 : i * 64 + 128] for half in halves)
            up[:, i * 128 : (i + 1) * 128] = jnp.where(lane, a, pltpu.roll(b, 64, 1))
            up[:, (i + 1) * 128 : (i + 2) * 128] = jnp.where(lane, pltpu.roll(a, 64, 1), b)
        at = 0
        for half in halves:
            for q in range(HALF // D):
                down[at : at + rows, :] = half[:, HALF + q * D : HALF + (q + 1) * D]
                at += rows

    return pl.pallas_call(
        body,
        out_shape=[
            jax.ShapeDtypeStruct((rows, 2 * HALF), jnp.float32),
            jax.ShapeDtypeStruct((4 * rows, D), jnp.float32),
        ],
        name="finish_mlp",
    )(*end_a, *end_b)


def pack_first(attn_gain, mlp_gain, gate, down_bias, up_bias, *matrices):
    rows = matrices[0].shape[0]
    vectors = [v.reshape(1, -1) for v in (attn_gain, mlp_gain, gate, down_bias, up_bias)]

    def body(a, m, g, d, u, table, *rest):
        out = rest[-1]
        up = f32(u[...])
        column = [f32(v[...]) for v in (a, m, g, d)]
        column += [up[:, i : i + rows] for i in range(0, up.shape[1], rows)]
        column = jnp.transpose(jnp.concatenate(column, 0))
        column = jnp.concatenate(
            [column, jnp.zeros((rows, VEC - column.shape[1]), jnp.float32)], 1
        )
        first = 0
        for part in [table[...], low(column)] + [r[...] for r in rest[:-1]]:
            out[:, first : first + part.shape[1]] = part
            first += part.shape[1]

    return pl.pallas_call(
        body,
        out_shape=jax.ShapeDtypeStruct((rows, VEC + sum(m.shape[1] for m in matrices)), jnp.bfloat16),
        name="pack_first",
    )(*vectors, *matrices)


def pack_rest(query, sinit, skey, svalue, out_weight, up, down):
    rows = query.shape[0]
    half = down.shape[0] // 2

    def body(r, s, k, w, o, up, down, second, third, fourth):
        first = 0
        for part in (r, s, k, w, o):
            second[:, first : first + part.shape[1]] = part[...]
            first += part.shape[1]
        lane = lax.broadcasted_iota(jnp.int32, (rows, 128), 1) < 64
        for i in range(0, CHUNKS, 2):
            a = f32(up[:, i * 128 : (i + 1) * 128])
            b = f32(up[:, (i + 1) * 128 : (i + 2) * 128])
            at = slice(i * 64, i * 64 + 128)
            third[:, at] = low(jnp.where(lane, a, pltpu.roll(b, 64, 1)))
            fourth[:, at] = low(jnp.where(lane, pltpu.roll(a, 64, 1), b))
        for i, out in enumerate((third, fourth)):
            for q in range(half // rows):
                start = i * half + q * rows
                out[:, HALF + q * D : HALF + (q + 1) * D] = down[start : start + rows, :]

    return pl.pallas_call(
        body,
        out_shape=[
            jax.ShapeDtypeStruct((rows, NSTATE + 4 * D), jnp.bfloat16),
            jax.ShapeDtypeStruct((rows, 2 * HALF), jnp.bfloat16),
            jax.ShapeDtypeStruct((rows, 2 * HALF), jnp.bfloat16),
        ],
        name="pack_rest",
    )(query, sinit, skey, svalue, out_weight, up, down)


def readout(gstate, skv_full):
    def body(g, w, read, sent):
        r = dot(g[0], w[:, :D], NT) + dot(g[1], w[:, D:], NT)
        read[...] = r
        sent[...] = low(r)

    return pl.pallas_call(
        body,
        out_shape=[
            jax.ShapeDtypeStruct((NSTATE, D), jnp.float32),
            jax.ShapeDtypeStruct((NSTATE, D), jnp.bfloat16),
        ],
        compiler_params=pltpu.CompilerParams(vmem_limit_bytes=32 * 2**20),
        cost_estimate=pl.CostEstimate(
            flops=4 * NSTATE * D * D, bytes_accessed=9 * 2**20, transcendentals=0
        ),
        name="readout",
    )(gstate, skv_full)


def embedding_back(gq, gk, gv, query_full, kv_full, embedded, grad_hidden, rows):
    def body(q, k, v, wq, w, e, g_out, r, grad, lowered, gain_grad):
        g = dot(q[...], wq[...], NT) + dot(k[...], w[:, :D], NT) + dot(v[...], w[:, D:], NT)
        emb = e[...]
        scale = lax.rsqrt(jnp.mean(emb * emb, -1, keepdims=True) + 1e-06)
        normed = emb * scale
        gain_grad[...] = jnp.broadcast_to(jnp.sum(g * normed, 0, keepdims=True), gain_grad.shape)
        g = g * r[0:1, :]
        g = g_out[...] + scale * (g - normed * jnp.mean(g * normed, -1, keepdims=True))
        grad[...] = g
        lowered[...] = low(g)

    return pl.pallas_call(
        body,
        out_shape=[
            jax.ShapeDtypeStruct((BLK, D), jnp.float32),
            jax.ShapeDtypeStruct((BLK, D), jnp.bfloat16),
            jax.ShapeDtypeStruct((8, D), jnp.float32),
        ],
        compiler_params=pltpu.CompilerParams(vmem_limit_bytes=48 * 2**20),
        cost_estimate=pl.CostEstimate(
            flops=6 * BLK * D * D, bytes_accessed=18 * 2**20, transcendentals=0
        ),
        name="embedding_back",
    )(gq, gk, gv, query_full, kv_full, embedded, grad_hidden, rows)


def layer(
    fast,
    char_ids,
    char_table,
    attn_gain,
    query_weight,
    key_weight,
    value_weight,
    out_weight,
    state_key_weight,
    state_value_weight,
    update_weight,
    state_query,
    state_init,
    gate_bias,
    position_table,
    mlp_gain,
    up_weight,
    up_bias,
    down_weight,
    down_bias,
    out_grad,
):
    rows = attn_gain.shape[0]
    ff = up_weight.shape[1]
    folds = ff // D
    main = VOCAB + VEC
    spot_of = here if fast else (lambda: (jnp.int32(0),) * 3)
    core_of = core_index if fast else (lambda: jnp.int32(0))
    layouts = (
        ((0, main, 1), (main, 2 * D, 1), (main + 2 * D, NSTATE, 1), (main + 2 * D + NSTATE, D, 1)),
        ((0, D, 1), (D, NSTATE, 1), (D + NSTATE, 2 * D, 1), (D + NSTATE + 2 * D, D, 1)),
    )
    if fast:
        shard1 = pack_first(
            attn_gain,
            mlp_gain,
            gate_bias,
            down_bias,
            up_bias,
            char_table,
            key_weight,
            value_weight,
            state_query,
            update_weight,
        )
        z1 = along_z(shard1)
        shard2, shard3, shard4 = pack_rest(
            query_weight,
            state_init,
            state_key_weight,
            state_value_weight,
            out_weight,
            up_weight,
            down_weight,
        )
        z1[:3], shard2, shard3, shard4 = join(z1[:3], shard2, shard3, shard4)
        p1 = stack_z(shard1, *z1)
        shard2 = tie(shard2, p1)
        z2 = along_z(shard2)
        sides1, z2[:3] = join(to_sides(p1), z2[:3])
        shard3, p2 = join(shard3, stack_z(shard2, *z2))
        corner1, near3 = join(to_corner(p1, sides1), send(shard3, Z_NEAR))
        z3, sides2 = far_z(shard3, near3), to_sides(p2, X_ROUTE, Y_ROUTE)
        table_vec, kv_full, squery_full, update_full = assemble(
            pieces(p1, sides1, corner1, last_corner(corner1)), layouts[0], True
        )
    else:
        vectors = jnp.concatenate([attn_gain, mlp_gain, gate_bias, down_bias, up_bias])
        vectors = vectors.reshape(4 + folds, rows)
        columns = jnp.pad(jnp.transpose(vectors), ((0, 0), (0, VEC - vectors.shape[0])))
        table_vec, kv_full, squery_full, update_full = gather_any(
            jnp.concatenate(
                [char_table, columns, key_weight, value_weight, state_query, update_weight], 1
            ),
            layouts[0],
        )

    vector_rows = jnp.transpose(f32(table_vec[:, VOCAB : VOCAB + 4 + folds]))
    biases = halves_of_columns(
        vector_rows[4:].reshape(folds, -1, rows).transpose(1, 0, 2).reshape(1, ff)
    )
    keep_gate = jax.nn.sigmoid(vector_rows[2])
    is_first = lax.axis_index("seq") == 0
    bias_rows = f32(position_table)[:, None, :]

    one_hot = (char_ids[:, None] == jnp.arange(VOCAB)[None, :]).astype(jnp.bfloat16)
    embedded = dot(one_hot, table_vec[:, :VOCAB], NT)
    normed_low = low(embedded * norm_scale(embedded) * vector_rows[0])
    kv = low(dot(normed_low, kv_full, NN))
    state_mix, state_lse = state_attention(kv, squery_full)
    update = dot(state_mix, update_full, NN)
    mine = low((1.0 - keep_gate) * update)
    if fast:
        sides2, z3[:3], mine = join(sides2, z3[:3], mine)
        sibling = send(mine, CORE_ROUTE)
        near = earlier_near(keep_gate, mine, sibling)
        prev = from_behind(tie(kv, mine), "seq", 1)
        corner2 = to_corner(p2, sides2, Y_ROUTE)
        near, corner2, prev, near4, p3 = join(
            near, corner2, prev, send(tie(shard4, mine), Z_NEAR), stack_z(shard3, *z3)
        )
        sides3, z4 = to_sides(p3), far_z(shard4, near4)
        query_full, sinit_full, skv_full, out_full = assemble(
            pieces(p2, sides2, corner2, last_corner(corner2)), layouts[1], False
        )
    else:
        prev = from_behind(kv, "seq", 1)
        query_full, sinit_full, skv_full, out_full = gather_any(
            jnp.concatenate(
                [query_weight, state_init, state_key_weight, state_value_weight, out_weight], 1
            ),
            layouts[1],
        )
    query = low(dot(normed_low, query_full, NN))
    start = f32(join(jnp.transpose(sinit_full))[0])
    if fast:
        state_prev = earlier_sum(keep_gate, near, sibling, start)
    else:
        gain, total = entering(keep_gate, mine, False)
        state_prev = gain * start + total
    state_low = low(state_prev)
    skv = low(dot(state_low, skv_full, NN))
    if fast:
        skv, query, sides3, z4[:3] = join(skv, query, sides3, z4[:3])
        corner3, p4 = to_corner(p3, sides3), stack_z(shard4, *z4)
    mixed, lse = attention(query, kv, prev, skv, bias_rows)
    hidden = embedded + dot(mixed, out_full, NN)

    if fast:
        corner3, hidden, p4 = join(corner3, hidden, p4)
        sides4 = to_sides(p4)
        parts = pieces(p3, sides3, corner3, last_corner(corner3))
        keep_a, away_a, bias_a, *before = mlp_half(
            spot_of, True, hidden, out_grad, vector_rows, biases[0], parts, None
        )
        sides4, away_a, before = join(sides4, away_a, before)
        corner4, got_a = join(to_corner(p4, sides4), to_core(away_a))
        parts = pieces(p4, sides4, corner4, last_corner(corner4))
        first_a = over_first(keep_a, got_a)
        keep_b, away_b, bias_b, *before = mlp_half(
            spot_of, True, hidden, out_grad, vector_rows, biases[1], parts, before
        )
        first_a, away_b, before = join(first_a, away_b, before)
    else:
        shard = jnp.concatenate([up_weight, fold(down_weight, rows)], 1)
        up_full, down_full = gather_any(shard, ((0, ff, 1), (ff, D, folds)))
        halves = []
        for up, down in zip(halves_of_columns(up_full), halves_of_rows(down_full, CHUNKS)):
            down = down.reshape(CHUNKS, 2, -1, D).transpose(0, 2, 1, 3).reshape(D, HALF)
            both = jnp.concatenate([up, down], 1).reshape(4, 2, 2, 2, -1, 2 * HALF)
            halves.append([both[:, i // 2 % 2, i % 2, i // 4] for i in range(8)])
        keep_a, away_a, bias_a, *before = mlp_half(
            spot_of, False, hidden, out_grad, vector_rows, biases[0], halves[0], None
        )
        keep_b, away_b, bias_b, *before = mlp_half(
            spot_of, False, hidden, out_grad, vector_rows, biases[1], halves[1], before
        )
    output, grad_hidden, grad_branch, mlp_sums = before

    grad_mixed = low(dot(grad_branch, out_full, NT))
    if fast:
        second_a = over_second(keep_a, got_a, first_a)
        got_b, grad_mixed = join(to_core(away_b), grad_mixed)
        first_b = over_first(keep_b, got_b)
    gq, gkv, gprev, gstate, gbias = attention_back(
        query, kv, prev, skv, bias_rows, lse, grad_mixed
    )
    gbias = gbias.reshape(HEADS, BLK)
    if fast:
        second_a, first_b, gprev, gstate = join(second_a, first_b, gprev, gstate)
    read, sent = readout(gstate, skv_full)
    if fast:
        sibling = send(sent, CORE_ROUTE)
        near = later_near(keep_gate, sent, sibling)
    first = weight_grads(
        core_of,
        [
            ("dot", mixed, grad_branch),
            ("dot", state_low, gstate[0], gstate[1]),
            ("dot", normed_low, gq),
        ],
    )
    if fast:
        pair_a = over_pairs(keep_a, got_a, first_a, tie(second_a, first[0]))
        near, first = join(near, first)
        gprev = tie(gprev, near)
        gnext = from_behind(gprev, "seq", -1)
        got_c = to_core(first[1])
        after = later_sum(keep_gate, near, sibling)
    else:
        gnext = from_behind(gprev, "seq", -1)
        after = entering(keep_gate, sent, True)[1]
    grad_update = low((1.0 - keep_gate) * after)
    grad_smix = low(dot(grad_update, update_full, NT))
    if fast:
        got_c, grad_smix = join(got_c, grad_smix)
        gbias = exchange(tie(gbias, grad_smix), CORE_ROUTE)
    gsum, gquery = state_attention_back(kv, squery_full, state_lse, grad_smix, gkv)
    if fast:
        gsum, after = join(gsum, after)
    state_init_grad = jnp.where(is_first, read + keep_gate * after, 0.0)
    last = weight_grads(
        core_of,
        [
            ("dot", state_mix, grad_update),
            ("rows", gquery),
            ("transposed", state_init_grad),
        ],
        0,
        4 * D + 512,
    )
    if fast:
        gnext, last, gbias, pair_a = join(gnext, last, gbias, pair_a)
        second_b = over_second(keep_b, got_b, tie(first_b, gnext))
        first_c = over_first(first[0], tie(got_c, gnext))
        gbias = exchange(gbias, X_ROUTE)
    gk, gv = (low(gsum[i] + f32(gnext[i])) for i in range(2))
    last = weight_grads(core_of, [("dot", normed_low, gk, gv)], 2 * D, 4 * D + 512, last)
    embedded_grad, embedded_low, gain_grad = embedding_back(
        gq, gk, gv, query_full, kv_full, embedded, grad_hidden, vector_rows
    )
    gate_bias_grad = jnp.sum(after * (state_prev - update), 0) * keep_gate * (1.0 - keep_gate)
    last = weight_grads(
        core_of,
        [
            ("dot", embedded_low, one_hot),
            ("vectors", gain_grad, mlp_sums, gate_bias_grad[None], bias_a, bias_b),
        ],
        4 * D,
        4 * D + 512,
        last,
    )
    if fast:
        second_b, first_c, last, gbias = join(second_b, first_c, last, gbias)
        got_d = to_core(last[1])
        pair_b = over_pairs(keep_b, got_b, first_b, second_b)
        first_d = over_first(last[0], got_d)
        second_c = over_second(first[0], got_c, first_c)
        end_a = within_pair(*pair_a)
        gbias = exchange(gbias, Y_ROUTE)
        second_c, first_d, pair_b, end_a, gbias = join(second_c, first_d, pair_b, end_a, gbias)
        second_d = over_second(last[0], got_d, first_d)
        pair_c = over_pairs(first[0], got_c, first_c, second_c)
        end_b = within_pair(*pair_b)
        gbias = exchange(gbias, Z_NEAR)
        second_d, end_b, gbias = join(second_d, end_b, gbias)
        up_sum, down_sum = finish_mlp(end_a, end_b)
        end_d = over_z(last[0], got_d, first_d, second_d)
        end_c = within_pair(*pair_c)
        position_table_grad = exchange(gbias, Z_FAR)
        first, last = finish(end_c), finish(end_d)
    else:
        pairs = [natural(keep_a, away_a), natural(keep_b, away_b)]
        up_sum = jnp.concatenate([s[:, :HALF].reshape(D, CHUNKS, -1) for s in pairs], 2)
        up_sum = scatter_any(up_sum.reshape(D, ff))
        down_sum = jnp.concatenate(
            [
                s[:, HALF:].reshape(CHUNKS, D // CHUNKS, -1, D).transpose(0, 2, 1, 3)
                for s in pairs
            ],
            1,
        )
        down_sum = scatter_any(down_sum.reshape(ff, D))
        first, last = (scatter_any(natural(*s)) for s in (first, last))
        position_table_grad = lax.psum(gbias, AX)
    main = 4 * D + VOCAB
    vector_sum = last[:, main:]
    return (
        output,
        embedded_grad,
        last[:, 4 * D : main],
        vector_sum[:, 0],
        first[:, 3 * D :],
        last[:, 2 * D : 3 * D],
        last[:, 3 * D : 4 * D],
        first[:, :D],
        first[:, D : 2 * D],
        first[:, 2 * D : 3 * D],
        last[:, :D],
        last[:, D : D + NSTATE],
        last[:, D + NSTATE : 2 * D],
        vector_sum[:, 2],
        position_table_grad,
        vector_sum[:, 1],
        up_sum,
        jnp.transpose(vector_sum[:, 4 : 4 + folds]).reshape(-1),
        down_sum,
        vector_sum[:, 3],
    )


def solution(mesh):
    fast = dict(mesh.shape) == {"dp": 8, "seq": 4}
    return jax.shard_map(
        functools.partial(layer, fast),
        mesh=mesh,
        in_specs=(
            P(("dp", "seq")),
            P(("dp", "seq"), None),
            P(("dp", "seq")),
            P(("dp", "seq"), None),
            P(("dp", "seq"), None),
            P(("dp", "seq"), None),
            P(("dp", "seq"), None),
            P(("dp", "seq"), None),
            P(("dp", "seq"), None),
            P(("dp", "seq"), None),
            P(("dp", "seq"), None),
            P(("dp", "seq"), None),
            P(("dp", "seq")),
            P(),
            P(("dp", "seq")),
            P(("dp", "seq"), None),
            P(("dp", "seq")),
            P(("dp", "seq"), None),
            P(("dp", "seq")),
            P(("dp", "seq"), None),
        ),
        out_specs=(
            P(("dp", "seq"), None),
            P(("dp", "seq"), None),
            P(("dp", "seq"), None),
            P(("dp", "seq")),
            P(("dp", "seq"), None),
            P(("dp", "seq"), None),
            P(("dp", "seq"), None),
            P(("dp", "seq"), None),
            P(("dp", "seq"), None),
            P(("dp", "seq"), None),
            P(("dp", "seq"), None),
            P(("dp", "seq"), None),
            P(("dp", "seq"), None),
            P(("dp", "seq")),
            P(),
            P(("dp", "seq")),
            P(("dp", "seq"), None),
            P(("dp", "seq")),
            P(("dp", "seq"), None),
            P(("dp", "seq")),
        ),
        check_vma=False,
    )
```
